32 devices in a mesh: ctx: 16 (over z, y, x), head: 2 (over core).
Axes of the slice: x: 2, y: 2, z: 4, core: 2. Of those that a mesh axis runs over, the one named last changes fastest.
Arguments:
- queries: bfloat16 [8192, 2048], P('ctx', 'head'), may hold values from -16 to 16
- keys: bfloat16 [8192, 2048], P('ctx', 'head'), may hold values from -16 to 16
- values: bfloat16 [8192, 2048], P('ctx', 'head'), may hold values from -12 to 12
- gain: bfloat16 [2048], P('head'), may hold values from 0.5 to 1.5
- cotangent: bfloat16 [8192, 2048], P('ctx', 'head'), may hold values from -6 to 6
Outputs:
- output: bfloat16 [8192, 2048], P('ctx', 'head')
- grad_queries: bfloat16 [8192, 2048], P('ctx', 'head')
- grad_keys: bfloat16 [8192, 2048], P('ctx', 'head')
- grad_values: bfloat16 [8192, 2048], P('ctx', 'head')
The draws below stay inside these ranges and needn't reach their ends.
All inputs are finite; a program needn't handle non-finite values.
Results may differ from the reference program's by a relative error of at most 0.0065.
Values may be sent and summed in bfloat16 or wider, within the bound.
No kernel may reach another device: no remote copies, remote signals or barrier semaphores. Data moves between devices by JAX's collectives and lax.ppermute only.
A program may use at most 128 MiB of HBM per device.

```python
import math
import jax
import jax.numpy as jnp
from jax import lax

HEAD_DIM = 128
HEADS = 16
WINDOW = 256
TOK_DEV = 512
TOKENS = 8192
FEATURES = 2048


def draw_queries(key, part):
    own_part = jnp.clip(jax.random.normal(jax.random.fold_in(key, 1), (TOKENS, FEATURES), jnp.float32), -5.0, 5.0)
    return own_part.astype(jnp.bfloat16)


def draw_keys(key, part):
    own_part = jnp.clip(jax.random.normal(jax.random.fold_in(key, 2), (TOKENS, FEATURES), jnp.float32), -5.0, 5.0)
    return own_part.astype(jnp.bfloat16)


def draw_values(key, part):
    key_entry, key_jitter = jax.random.split(jax.random.fold_in(key, 3), 2)
    grade = jnp.arange(HEADS, dtype=jnp.float32) / max(HEADS - 1, 1)
    jitter = jnp.exp(jax.random.uniform(key_jitter, (HEADS,), jnp.float32, -0.15, 0.15))
    head_scale = 0.5 * jnp.exp(grade * jnp.log(3.0)) * jitter
    entries = jnp.clip(jax.random.normal(key_entry, (TOKENS, HEADS, HEAD_DIM), jnp.float32), -6.0, 6.0)
    return (entries * head_scale[None, :, None]).reshape(TOKENS, FEATURES).astype(jnp.bfloat16)


def block_scale(stream_key, shape, pieces, smallest, high):
    def one(position, blocks):
        heights = jax.random.uniform(jax.random.fold_in(jax.random.fold_in(stream_key, 6), position), (blocks,), jnp.float32, smallest / len(pieces), high / len(pieces))
        return jnp.repeat(jnp.exp(heights), shape[position] // blocks).reshape((-1,) + (1,) * (len(shape) - position - 1))

    factor_of = one(*pieces[0])
    for cut in pieces[1:]:
        factor_of = factor_of * one(*cut)
    return factor_of


def bell_draw(key, shape, spread, limit, cuts=(), kind=jnp.bfloat16):
    result = spread * jax.random.normal(key, shape, jnp.float32)
    if cuts:
        result = result * block_scale(key, shape, cuts, -0.22, 0.18)
    return jnp.clip(result, -limit, limit).astype(kind)


def setup_inputs(seed: int = 0) -> dict:
    splits = jax.random.split(jax.random.key(seed), 6)
    return {
        "queries": draw_queries(jax.random.fold_in(splits[5], 71), 0),
        "keys": draw_keys(jax.random.fold_in(splits[5], 71), 0),
        "values": draw_values(jax.random.fold_in(splits[5], 71), 0),
        "gain": jnp.clip(1.0 + 0.1 * jax.random.normal(splits[3], (FEATURES,), jnp.float32), 0.5, 1.5).astype(jnp.bfloat16),
        "cotangent": bell_draw(splits[4], (TOKENS, FEATURES), 1.0, 6.0, ((0, 16), (1, 2))),
    }


epsilon = 1e-06

def matmul(left, right):
    return jnp.dot(left, right, preferred_element_type=jnp.float32)

def reference(queries, keys, values, gain, cotangent):
    seq_len = queries.shape[0]
    num_blocks = seq_len // TOK_DEV
    inv_root = 1.0 / math.sqrt(HEAD_DIM)

    def by_head(array):
        return array.reshape(num_blocks, TOK_DEV, HEADS, HEAD_DIM).transpose(2, 0, 1, 3)

    def from_heads(array):
        return array.transpose(1, 2, 0, 3).reshape(seq_len, FEATURES)
    positions = jnp.arange(seq_len, dtype=jnp.int32)
    coefs = 1.0 / jnp.sqrt(HEAD_DIM * (positions + 1).astype(jnp.float32))
    coef_blocks = coefs.reshape(num_blocks, TOK_DEV)
    in_block = jnp.arange(TOK_DEV, dtype=jnp.int32)
    causal = in_block[:, None] >= in_block[None, :]
    ext_cols = jnp.arange(TOK_DEV + WINDOW, dtype=jnp.int32)
    block_ids = jnp.arange(num_blocks, dtype=jnp.int32)

    def window_mask(block_id):
        after = ext_cols[None, :] > in_block[:, None]
        within = ext_cols[None, :] <= in_block[:, None] + WINDOW
        inside = block_id * TOK_DEV - WINDOW + ext_cols[None, :] >= 0
        return after & within & inside

    def with_tails(array_h):
        tails = array_h[:-1, TOK_DEV - WINDOW:]
        return jnp.concatenate([jnp.zeros((1, WINDOW, HEAD_DIM), array_h.dtype), tails], 0)

    def forward_head(operands):
        query_h, key_h, value_h = operands

        def step(state, inputs):
            query_blk, key_blk, value_blk, key_tail, value_tail, coef_row, block_id = inputs
            state_b = state.astype(jnp.bfloat16)
            lin_weights = jnp.where(causal, matmul(query_blk, key_blk.T) * coef_row[:, None], 0.0).astype(jnp.bfloat16)
            linear = coef_row[:, None] * matmul(query_blk, state_b) + matmul(lin_weights, value_blk)
            key_ext = jnp.concatenate([key_tail, key_blk], 0)
            value_ext = jnp.concatenate([value_tail, value_blk], 0)
            mask = window_mask(block_id)
            logits = matmul(query_blk, key_ext.T) * inv_root
            row_peak = lax.optimization_barrier(jnp.max(jnp.where(mask, logits, -1e+30), 1))
            row_total = lax.optimization_barrier(jnp.sum(jnp.where(mask, jnp.exp(logits - row_peak[:, None]), 0.0), 1))
            log_total = row_peak + jnp.log(row_total)
            probs = jnp.where(mask, jnp.exp(logits - log_total[:, None]), 0.0)
            local_window = matmul(probs.astype(jnp.bfloat16), value_ext)
            return (state + matmul(key_blk.T, value_blk), (linear + local_window, local_window, log_total, state_b))
        init = jnp.zeros((HEAD_DIM, HEAD_DIM), jnp.float32)
        _, results = lax.scan(step, init, (query_h, key_h, value_h, with_tails(key_h), with_tails(value_h), coef_blocks, block_ids))
        return results
    query_all, key_all, value_all = (by_head(queries), by_head(keys), by_head(values))
    hidden_h, window_h, lse_h, prefix_h = lax.map(forward_head, (query_all, key_all, value_all))
    hidden = from_heads(hidden_h)
    gain_f = gain.astype(jnp.float32)
    scaled = gain_f[None, :] * cotangent.astype(jnp.float32)
    squares = lax.optimization_barrier(jnp.sum(hidden * hidden, 1))
    crossed = lax.optimization_barrier(jnp.sum(hidden * scaled, 1))
    recip = 1.0 / jnp.sqrt(squares / FEATURES + epsilon)
    output = (hidden * recip[:, None] * gain_f[None, :]).astype(jnp.bfloat16)
    grad_full = recip[:, None] * scaled - hidden * (recip ** 3 * crossed / FEATURES)[:, None]
    grad_h = grad_full.astype(jnp.bfloat16)
    grad_u = (grad_full * coefs[:, None]).astype(jnp.bfloat16)

    def backward_head(operands):
        query_h, key_h, value_h, grad_hh, gradu_h, window_hh, lse_hh, prefix_hh = operands

        def step(carry, inputs):
            suffix, pend_key, pend_value = carry
            query_blk, key_blk, value_blk, key_tail, value_tail, grad_blk, gradu_blk, window_blk, lse_blk, prefix_blk, coef_row, block_id = inputs
            suffix_b = suffix.astype(jnp.bfloat16)
            lin_weights = jnp.where(causal, matmul(query_blk, key_blk.T) * coef_row[:, None], 0.0).astype(jnp.bfloat16)
            back_lin = jnp.where(causal, matmul(gradu_blk, value_blk.T), 0.0).astype(jnp.bfloat16)
            d_query = matmul(gradu_blk, prefix_blk.T) + matmul(back_lin, key_blk)
            d_key = matmul(back_lin.T, query_blk) + matmul(value_blk, suffix_b.T)
            d_value = matmul(lin_weights.T, grad_blk) + matmul(key_blk, suffix_b)
            key_ext = jnp.concatenate([key_tail, key_blk], 0)
            value_ext = jnp.concatenate([value_tail, value_blk], 0)
            mask = window_mask(block_id)
            logits = matmul(query_blk, key_ext.T) * inv_root
            probs = jnp.where(mask, jnp.exp(logits - lse_blk[:, None]), 0.0)
            d_probs = matmul(grad_blk, value_ext.T)
            delta = lax.optimization_barrier(jnp.sum(grad_blk.astype(jnp.float32) * window_blk, 1))
            d_logits = (probs * (d_probs - delta[:, None]) * inv_root).astype(jnp.bfloat16)
            d_query = d_query + matmul(d_logits, key_ext)
            d_key_ext = matmul(d_logits.T, query_blk)
            d_value_ext = matmul(probs.astype(jnp.bfloat16).T, grad_blk)
            pad_rows = jnp.zeros((TOK_DEV - WINDOW, HEAD_DIM), jnp.float32)
            d_key = d_key + d_key_ext[WINDOW:] + jnp.concatenate([pad_rows, pend_key], 0)
            d_value = d_value + d_value_ext[WINDOW:] + jnp.concatenate([pad_rows, pend_value], 0)
            new_carry = (suffix + matmul(query_blk.T, gradu_blk), d_key_ext[:WINDOW], d_value_ext[:WINDOW])
            return (new_carry, (d_query.astype(jnp.bfloat16), d_key.astype(jnp.bfloat16), d_value.astype(jnp.bfloat16)))
        init = (jnp.zeros((HEAD_DIM, HEAD_DIM), jnp.float32), jnp.zeros((WINDOW, HEAD_DIM), jnp.float32), jnp.zeros((WINDOW, HEAD_DIM), jnp.float32))
        xs = (query_h, key_h, value_h, with_tails(key_h), with_tails(value_h), grad_hh, gradu_h, window_hh, lse_hh, prefix_hh, coef_blocks, block_ids)
        _, results = lax.scan(step, init, xs, reverse=True)
        return results
    dq_h, dk_h, dv_h = lax.map(backward_head, (query_all, key_all, value_all, by_head(grad_h), by_head(grad_u), window_h, lse_h, prefix_h))
    return (output, from_heads(dq_h), from_heads(dk_h), from_heads(dv_h))
```

```python
import math

import jax
import jax.numpy as jnp
from jax import lax
from jax.experimental import pallas as pl
from jax.experimental.pallas import tpu as pltpu
from jax.sharding import PartitionSpec as P

HEAD_DIM = 128
WINDOW = 256
GROUP = 4
STATS = 8
EPSILON = 1e-06
SCALE = 1.0 / math.sqrt(HEAD_DIM)
SCALE_LOG2 = SCALE * math.log2(math.e)
LN2 = math.log(2.0)
MASKED = -1e30
BF16 = jnp.bfloat16
F32 = jnp.float32
VMEM_LIMIT = 24 * 1024 * 1024


def dot_nn(left, right):
    return lax.dot_general(left, right, (((1,), (0,)), ((), ())), preferred_element_type=F32)


def dot_nt(left, right):
    return lax.dot_general(left, right, (((1,), (1,)), ((), ())), preferred_element_type=F32)


def dot_tn(left, right):
    return lax.dot_general(left, right, (((0,), (0,)), ((), ())), preferred_element_type=F32)


def tile_iotas():
    keys_at = lax.broadcasted_iota(jnp.int32, (WINDOW, WINDOW), 0)
    queries_at = lax.broadcasted_iota(jnp.int32, (WINDOW, WINDOW), 1)
    return keys_at, queries_at


def coef_row(start, count):
    at = start + lax.broadcasted_iota(jnp.int32, (1, count), 1)
    return 1.0 / jnp.sqrt(HEAD_DIM * (at + 1).astype(F32))


def coef_column(start, count):
    at = start + lax.broadcasted_iota(jnp.int32, (count, HEAD_DIM), 0)
    return 1.0 / jnp.sqrt(HEAD_DIM * (at + 1).astype(F32))


def heads_a_step(heads):
    return 2 if heads % 2 == 0 else 1


def call(body, grid, in_specs, out_specs, out_shape, scratch, flops, moved):
    return pl.pallas_call(
        body,
        grid=grid,
        in_specs=in_specs,
        out_specs=out_specs,
        out_shape=out_shape,
        scratch_shapes=scratch,
        compiler_params=pltpu.CompilerParams(
            vmem_limit_bytes=VMEM_LIMIT,
            dimension_semantics=("arbitrary",) * len(grid),
        ),
        cost_estimate=pl.CostEstimate(flops=flops, bytes_accessed=moved, transcendentals=0),
    )


def whole(shape):
    return pl.BlockSpec(shape, lambda *_: (0,) * len(shape))


def put_state(held, head, state):
    rows = held.shape[1]
    step = min(rows, HEAD_DIM)
    for part in range(HEAD_DIM // step):
        at = head * HEAD_DIM + part * step
        held[at // rows, at % rows : at % rows + step, :] = state[part * step : (part + 1) * step]


def get_state(held, head):
    rows = held.shape[1]
    step = min(rows, HEAD_DIM)
    parts = []
    for part in range(HEAD_DIM // step):
        at = head * HEAD_DIM + part * step
        parts.append(held[at // rows, at % rows : at % rows + step, :])
    return parts[0] if len(parts) == 1 else jnp.concatenate(parts, 0)


def spread(held, outs):
    place = lax.rem(lax.axis_index("ctx"), GROUP)
    for other in range(GROUP):
        outs[other][...] = held[lax.bitwise_xor(place, jnp.int32(other))]


def collect(ins, held):
    place = lax.rem(lax.axis_index("ctx"), GROUP)
    for other in range(GROUP):
        held[lax.bitwise_xor(place, jnp.int32(other))] = ins[other][...]


def state_body(k_ref, v_ref, *rest):
    outs, held = rest[:GROUP], rest[GROUP]
    for head in range(k_ref.shape[1] // HEAD_DIM):
        cols = slice(head * HEAD_DIM, (head + 1) * HEAD_DIM)
        put_state(held, head, dot_tn(k_ref[:, cols], v_ref[:, cols]).astype(BF16))
    spread(held, outs)


def local_states(keys, values):
    rows, width = keys.shape
    piece = (width // GROUP, HEAD_DIM)
    return call(
        state_body,
        (1,),
        [whole((rows, width))] * 2,
        [whole(piece)] * GROUP,
        [jax.ShapeDtypeStruct(piece, BF16)] * GROUP,
        [pltpu.VMEM((GROUP,) + piece, BF16)],
        2 * rows * width * HEAD_DIM,
        2 * 2 * rows * width,
    )(keys, values)


def total_body(*refs):
    total = refs[0][...].astype(F32)
    for ref in refs[1:-1]:
        total = total + ref[...].astype(F32)
    refs[-1][...] = total.astype(refs[-1].dtype)


def merge_body(reverse, groups, *refs):
    block = lax.axis_index("ctx")
    group = block // GROUP
    place = lax.rem(block, GROUP)
    others = refs[: groups - 1]
    own = refs[groups - 1 : groups - 1 + GROUP]
    outs = refs[groups - 1 + GROUP :]
    total = jnp.zeros(outs[0].shape, F32)
    for step in range(1, groups):
        wanted = group - step < 0 if reverse else group - step >= 0
        total = total + others[step - 1][...].astype(F32) * wanted.astype(F32)
    for target in range(GROUP):
        to = lax.bitwise_xor(place, jnp.int32(target))
        result = total
        for source in range(GROUP):
            if source == target:
                continue
            of = lax.bitwise_xor(place, jnp.int32(source))
            wanted = of > to if reverse else of < to
            result = result + own[source][...].astype(F32) * wanted.astype(F32)
        outs[target][...] = result.astype(outs[target].dtype)


def swap(value, mask):
    count = lax.axis_size("ctx")
    return lax.ppermute(value, "ctx", [(at, at ^ mask) for at in range(count)])


def turn(value, steps):
    count = lax.axis_size("ctx")
    return lax.ppermute(value, "ctx", [(at, (at + steps) % count) for at in range(count)])


def scan(pieces, reverse):
    groups = lax.axis_size("ctx") // GROUP
    shape = pieces[0].shape
    full = whole(shape)
    size = shape[0] * shape[1]
    own = [pieces[0]] + [swap(pieces[other], other) for other in range(1, GROUP)]
    total = call(
        total_body, (1,), [full] * GROUP, full, jax.ShapeDtypeStruct(shape, BF16), [], GROUP * size, 2 * 5 * size
    )(*own)
    others = [turn(total, GROUP * step) for step in range(1, groups)]
    merged = call(
        lambda *refs: merge_body(reverse, groups, *refs),
        (1,),
        [full] * (groups - 1 + GROUP),
        [full] * GROUP,
        [jax.ShapeDtypeStruct(shape, BF16)] * GROUP,
        [],
        20 * size,
        2 * 11 * size,
    )(*others, *own)
    return [merged[0]] + [swap(merged[other], other) for other in range(1, GROUP)]


def attend(scores, masks, coef, linear):
    shown = [jnp.where(mask, score, MASKED) for score, mask in zip(scores, masks)]
    peak = jnp.max(shown[0], 0, keepdims=True)
    for tile in shown[1:]:
        peak = jnp.maximum(peak, jnp.max(tile, 0, keepdims=True))
    powers = [jnp.exp2((tile - peak) * SCALE_LOG2) for tile in shown]
    norm = jnp.sum(powers[0], 0, keepdims=True)
    for tile in powers[1:]:
        norm = norm + jnp.sum(tile, 0, keepdims=True)
    share = 1.0 / norm
    probs = [tile * share for tile in powers]
    sums = []
    for prob, score, mask, kind in zip(probs, scores, masks, linear):
        if kind == "none":
            sums.append(None)
        elif kind == "all":
            sums.append((prob + score * coef).astype(BF16))
        else:
            sums.append((prob + jnp.where(mask, score * coef, 0.0)).astype(BF16))
    lse = peak * SCALE + jnp.log(norm)
    return [prob.astype(BF16) for prob in probs], sums, lse


def late_body(q_ref, k_ref, v_ref, prob_ref, sum_ref, part_ref):
    rows = k_ref.shape[0]
    start = lax.axis_index("ctx") * rows
    keys_at, queries_at = tile_iotas()
    coef = coef_row(start + WINDOW, WINDOW)
    masks = [keys_at > queries_at, keys_at <= queries_at]
    for head in range(q_ref.shape[1] // HEAD_DIM):
        cols = slice(head * HEAD_DIM, (head + 1) * HEAD_DIM)
        query = q_ref[:, cols]
        scores = [dot_nt(k_ref[at * WINDOW : (at + 1) * WINDOW, cols], query) for at in range(2)]
        probs, sums, _ = attend(scores, masks, coef, ["all", "masked"])
        total = jnp.zeros((HEAD_DIM, WINDOW), F32)
        for at in range(2):
            prob_ref[head, at] = probs[at]
            sum_ref[head, at] = sums[at]
            total = total + dot_tn(v_ref[at * WINDOW : (at + 1) * WINDOW, cols], sums[at])
        part_ref[:, cols] = total.T


def late_rows(queries, keys, values):
    rows, width = keys.shape
    heads = width // HEAD_DIM
    step = heads_a_step(heads)
    tiles = (heads, 2, WINDOW, WINDOW)
    tile_spec = pl.BlockSpec((step,) + tiles[1:], lambda at: (at, 0, 0, 0))
    wide = step * HEAD_DIM
    return call(
        late_body,
        (heads // step,),
        [
            pl.BlockSpec((WINDOW, wide), lambda at: (1, at)),
            pl.BlockSpec((rows, wide), lambda at: (0, at)),
            pl.BlockSpec((rows, wide), lambda at: (0, at)),
        ],
        [tile_spec, tile_spec, pl.BlockSpec((WINDOW, wide), lambda at: (0, at))],
        [
            jax.ShapeDtypeStruct(tiles, BF16),
            jax.ShapeDtypeStruct(tiles, BF16),
            jax.ShapeDtypeStruct((WINDOW, width), F32),
        ],
        [],
        4 * 2 * WINDOW * WINDOW * width * 4,
        12 * WINDOW * width * 2,
    )(queries, keys, values)


def mid_body(steps, q_ref, k_ref, v_ref, kp_ref, vp_ref, part_ref, gain_ref, cot_ref, *rest):
    ins = rest[:GROUP]
    prob_ref, sum_ref, hidden_ref, window_ref, lse_ref, norm_ref, held, squares, crossed = rest[GROUP:]
    rows = q_ref.shape[0]
    block = lax.axis_index("ctx")
    start = block * rows
    at_step = pl.program_id(0)
    step = q_ref.shape[1] // HEAD_DIM

    @pl.when(at_step == 0)
    def _():
        collect(ins, held)
        squares[...] = jnp.zeros_like(squares)
        crossed[...] = jnp.zeros_like(crossed)
        lse_ref[...] = jnp.zeros_like(lse_ref)

    keys_at, queries_at = tile_iotas()
    beyond = jnp.where(block > 0, 0, 2 * WINDOW)
    masks = [keys_at > queries_at + beyond, keys_at <= queries_at]
    coef = coef_row(start, WINDOW)
    columns = coef_column(start, rows)
    for head in range(step):
        cols = slice(head * HEAD_DIM, (head + 1) * HEAD_DIM)
        query = q_ref[:WINDOW, cols]
        scores = [dot_nt(kp_ref[:, cols], query), dot_nt(k_ref[:, cols], query)]
        probs, sums, lse = attend(scores, masks, coef, ["none", "masked"])
        prob_ref[head, 0] = probs[0]
        prob_ref[head, 1] = probs[1]
        sum_ref[head] = sums[1]
        lse_ref[pl.ds(at_step * step + head, 1), :] = lse
        value = v_ref[:, cols]
        before = dot_tn(vp_ref[:, cols], probs[0])
        window = before + dot_tn(value, probs[1])
        window_ref[:, cols] = window.T
        inside = (before + dot_tn(value, sums[1])).T
        state = held_state(held, at_step * step + head)
        carried = columns * dot_nn(q_ref[:, cols], state)
        hidden = jnp.concatenate([inside, part_ref[:, cols]], 0) + carried
        hidden_ref[:, cols] = hidden
        scaled = gain_ref[:, cols].astype(F32) * cot_ref[:, cols].astype(F32)
        squares[...] += hidden * hidden
        crossed[...] += hidden * scaled

    @pl.when(at_step == steps - 1)
    def _():
        norm_ref[...] = jnp.zeros_like(norm_ref)
        norm_ref[0:1, :] = jnp.sum(squares[...].T, 0, keepdims=True)
        norm_ref[1:2, :] = jnp.sum(crossed[...].T, 0, keepdims=True)


def held_state(held, head):
    rows = held.shape[1]
    if rows >= HEAD_DIM:
        each = rows // HEAD_DIM
        at = pl.multiple_of(lax.rem(head, each) * HEAD_DIM, HEAD_DIM)
        return held[head // each, pl.ds(at, HEAD_DIM), :]
    each = HEAD_DIM // rows
    return jnp.concatenate([held[head * each + part] for part in range(each)], 0)


def middle(queries, keys, values, keys_before, values_before, part, gain, cotangent, prefix):
    rows, width = keys.shape
    heads = width // HEAD_DIM
    step = heads_a_step(heads)
    steps = heads // step
    wide = step * HEAD_DIM
    piece = prefix[0].shape
    half = pl.BlockSpec((WINDOW, wide), lambda at: (0, at))
    full = pl.BlockSpec((rows, wide), lambda at: (0, at))
    tiles = (heads, 2, WINDOW, WINDOW)
    return call(
        lambda *refs: mid_body(steps, *refs),
        (steps,),
        [full, half, half, half, half, half, pl.BlockSpec((1, wide), lambda at: (0, at)), full] + [whole(piece)] * GROUP,
        [
            pl.BlockSpec((step,) + tiles[1:], lambda at: (at, 0, 0, 0)),
            pl.BlockSpec((step, WINDOW, WINDOW), lambda at: (at, 0, 0)),
            full,
            half,
            whole((STATS, WINDOW)),
            whole((STATS, rows)),
        ],
        [
            jax.ShapeDtypeStruct(tiles, BF16),
            jax.ShapeDtypeStruct((heads, WINDOW, WINDOW), BF16),
            jax.ShapeDtypeStruct((rows, width), F32),
            jax.ShapeDtypeStruct((WINDOW, width), F32),
            jax.ShapeDtypeStruct((STATS, WINDOW), F32),
            jax.ShapeDtypeStruct((STATS, rows), F32),
        ],
        [
            pltpu.VMEM((GROUP,) + piece, BF16),
            pltpu.VMEM((rows, HEAD_DIM), F32),
            pltpu.VMEM((rows, HEAD_DIM), F32),
        ],
        6 * 2 * WINDOW * WINDOW * width * 4,
        16 * WINDOW * width * 2,
    )(queries, keys, values, keys_before, values_before, part, gain, cotangent, *prefix)


def norm_body(steps, features, norm_ref, hidden_ref, gain_ref, cot_ref, q_ref, window_ref, lse_ref, *rest):
    out_ref, grad_ref, first_ref, stat_ref = rest[:4]
    outs = rest[4 : 4 + GROUP]
    held, recip, pull = rest[4 + GROUP :]
    rows = q_ref.shape[0]
    start = lax.axis_index("ctx") * rows
    at_step = pl.program_id(0)
    step = q_ref.shape[1] // HEAD_DIM

    @pl.when(at_step == 0)
    def _():
        root = 1.0 / jnp.sqrt(norm_ref[0:1, :] / features + EPSILON)
        slope = root * root * root * norm_ref[1:2, :] / features
        recip[...] = jnp.broadcast_to(root, (HEAD_DIM, rows)).T
        pull[...] = jnp.broadcast_to(slope, (HEAD_DIM, rows)).T
        stat_ref[...] = jnp.zeros_like(stat_ref)
        stat_ref[:STATS, :] = lse_ref[...]

    columns = coef_column(start, rows)
    for head in range(step):
        cols = slice(head * HEAD_DIM, (head + 1) * HEAD_DIM)
        hidden = hidden_ref[:, cols]
        gain = gain_ref[:, cols].astype(F32)
        kept = recip[...]
        out_ref[:, cols] = (hidden * kept * gain).astype(BF16)
        full = kept * (gain * cot_ref[:, cols].astype(F32)) - hidden * pull[...]
        grad = full.astype(BF16)
        grad_ref[:, cols] = grad
        first_ref[:, cols] = grad[:WINDOW]
        delta = (grad[:WINDOW].astype(F32) * window_ref[:, cols]).T
        stat_ref[pl.ds(STATS + at_step * step + head, 1), :] = jnp.sum(delta, 0, keepdims=True)
        state = dot_tn(q_ref[:, cols], (full * columns).astype(BF16)).astype(BF16)
        store_state(held, at_step * step + head, state)

    @pl.when(at_step == steps - 1)
    def _():
        spread(held, outs)


def store_state(held, head, state):
    rows = held.shape[1]
    if rows >= HEAD_DIM:
        each = rows // HEAD_DIM
        at = pl.multiple_of(lax.rem(head, each) * HEAD_DIM, HEAD_DIM)
        held[head // each, pl.ds(at, HEAD_DIM), :] = state
    else:
        each = HEAD_DIM // rows
        for part in range(each):
            held[head * each + part] = state[part * rows : (part + 1) * rows]


def normalize(norms, hidden, gain, cotangent, queries, window, lse, features):
    rows, width = queries.shape
    heads = width // HEAD_DIM
    step = heads_a_step(heads)
    steps = heads // step
    wide = step * HEAD_DIM
    piece = (width // GROUP, HEAD_DIM)
    half = pl.BlockSpec((WINDOW, wide), lambda at: (0, at))
    full = pl.BlockSpec((rows, wide), lambda at: (0, at))
    return call(
        lambda *refs: norm_body(steps, features, *refs),
        (steps,),
        [
            whole((STATS, rows)),
            full,
            pl.BlockSpec((1, wide), lambda at: (0, at)),
            full,
            full,
            half,
            whole((STATS, WINDOW)),
        ],
        [full, full, half, whole((2 * STATS, WINDOW))] + [whole(piece)] * GROUP,
        [
            jax.ShapeDtypeStruct((rows, width), BF16),
            jax.ShapeDtypeStruct((rows, width), BF16),
            jax.ShapeDtypeStruct((WINDOW, width), BF16),
            jax.ShapeDtypeStruct((2 * STATS, WINDOW), F32),
        ]
        + [jax.ShapeDtypeStruct(piece, BF16)] * GROUP,
        [
            pltpu.VMEM((GROUP,) + piece, BF16),
            pltpu.VMEM((rows, HEAD_DIM), F32),
            pltpu.VMEM((rows, HEAD_DIM), F32),
        ],
        2 * rows * width * HEAD_DIM,
        14 * rows * width,
    )(norms, hidden, gain, cotangent, queries, window, lse)


def back_body(q_ref, k_ref, v_ref, g_ref, kp_ref, vp_ref, p0_ref, s0_ref, p1_ref, s1_ref, *rest):
    ins = rest[:GROUP]
    dq_ref, dk_ref, dv_ref, held = rest[GROUP:]
    rows = q_ref.shape[0]
    start = lax.axis_index("ctx") * rows
    at_step = pl.program_id(0)
    step = q_ref.shape[1] // HEAD_DIM

    @pl.when(at_step == 0)
    def _():
        collect(ins, held)

    keys_at, queries_at = tile_iotas()
    causal = keys_at <= queries_at
    columns = coef_column(start, rows)
    ratios = coef_row(start, rows) * (1.0 / SCALE)
    for head in range(step):
        cols = slice(head * HEAD_DIM, (head + 1) * HEAD_DIM)
        early, late = slice(0, WINDOW), slice(WINDOW, 2 * WINDOW)
        grads = g_ref[early, cols], g_ref[late, cols]
        queries = q_ref[early, cols], q_ref[late, cols]
        keys = kp_ref[:, cols], k_ref[early, cols], k_ref[late, cols]
        values = vp_ref[:, cols], v_ref[early, cols], v_ref[late, cols]
        probs = (
            (p0_ref[head, 0].astype(F32), p0_ref[head, 1].astype(F32)),
            (p1_ref[head, 0].astype(F32), p1_ref[head, 1].astype(F32)),
        )
        edges = []
        for half in range(2):
            ratio = ratios[:, half * WINDOW : (half + 1) * WINDOW]
            pulls = [dot_nt(values[half + at], grads[half]) for at in range(2)]
            delta = jnp.sum(probs[half][0] * pulls[0] + probs[half][1] * pulls[1], 0, keepdims=True)
            before = probs[half][0] * (pulls[0] - delta)
            if half == 1:
                before = before + pulls[0] * ratio
            here = probs[half][1] * (pulls[1] - delta) + jnp.where(causal, pulls[1] * ratio, 0.0)
            edges.append((before.astype(BF16), here.astype(BF16)))
        state = held_state(held, at_step * step + head)
        inner = [
            (dot_tn(keys[half], edges[half][0]) + dot_tn(keys[half + 1], edges[half][1])).T * SCALE for half in range(2)
        ]
        carried = columns * dot_nt(g_ref[:, cols], state)
        dq_ref[:, cols] = (jnp.concatenate(inner, 0) + carried).astype(BF16)
        dk_ref[early, cols] = SCALE * (dot_nn(edges[0][1], queries[0]) + dot_nn(edges[1][0], queries[1]))
        dk_ref[late, cols] = SCALE * dot_nn(edges[1][1], queries[1])
        dv_ref[early, cols] = dot_nn(s0_ref[head], grads[0]) + dot_nn(s1_ref[head, 0], grads[1])
        dv_ref[late, cols] = dot_nn(s1_ref[head, 1], grads[1])


def backward(queries, keys, values, grads, keys_before, values_before, probs0, sums0, probs1, sums1, prefix):
    rows, width = keys.shape
    heads = width // HEAD_DIM
    step = heads_a_step(heads)
    wide = step * HEAD_DIM
    piece = prefix[0].shape
    half = pl.BlockSpec((WINDOW, wide), lambda at: (0, at))
    full = pl.BlockSpec((rows, wide), lambda at: (0, at))
    pair = pl.BlockSpec((step, 2, WINDOW, WINDOW), lambda at: (at, 0, 0, 0))
    single = pl.BlockSpec((step, WINDOW, WINDOW), lambda at: (at, 0, 0))
    return call(
        back_body,
        (heads // step,),
        [full, full, full, full, half, half, pair, single, pair, pair] + [whole(piece)] * GROUP,
        [full, full, full],
        [
            jax.ShapeDtypeStruct((rows, width), BF16),
            jax.ShapeDtypeStruct((rows, width), F32),
            jax.ShapeDtypeStruct((rows, width), F32),
        ],
        [pltpu.VMEM((GROUP,) + piece, BF16)],
        16 * 2 * WINDOW * WINDOW * width * 2,
        40 * WINDOW * width * 2,
    )(queries, keys, values, grads, keys_before, values_before, probs0, sums0, probs1, sums1, *prefix)


def last_body(last, k_ref, v_ref, dk_in, dv_in, qn_ref, gn_ref, stat_ref, *rest):
    ins = rest[:GROUP]
    dk_ref, dv_ref, held = rest[GROUP:]
    at_step = pl.program_id(0)
    step = k_ref.shape[1] // HEAD_DIM

    @pl.when(at_step == 0)
    def _():
        collect(ins, held)

    keys_at, queries_at = tile_iotas()
    beyond = jnp.where(lax.axis_index("ctx") < last, 0, 2 * WINDOW)
    mask = keys_at > queries_at + beyond
    for head in range(step):
        cols = slice(head * HEAD_DIM, (head + 1) * HEAD_DIM)
        at = at_step * step + head
        early, late = slice(0, WINDOW), slice(WINDOW, 2 * WINDOW)
        query, grad = qn_ref[:, cols], gn_ref[:, cols]
        lse = stat_ref[pl.ds(at, 1), :] * (1.0 / LN2)
        delta = stat_ref[pl.ds(STATS + at, 1), :]
        scores = dot_nt(k_ref[late, cols], query) * SCALE_LOG2
        probs = jnp.where(mask, jnp.exp2(scores - lse), 0.0)
        edges = probs * (dot_nt(v_ref[late, cols], grad) - delta)
        state = held_state(held, at)
        keys = dk_in[:, cols] + dot_nt(v_ref[:, cols], state)
        values = dv_in[:, cols] + dot_nn(k_ref[:, cols], state)
        dk_ref[early, cols] = keys[early].astype(BF16)
        dv_ref[early, cols] = values[early].astype(BF16)
        dk_ref[late, cols] = (keys[late] + SCALE * dot_nn(edges.astype(BF16), query)).astype(BF16)
        dv_ref[late, cols] = (values[late] + dot_nn(probs.astype(BF16), grad)).astype(BF16)


def finish(keys, values, dk_part, dv_part, queries_after, grads_after, stats_after, suffix):
    rows, width = keys.shape
    heads = width // HEAD_DIM
    step = heads_a_step(heads)
    wide = step * HEAD_DIM
    piece = suffix[0].shape
    last = lax.axis_size("ctx") - 1
    half = pl.BlockSpec((WINDOW, wide), lambda at: (0, at))
    full = pl.BlockSpec((rows, wide), lambda at: (0, at))
    return call(
        lambda *refs: last_body(last, *refs),
        (heads // step,),
        [full, full, full, full, half, half, whole((2 * STATS, WINDOW))] + [whole(piece)] * GROUP,
        [full, full],
        [jax.ShapeDtypeStruct((rows, width), BF16)] * 2,
        [pltpu.VMEM((GROUP,) + piece, BF16)],
        8 * 2 * WINDOW * WINDOW * width,
        18 * rows * width,
    )(keys, values, dk_part, dv_part, queries_after, grads_after, stats_after, *suffix)


def on_device(queries, keys, values, gain, cotangent):
    rows, width = queries.shape
    features = width * lax.axis_size("head")
    gain = gain.reshape(1, width)
    keys_before = turn(keys[rows - WINDOW :], 1)
    values_before = turn(values[rows - WINDOW :], 1)
    prefix = scan(local_states(keys, values), False)
    queries_after = turn(queries[:WINDOW], -1)
    probs1, sums1, part = late_rows(queries, keys, values)
    probs0, sums0, hidden, window, lse, norms = middle(
        queries, keys, values, keys_before, values_before, part, gain, cotangent, prefix
    )
    norms = lax.psum(norms, "head")
    output, grads, first, stats, *states = normalize(norms, hidden, gain, cotangent, queries, window, lse, features)
    grads_after = turn(first, -1)
    stats_after = turn(stats, -1)
    suffix = scan(states, True)
    grad_queries, dk_part, dv_part = backward(
        queries, keys, values, grads, keys_before, values_before, probs0, sums0, probs1, sums1, prefix
    )
    grad_keys, grad_values = finish(
        keys, values, dk_part, dv_part, queries_after, grads_after, stats_after, suffix
    )
    return output, grad_queries, grad_keys, grad_values


def solution(mesh):
    wide = P("ctx", "head")
    return jax.shard_map(
        on_device,
        mesh=mesh,
        in_specs=(wide, wide, wide, P("head"), wide),
        out_specs=(wide, wide, wide, wide),
        check_vma=False,
    )
```

```python
import math

import jax
import jax.numpy as jnp
from jax import lax
from jax.experimental import pallas as pl
from jax.experimental.pallas import tpu as pltpu
from jax.sharding import PartitionSpec as P

HEAD_DIM = 128
WINDOW = 256
GROUP = 4
HOLDERS = 3
STATS = 8
EPSILON = 1e-06
SCALE = 1.0 / math.sqrt(HEAD_DIM)
SCALE_LOG2 = SCALE * math.log2(math.e)
LN2 = math.log(2.0)
MASKED = -1e30
BF16 = jnp.bfloat16
F32 = jnp.float32
VMEM_LIMIT = 16 * 1024 * 1024
VMEM_MOST = 60 * 1024 * 1024


def dot_nn(left, right):
    return lax.dot_general(left, right, (((1,), (0,)), ((), ())), preferred_element_type=F32)


def dot_nt(left, right):
    return lax.dot_general(left, right, (((1,), (1,)), ((), ())), preferred_element_type=F32)


def dot_tn(left, right):
    return lax.dot_general(left, right, (((0,), (0,)), ((), ())), preferred_element_type=F32)


def tile_iotas():
    keys_at = lax.broadcasted_iota(jnp.int32, (WINDOW, WINDOW), 0)
    queries_at = lax.broadcasted_iota(jnp.int32, (WINDOW, WINDOW), 1)
    return keys_at, queries_at


def coef_row(start, count):
    at = start + lax.broadcasted_iota(jnp.int32, (1, count), 1)
    return 1.0 / jnp.sqrt(HEAD_DIM * (at + 1).astype(F32))


def coef_column(start, count):
    at = start + lax.broadcasted_iota(jnp.int32, (count, HEAD_DIM), 0)
    return 1.0 / jnp.sqrt(HEAD_DIM * (at + 1).astype(F32))


def heads_a_step(heads):
    return 2 if heads % 2 == 0 else 1


def chunks_of(heads):
    return 2 if heads % 4 == 0 else 1


def call(body, grid, in_specs, out_specs, out_shape, scratch, flops, moved, operands, aliases=None, along=(), after=(), vmem=VMEM_LIMIT):
    inputs, results, handed, skipped = len(operands), len(out_shape), len(along), len(after)

    def run(*refs):
        outs = inputs + handed + skipped
        body(*refs[:inputs], *refs[outs : outs + results], *refs[outs + results + handed :])

    given = pl.pallas_call(
        run,
        grid=grid,
        input_output_aliases={**(aliases or {}), **{inputs + at: results + at for at in range(handed)}},
        in_specs=list(in_specs) + [ANY] * (handed + skipped),
        out_specs=list(out_specs) + [ANY] * handed,
        out_shape=list(out_shape) + [jax.ShapeDtypeStruct(array.shape, array.dtype) for array in along],
        scratch_shapes=scratch,
        compiler_params=pltpu.CompilerParams(
            vmem_limit_bytes=vmem,
            dimension_semantics=("arbitrary",) * len(grid),
        ),
        cost_estimate=pl.CostEstimate(flops=flops, bytes_accessed=moved, transcendentals=0),
    )(*operands, *along, *after)
    return list(given[:results]), list(given[results:])


ANY = pl.BlockSpec(memory_space=pl.ANY)
HBM = pl.BlockSpec(memory_space=pltpu.HBM)


def chunk_spec(rows, wide, chunk, steps):
    return pl.BlockSpec((rows, wide), lambda at: (0, jnp.clip(at - chunk * steps, 0, steps - 1)))


def whole(shape):
    return pl.BlockSpec(shape, lambda *_: (0,) * len(shape))


def heads_a_part(heads):
    return -(-heads // HOLDERS)


def part_shape(heads):
    return (heads_a_part(heads) * HEAD_DIM, HEAD_DIM)


def part_at(held, head, reverse):
    each = held.shape[1] // HEAD_DIM
    at = lax.rem(head, each) * HEAD_DIM
    if not isinstance(at, int):
        at = pl.multiple_of(at, HEAD_DIM)
    return head // each + (GROUP - HOLDERS if reverse else 0), pl.ds(at, HEAD_DIM)


def store_state(held, head, state, reverse):
    slot, rows = part_at(held, head, reverse)
    held[slot, rows, :] = state


def held_state(held, head, reverse):
    slot, rows = part_at(held, head, reverse)
    return held[slot, rows, :]


def spread(held, outs):
    place = lax.rem(lax.axis_index("ctx"), GROUP)
    for other in range(GROUP):
        outs[other][...] = held[lax.bitwise_xor(place, jnp.int32(other))]


def collect(ins, held):
    place = lax.rem(lax.axis_index("ctx"), GROUP)
    for other in range(GROUP):
        held[lax.bitwise_xor(place, jnp.int32(other))] = ins[other][...]


def state_body(steps, k_ref, v_ref, *rest):
    outs, tails = rest[:GROUP], rest[GROUP:-4]
    k_held, v_held, held, done = rest[-4:]
    rows, width = k_held.shape
    wide = width // steps
    chunks = len(tails)
    columns = width // chunks
    loads, sends = [], {}
    for step in range(steps):
        cols = pl.ds(step * wide, wide)
        for at, (source, target) in enumerate(((k_ref, k_held), (v_ref, v_held))):
            loads.append(pltpu.make_async_copy(source.at[:, cols], target.at[:, cols], done.at[2 * step + at]))
    for step in range(steps):
        cols = pl.ds(step * wide, wide)
        chunk = step * wide // columns
        sends[step] = [
            pltpu.make_async_copy(
                source.at[pl.ds(rows - WINDOW, WINDOW), cols],
                tails[chunk].at[pl.ds(at * WINDOW, WINDOW), pl.ds(step * wide - chunk * columns, wide)],
                done.at[2 * (steps + step) + at],
            )
            for at, source in enumerate((k_held, v_held))
        ]
    held[...] = jnp.zeros_like(held)
    for copy in loads:
        copy.start()
    for step in range(steps):
        loads[2 * step].wait()
        loads[2 * step + 1].wait()
        for copy in sends[step]:
            copy.start()
        for head in range(step * wide // HEAD_DIM, (step + 1) * wide // HEAD_DIM):
            cols = slice(head * HEAD_DIM, (head + 1) * HEAD_DIM)
            store_state(held, head, dot_tn(k_held[:, cols], v_held[:, cols]).astype(BF16), False)
    spread(held, outs)
    for step in range(steps):
        for copy in sends[step]:
            copy.wait()


def local_states(keys, values):
    rows, width = keys.shape
    heads = width // HEAD_DIM
    chunks = chunks_of(heads)
    steps = heads // heads_a_step(heads)
    piece = part_shape(heads)
    tail = (2 * WINDOW, width // chunks)
    results, _ = call(
        lambda *refs: state_body(steps, *refs),
        (1,),
        [HBM] * 2,
        [whole(piece)] * GROUP + [ANY] * chunks,
        [jax.ShapeDtypeStruct(piece, BF16)] * GROUP + [jax.ShapeDtypeStruct(tail, BF16)] * chunks,
        [
            pltpu.VMEM((rows, width), BF16),
            pltpu.VMEM((rows, width), BF16),
            pltpu.VMEM((GROUP,) + piece, BF16),
            pltpu.SemaphoreType.DMA((4 * steps,)),
        ],
        2 * rows * width * HEAD_DIM,
        2 * 2 * rows * width,
        [keys, values],
        vmem=VMEM_MOST,
    )
    return results[:GROUP], results[GROUP:]


def total_body(*refs):
    total = refs[0][...].astype(F32)
    for ref in refs[1:-1]:
        total = total + ref[...].astype(F32)
    refs[-1][...] = total.astype(refs[-1].dtype)


def merge_body(reverse, groups, *refs):
    block = lax.axis_index("ctx")
    group = block // GROUP
    place = lax.rem(block, GROUP)
    others = refs[: groups - 1]
    own = refs[groups - 1 : groups - 1 + GROUP]
    outs = refs[groups - 1 + GROUP :]
    total = jnp.zeros(outs[0].shape, F32)
    for step in range(1, groups):
        wanted = group + step < groups if reverse else group - step >= 0
        total = total + others[step - 1][...].astype(F32) * wanted.astype(F32)
    for target in range(GROUP):
        to = lax.bitwise_xor(place, jnp.int32(target))
        result = total
        for source in range(GROUP):
            if source == target:
                continue
            of = lax.bitwise_xor(place, jnp.int32(source))
            wanted = of > to if reverse else of < to
            result = result + own[source][...].astype(F32) * wanted.astype(F32)
        outs[target][...] = result.astype(outs[target].dtype)


def swap(value, mask):
    count = lax.axis_size("ctx")
    return lax.ppermute(value, "ctx", [(at, at ^ mask) for at in range(count)])


def turn(value, steps):
    count = lax.axis_size("ctx")
    return lax.ppermute(value, "ctx", [(at, (at + steps) % count) for at in range(count)])


def shift(value, steps, places):
    count = lax.axis_size("ctx")
    return lax.ppermute(
        value, "ctx", [(at, at + steps) for at in range(count) if at % GROUP in places and 0 <= at + steps < count]
    )


def scan(pieces, reverse, first, second):
    groups = lax.axis_size("ctx") // GROUP
    shape = pieces[0].shape
    full = whole(shape)
    size = shape[0] * shape[1]
    out = jax.ShapeDtypeStruct(shape, BF16)
    own = [pieces[0]] + [swap(pieces[other], other) for other in range(1, GROUP)]
    along, after = first()
    (total,), held = call(
        total_body, (1,), [full] * GROUP, [full], [out], [], GROUP * size, 2 * 5 * size, own, None, along, after
    )
    holders = range(GROUP - HOLDERS, GROUP) if reverse else range(HOLDERS)
    others = [shift(total, (-GROUP if reverse else GROUP) * at, holders) for at in range(1, groups)]
    operands = others + own
    along, after = second(total, held)
    merged, held = call(
        lambda *refs: merge_body(reverse, groups, *refs),
        (1,),
        [full] * len(operands),
        [full] * GROUP,
        [out] * GROUP,
        [],
        20 * size,
        2 * 11 * size,
        operands,
        None,
        along,
        after,
    )
    return [merged[0]] + [swap(merged[other], other) for other in range(1, GROUP)], merged, held


def attend(scores, masks, coef, linear):
    shown = [jnp.where(mask, score, MASKED) for score, mask in zip(scores, masks)]
    peak = jnp.max(shown[0], 0, keepdims=True)
    for tile in shown[1:]:
        peak = jnp.maximum(peak, jnp.max(tile, 0, keepdims=True))
    powers = [jnp.exp2((tile - peak) * SCALE_LOG2) for tile in shown]
    norm = jnp.sum(powers[0], 0, keepdims=True)
    for tile in powers[1:]:
        norm = norm + jnp.sum(tile, 0, keepdims=True)
    share = 1.0 / norm
    probs = [tile * share for tile in powers]
    sums = []
    for prob, score, mask, kind in zip(probs, scores, masks, linear):
        if kind == "none":
            sums.append(None)
        elif kind == "all":
            sums.append((prob + score * coef).astype(BF16))
        else:
            sums.append((prob + jnp.where(mask, score * coef, 0.0)).astype(BF16))
    lse = peak * SCALE + jnp.log(norm)
    return [prob.astype(BF16) for prob in probs], sums, lse


def late_body(q_ref, k_ref, v_ref, *rest):
    prob_ref, sum_ref, part_ref = rest[-3:]
    rows = k_ref.shape[0]
    start = lax.axis_index("ctx") * rows
    keys_at, queries_at = tile_iotas()
    coef = coef_row(start + WINDOW, WINDOW)
    masks = [keys_at > queries_at, keys_at <= queries_at]
    for head in range(q_ref.shape[1] // HEAD_DIM):
        cols = slice(head * HEAD_DIM, (head + 1) * HEAD_DIM)
        query = q_ref[:, cols]
        scores = [dot_nt(k_ref[at * WINDOW : (at + 1) * WINDOW, cols], query) for at in range(2)]
        probs, sums, _ = attend(scores, masks, coef, ["all", "masked"])
        total = jnp.zeros((HEAD_DIM, WINDOW), F32)
        for at in range(2):
            prob_ref[head, at] = probs[at]
            sum_ref[head, at] = sums[at]
            total = total + dot_tn(v_ref[at * WINDOW : (at + 1) * WINDOW, cols], sums[at])
        part_ref[:, cols] = total.T


def late_rows(chunk, queries, keys, values, done, along, after):
    rows, width = keys.shape
    heads = width // HEAD_DIM
    step = heads_a_step(heads)
    steps = heads // step // chunks_of(heads)
    ahead = chunk * steps
    tiles = (heads, 2, WINDOW, WINDOW)
    tile_spec = pl.BlockSpec((step,) + tiles[1:], lambda at: (at + ahead, 0, 0, 0))
    wide = step * HEAD_DIM
    return call(
        late_body,
        (steps,),
        [
            pl.BlockSpec((WINDOW, wide), lambda at: (1, at + ahead)),
            pl.BlockSpec((rows, wide), lambda at: (0, at + ahead)),
            pl.BlockSpec((rows, wide), lambda at: (0, at + ahead)),
        ]
        + [ANY] * len(done),
        [tile_spec, tile_spec, pl.BlockSpec((WINDOW, wide), lambda at: (0, at + ahead))],
        [
            jax.ShapeDtypeStruct(tiles, BF16),
            jax.ShapeDtypeStruct(tiles, BF16),
            jax.ShapeDtypeStruct((WINDOW, width), F32),
        ],
        [],
        4 * 2 * WINDOW * WINDOW * width * 2,
        12 * WINDOW * width,
        [queries, keys, values, *done],
        {3 + at: at for at in range(3)} if done else None,
        along,
        after,
    )


def early_body(first, q_ref, k_ref, v_ref, tail_ref, *rest):
    prob_ref, sum_ref, inside_ref, window_ref, lse_ref = rest[-5:]
    done = rest[:-5]
    rows = k_ref.shape[0] * 2
    block = lax.axis_index("ctx")
    at_step = pl.program_id(0)

    @pl.when(at_step == 0)
    def _():
        lse_ref[...] = done[4][...] if done else jnp.zeros_like(lse_ref)

    keys_at, queries_at = tile_iotas()
    beyond = jnp.where(block > 0, 0, 2 * WINDOW)
    masks = [keys_at > queries_at + beyond, keys_at <= queries_at]
    coef = coef_row(block * rows, WINDOW)
    step = q_ref.shape[1] // HEAD_DIM
    for head in range(step):
        cols = slice(head * HEAD_DIM, (head + 1) * HEAD_DIM)
        query = q_ref[:, cols]
        scores = [dot_nt(tail_ref[:WINDOW, cols], query), dot_nt(k_ref[:, cols], query)]
        probs, sums, lse = attend(scores, masks, coef, ["none", "masked"])
        prob_ref[head, 0] = probs[0]
        prob_ref[head, 1] = probs[1]
        sum_ref[head] = sums[1]
        lse_ref[pl.ds(first + at_step * step + head, 1), :] = lse
        value = v_ref[:, cols]
        before = dot_tn(tail_ref[WINDOW:, cols], probs[0])
        window_ref[:, cols] = (before + dot_tn(value, probs[1])).T
        inside_ref[:, cols] = (before + dot_tn(value, sums[1])).T


def early_rows(chunk, queries, keys, values, before, done, along):
    rows, width = keys.shape
    heads = width // HEAD_DIM
    step = heads_a_step(heads)
    steps = heads // step // chunks_of(heads)
    ahead = chunk * steps
    wide = step * HEAD_DIM
    half = pl.BlockSpec((WINDOW, wide), lambda at: (0, at + ahead))
    own = pl.BlockSpec((2 * WINDOW, wide), lambda at: (0, at))
    tiles = (heads, 2, WINDOW, WINDOW)
    small = whole((STATS, WINDOW))
    return call(
        lambda *refs: early_body(ahead * step, *refs),
        (steps,),
        [half, half, half, own] + ([ANY] * 4 + [small] if done else []),
        [
            pl.BlockSpec((step,) + tiles[1:], lambda at: (at + ahead, 0, 0, 0)),
            pl.BlockSpec((step, WINDOW, WINDOW), lambda at: (at + ahead, 0, 0)),
            half,
            half,
            small,
        ],
        [
            jax.ShapeDtypeStruct(tiles, BF16),
            jax.ShapeDtypeStruct((heads, WINDOW, WINDOW), BF16),
            jax.ShapeDtypeStruct((WINDOW, width), F32),
            jax.ShapeDtypeStruct((WINDOW, width), F32),
            jax.ShapeDtypeStruct((STATS, WINDOW), F32),
        ],
        [],
        5 * 2 * WINDOW * WINDOW * width * 2,
        8 * WINDOW * width,
        [queries, keys, values, before, *done],
        {4 + at: at for at in range(4)} if done else None,
        along,
    )


def sum_body(steps, q_ref, inside_ref, part_ref, gain_ref, cot_ref, *rest):
    ins = rest[:GROUP]
    hidden_ref, norm_ref, held, squares, crossed = rest[GROUP:]
    rows = q_ref.shape[0]
    at_step = pl.program_id(0)
    step = q_ref.shape[1] // HEAD_DIM

    @pl.when(at_step == 0)
    def _():
        collect(ins, held)
        squares[...] = jnp.zeros_like(squares)
        crossed[...] = jnp.zeros_like(crossed)

    columns = coef_column(lax.axis_index("ctx") * rows, rows)
    for head in range(step):
        cols = slice(head * HEAD_DIM, (head + 1) * HEAD_DIM)
        carried = columns * dot_nn(q_ref[:, cols], held_state(held, at_step * step + head, False))
        hidden = jnp.concatenate([inside_ref[:, cols], part_ref[:, cols]], 0) + carried
        hidden_ref[:, cols] = hidden
        scaled = gain_ref[:, cols].astype(F32) * cot_ref[:, cols].astype(F32)
        squares[...] += hidden * hidden
        crossed[...] += hidden * scaled

    @pl.when(at_step == steps - 1)
    def _():
        norm_ref[...] = jnp.zeros_like(norm_ref)
        norm_ref[0:1, :] = jnp.sum(squares[...].T, 0, keepdims=True)
        norm_ref[1:2, :] = jnp.sum(crossed[...].T, 0, keepdims=True)


def add_prefix(queries, inside, part, gain, cotangent, prefix):
    rows, width = queries.shape
    heads = width // HEAD_DIM
    step = heads_a_step(heads)
    steps = heads // step
    wide = step * HEAD_DIM
    piece = prefix[0].shape
    half = pl.BlockSpec((WINDOW, wide), lambda at: (0, at))
    full = pl.BlockSpec((rows, wide), lambda at: (0, at))
    return call(
        lambda *refs: sum_body(steps, *refs),
        (steps,),
        [full, half, half, pl.BlockSpec((1, wide), lambda at: (0, at)), full] + [whole(piece)] * GROUP,
        [full, whole((STATS, rows))],
        [jax.ShapeDtypeStruct((rows, width), F32), jax.ShapeDtypeStruct((STATS, rows), F32)],
        [
            pltpu.VMEM((GROUP,) + piece, BF16),
            pltpu.VMEM((rows, HEAD_DIM), F32),
            pltpu.VMEM((rows, HEAD_DIM), F32),
        ],
        2 * rows * width * HEAD_DIM,
        12 * rows * width,
        [queries, inside, part, gain, cotangent, *prefix],
    )[0]


def stat_rows(width):
    return 2 * STATS * -(-3 * WINDOW // width)


def stat_place(width, part):
    across = width // WINDOW
    return (
        slice(WINDOW + part // across * 2 * STATS, WINDOW + (part // across + 1) * 2 * STATS),
        slice(part % across * WINDOW, (part % across + 1) * WINDOW),
    )


def norm_body(steps, features, norm_ref, hidden_ref, gain_ref, cot_ref, q_ref, window_ref, lse_ref, *rest):
    out_ref, grad_ref, first_ref = rest[:3]
    outs = rest[3 : 3 + GROUP]
    held, recip, pull, stats = rest[3 + GROUP :]
    rows, wide = q_ref.shape
    start = lax.axis_index("ctx") * rows
    at_step = pl.program_id(0)
    step = wide // HEAD_DIM

    @pl.when(at_step == 0)
    def _():
        root = 1.0 / jnp.sqrt(norm_ref[0:1, :] / features + EPSILON)
        slope = root * root * root * norm_ref[1:2, :] / features
        recip[...] = jnp.broadcast_to(root, (HEAD_DIM, rows)).T
        pull[...] = jnp.broadcast_to(slope, (HEAD_DIM, rows)).T
        stats[...] = jnp.zeros_like(stats)
        stats[:STATS, :] = lse_ref[...]
        held[...] = jnp.zeros_like(held)

    columns = coef_column(start, rows)
    for head in range(step):
        cols = slice(head * HEAD_DIM, (head + 1) * HEAD_DIM)
        hidden = hidden_ref[:, cols]
        gain = gain_ref[:, cols].astype(F32)
        kept = recip[...]
        out_ref[:, cols] = (hidden * kept * gain).astype(BF16)
        full = kept * (gain * cot_ref[:, cols].astype(F32)) - hidden * pull[...]
        grad = full.astype(BF16)
        grad_ref[:, cols] = grad
        first_ref[:WINDOW, pl.ds(pl.multiple_of(at_step * wide, HEAD_DIM) + head * HEAD_DIM, HEAD_DIM)] = grad[:WINDOW]
        delta = (grad[:WINDOW].astype(F32) * window_ref[:, cols]).T
        stats[pl.ds(STATS + at_step * step + head, 1), :] = jnp.sum(delta, 0, keepdims=True)
        state = dot_tn(q_ref[:, cols], (full * columns).astype(BF16)).astype(BF16)
        store_state(held, at_step * step + head, state, True)

    @pl.when(at_step == steps - 1)
    def _():
        spread(held, outs)
        left = stats[...]
        first_ref[WINDOW:, :] = jnp.zeros((first_ref.shape[0] - WINDOW, first_ref.shape[1]), BF16)
        for part in range(3):
            at_rows, at_cols = stat_place(first_ref.shape[1], part)
            taken = left.astype(BF16)
            first_ref[at_rows, at_cols] = taken
            left = left - taken.astype(F32)


def normalize(norms, hidden, gain, cotangent, queries, window, lse, features):
    rows, width = queries.shape
    heads = width // HEAD_DIM
    step = heads_a_step(heads)
    steps = heads // step
    wide = step * HEAD_DIM
    piece = part_shape(heads)
    first = (WINDOW + stat_rows(width), width)
    half = pl.BlockSpec((WINDOW, wide), lambda at: (0, at))
    full = pl.BlockSpec((rows, wide), lambda at: (0, at))
    return call(
        lambda *refs: norm_body(steps, features, *refs),
        (steps,),
        [
            whole((STATS, rows)),
            full,
            pl.BlockSpec((1, wide), lambda at: (0, at)),
            full,
            full,
            half,
            whole((STATS, WINDOW)),
        ],
        [full, full, whole(first)] + [whole(piece)] * GROUP,
        [
            jax.ShapeDtypeStruct((rows, width), BF16),
            jax.ShapeDtypeStruct((rows, width), BF16),
            jax.ShapeDtypeStruct(first, BF16),
        ]
        + [jax.ShapeDtypeStruct(piece, BF16)] * GROUP,
        [
            pltpu.VMEM((GROUP,) + piece, BF16),
            pltpu.VMEM((rows, HEAD_DIM), F32),
            pltpu.VMEM((rows, HEAD_DIM), F32),
            pltpu.VMEM((2 * STATS, WINDOW), F32),
        ],
        2 * rows * width * HEAD_DIM,
        14 * rows * width,
        [norms, hidden, gain, cotangent, queries, window, lse],
    )[0]


def back_body(first, q_ref, k_ref, v_ref, g_ref, tail_ref, p0_ref, s0_ref, p1_ref, s1_ref, *rest):
    ins = rest[:GROUP]
    dq_ref, dk_ref, dv_ref, held = rest[-4:]
    rows = q_ref.shape[0]
    start = lax.axis_index("ctx") * rows
    at_step = pl.program_id(0)
    step = q_ref.shape[1] // HEAD_DIM

    @pl.when(at_step == 0)
    def _():
        collect(ins, held)

    keys_at, queries_at = tile_iotas()
    causal = keys_at <= queries_at
    columns = coef_column(start, rows)
    ratios = coef_row(start, rows) * (1.0 / SCALE)
    for head in range(step):
        cols = slice(head * HEAD_DIM, (head + 1) * HEAD_DIM)
        early, late = slice(0, WINDOW), slice(WINDOW, 2 * WINDOW)
        grads = g_ref[early, cols], g_ref[late, cols]
        queries = q_ref[early, cols], q_ref[late, cols]
        keys = tail_ref[:WINDOW, cols], k_ref[early, cols], k_ref[late, cols]
        values = tail_ref[WINDOW:, cols], v_ref[early, cols], v_ref[late, cols]
        probs = (
            (p0_ref[head, 0].astype(F32), p0_ref[head, 1].astype(F32)),
            (p1_ref[head, 0].astype(F32), p1_ref[head, 1].astype(F32)),
        )
        edges = []
        for half in range(2):
            ratio = ratios[:, half * WINDOW : (half + 1) * WINDOW]
            pulls = [dot_nt(values[half + at], grads[half]) for at in range(2)]
            delta = jnp.sum(probs[half][0] * pulls[0] + probs[half][1] * pulls[1], 0, keepdims=True)
            before = probs[half][0] * (pulls[0] - delta)
            if half == 1:
                before = before + pulls[0] * ratio
            here = probs[half][1] * (pulls[1] - delta) + jnp.where(causal, pulls[1] * ratio, 0.0)
            edges.append((before.astype(BF16), here.astype(BF16)))
        state = held_state(held, first + at_step * step + head, False)
        inner = [
            (dot_tn(keys[half], edges[half][0]) + dot_tn(keys[half + 1], edges[half][1])).T * SCALE for half in range(2)
        ]
        carried = columns * dot_nt(g_ref[:, cols], state)
        dq_ref[:, cols] = (jnp.concatenate(inner, 0) + carried).astype(BF16)
        dk_ref[early, cols] = SCALE * (dot_nn(edges[0][1], queries[0]) + dot_nn(edges[1][0], queries[1]))
        dk_ref[late, cols] = SCALE * dot_nn(edges[1][1], queries[1])
        dv_ref[early, cols] = dot_nn(s0_ref[head], grads[0]) + dot_nn(s1_ref[head, 0], grads[1])
        dv_ref[late, cols] = dot_nn(s1_ref[head, 1], grads[1])


def backward(chunk, queries, keys, values, grads, before, probs0, sums0, probs1, sums1, prefix, done, along, after):
    rows, width = keys.shape
    heads = width // HEAD_DIM
    chunks = chunks_of(heads)
    step = heads_a_step(heads)
    steps = heads // step // chunks
    ahead = chunk * steps
    wide = step * HEAD_DIM
    piece = prefix[0].shape
    own_tail = pl.BlockSpec((2 * WINDOW, wide), lambda at: (0, at))
    own_full = pl.BlockSpec((rows, wide), lambda at: (0, at))
    full = pl.BlockSpec((rows, wide), lambda at: (0, at + ahead))
    pair = pl.BlockSpec((step, 2, WINDOW, WINDOW), lambda at: (at + ahead, 0, 0, 0))
    single = pl.BlockSpec((step, WINDOW, WINDOW), lambda at: (at + ahead, 0, 0))
    return call(
        lambda *refs: back_body(ahead * step, *refs),
        (steps,),
        [full, full, full, full, own_tail, pair, single, pair, pair] + [whole(piece)] * GROUP + [ANY] * len(done),
        [full, own_full, own_full],
        [
            jax.ShapeDtypeStruct((rows, width), BF16),
            jax.ShapeDtypeStruct((rows, width // chunks), F32),
            jax.ShapeDtypeStruct((rows, width // chunks), F32),
        ],
        [pltpu.VMEM((GROUP,) + piece, BF16)],
        8 * 2 * WINDOW * WINDOW * width * 2,
        20 * WINDOW * width * 2,
        [queries, keys, values, grads, before, probs0, sums0, probs1, sums1, *prefix, *done],
        {9 + GROUP: 0} if done else None,
        along,
        after,
    )


def last_body(first, last, k_ref, v_ref, dk_in, dv_in, qn_ref, gn_ref, sent_ref, *rest):
    ins = rest[:GROUP]
    dk_ref, dv_ref, held, stats = rest[-4:]
    at_step = pl.program_id(0)
    step = k_ref.shape[1] // HEAD_DIM

    @pl.when(at_step == 0)
    def _():
        collect(ins, held)
        total = jnp.zeros(stats.shape, F32)
        for part in range(3):
            at_rows, at_cols = stat_place(sent_ref.shape[1], 2 - part)
            total = total + sent_ref[at_rows, at_cols].astype(F32)
        stats[...] = total

    keys_at, queries_at = tile_iotas()
    beyond = jnp.where(lax.axis_index("ctx") < last, 0, 2 * WINDOW)
    mask = keys_at > queries_at + beyond
    for head in range(step):
        cols = slice(head * HEAD_DIM, (head + 1) * HEAD_DIM)
        at = first + at_step * step + head
        early, late = slice(0, WINDOW), slice(WINDOW, 2 * WINDOW)
        query, grad = qn_ref[:, cols], gn_ref[:, cols]
        lse = stats[pl.ds(at, 1), :] * (1.0 / LN2)
        delta = stats[pl.ds(STATS + at, 1), :]
        scores = dot_nt(k_ref[late, cols], query) * SCALE_LOG2
        probs = jnp.where(mask, jnp.exp2(scores - lse), 0.0)
        edges = probs * (dot_nt(v_ref[late, cols], grad) - delta)
        state = held_state(held, at, True)
        keys = dk_in[:, cols] + dot_nt(v_ref[:, cols], state)
        values = dv_in[:, cols] + dot_nn(k_ref[:, cols], state)
        dk_ref[early, cols] = keys[early].astype(BF16)
        dv_ref[early, cols] = values[early].astype(BF16)
        dk_ref[late, cols] = (keys[late] + SCALE * dot_nn(edges.astype(BF16), query)).astype(BF16)
        dv_ref[late, cols] = (values[late] + dot_nn(probs.astype(BF16), grad)).astype(BF16)


def finish(chunk, keys, values, dk_part, dv_part, queries_after, grads_after, suffix, done):
    rows, width = keys.shape
    heads = width // HEAD_DIM
    step = heads_a_step(heads)
    steps = heads // step // chunks_of(heads)
    ahead = chunk * steps
    wide = step * HEAD_DIM
    piece = suffix[0].shape
    last = lax.axis_size("ctx") - 1
    half = pl.BlockSpec((WINDOW, wide), lambda at: (0, at + ahead))
    own_full = pl.BlockSpec((rows, wide), lambda at: (0, at))
    full = pl.BlockSpec((rows, wide), lambda at: (0, at + ahead))
    return call(
        lambda *refs: last_body(ahead * step, last, *refs),
        (steps,),
        [full, full, own_full, own_full, half, half, whole(grads_after.shape)] + [whole(piece)] * GROUP + [ANY] * len(done),
        [full, full],
        [jax.ShapeDtypeStruct((rows, width), BF16)] * 2,
        [pltpu.VMEM((GROUP,) + piece, BF16), pltpu.VMEM((2 * STATS, WINDOW), F32)],
        4 * 2 * WINDOW * WINDOW * width,
        9 * rows * width,
        [keys, values, dk_part, dv_part, queries_after, grads_after, grads_after, *suffix, *done],
        {7 + GROUP: 0, 8 + GROUP: 1} if done else None,
    )[0]


def summed(value, axis):
    count = lax.axis_size(axis)
    mask = 1
    while mask < count:
        value = value + lax.ppermute(value, axis, [(at, at ^ mask) for at in range(count)])
        mask *= 2
    return value


def on_device(queries, keys, values, gain, cotangent):
    rows, width = queries.shape
    features = width * lax.axis_size("head")
    chunks = chunks_of(width // HEAD_DIM)
    gain = gain.reshape(1, width)
    before, own = [], {}

    pieces, tails = local_states(keys, values)

    def send_tails(total, held):
        before.extend(turn(tail, 1) for tail in held)
        return [], []

    prefix, merged, _ = scan(pieces, False, lambda: (tails, []), send_tails)
    late = []
    for chunk in range(chunks):
        late, _ = late_rows(chunk, queries, keys, values, late, [], merged[:1])
    probs1, sums1, part = late
    early, handed = [], [queries[:WINDOW]]
    for chunk in range(chunks):
        early, sent = early_rows(chunk, queries, keys, values, before[chunk], early, handed)
        if chunk == 0:
            after, handed = turn(sent[0], -1), []
    probs0, sums0, inside, window, lse = early
    hidden, norms = add_prefix(queries, inside, part, gain, cotangent, prefix)
    norms = summed(norms, "head")
    output, grads, first, *states = normalize(norms, hidden, gain, cotangent, queries, window, lse, features)

    def own_chunk(chunk, after):
        own[chunk], _ = backward(
            chunk, queries, keys, values, grads, before[chunk], probs0, sums0, probs1, sums1, prefix,
            own[chunk - 1][:1] if chunk else [], [], after,
        )

    def send_grads(total, held):
        grads_after.append(turn(held[0], -1))
        return [], []

    grads_after = []
    own_chunk(0, [])
    suffix, merged, _ = scan(states, True, lambda: ([first], [after, own[0][1]]), send_grads)
    for chunk in range(1, chunks):
        own_chunk(chunk, merged[:1])
    result = []
    for chunk in range(chunks):
        _, dk_part, dv_part = own[chunk]
        result = finish(chunk, keys, values, dk_part, dv_part, after, grads_after[0], suffix, result)
    return output, own[chunks - 1][0], *result


def solution(mesh):
    wide = P("ctx", "head")
    return jax.shard_map(
        on_device,
        mesh=mesh,
        in_specs=(wide, wide, wide, P("head"), wide),
        out_specs=(wide, wide, wide, wide),
        check_vma=False,
    )
```

```python
import math

import jax
import jax.numpy as jnp
from jax import lax
from jax.experimental import pallas as pl
from jax.experimental.pallas import tpu as pltpu
from jax.sharding import PartitionSpec as P

HEAD_DIM = 128
WINDOW = 256
GROUP = 4
HOLDERS = 3
STATS = 8
AHEAD = 192
EPSILON = 1e-06
SCALE = 1.0 / math.sqrt(HEAD_DIM)
SCALE_LOG2 = SCALE * math.log2(math.e)
LN2 = math.log(2.0)
MASKED = -1e30
BF16 = jnp.bfloat16
F32 = jnp.float32
VMEM_LIMIT = 24 * 1024 * 1024
VMEM_MOST = 60 * 1024 * 1024


def dot_nn(left, right):
    return lax.dot_general(left, right, (((1,), (0,)), ((), ())), preferred_element_type=F32)


def dot_nt(left, right):
    return lax.dot_general(left, right, (((1,), (1,)), ((), ())), preferred_element_type=F32)


def dot_tn(left, right):
    return lax.dot_general(left, right, (((0,), (0,)), ((), ())), preferred_element_type=F32)


def tile_iotas():
    keys_at = lax.broadcasted_iota(jnp.int32, (WINDOW, WINDOW), 0)
    queries_at = lax.broadcasted_iota(jnp.int32, (WINDOW, WINDOW), 1)
    return keys_at, queries_at


def coef_row(start, count):
    at = start + lax.broadcasted_iota(jnp.int32, (1, count), 1)
    return 1.0 / jnp.sqrt(HEAD_DIM * (at + 1).astype(F32))


def coef_column(start, count):
    at = start + lax.broadcasted_iota(jnp.int32, (count, HEAD_DIM), 0)
    return 1.0 / jnp.sqrt(HEAD_DIM * (at + 1).astype(F32))


def heads_a_step(heads):
    return 2 if heads % 2 == 0 else 1


def sent_chunks(heads):
    return [(0, 2), (2, heads - 2)] if heads > 2 else [(0, heads)]


def even_chunks(heads):
    return [(0, heads // 2), (heads // 2, heads - heads // 2)] if heads > 1 else [(0, 1)]


def picked(chunks, refs, head):
    for (first, count), ref in zip(chunks, refs):
        if first <= head < first + count:
            return ref, head - first
    raise ValueError


def columns_of(head):
    return slice(head * HEAD_DIM, (head + 1) * HEAD_DIM)


def call(body, grid, in_specs, out_specs, out_shape, scratch, flops, moved, operands, aliases=None, along=(), after=(), vmem=VMEM_LIMIT):
    inputs, results, handed, skipped = len(operands), len(out_shape), len(along), len(after)

    def run(*refs):
        outs = inputs + handed + skipped
        body(*refs[:inputs], *refs[outs : outs + results], *refs[outs + results + handed :])

    given = pl.pallas_call(
        run,
        grid=grid,
        input_output_aliases={**(aliases or {}), **{inputs + at: results + at for at in range(handed)}},
        in_specs=list(in_specs) + [ANY] * (handed + skipped),
        out_specs=list(out_specs) + [ANY] * handed,
        out_shape=list(out_shape) + [jax.ShapeDtypeStruct(array.shape, array.dtype) for array in along],
        scratch_shapes=scratch,
        compiler_params=pltpu.CompilerParams(
            vmem_limit_bytes=vmem,
            dimension_semantics=("arbitrary",) * len(grid),
        ),
        cost_estimate=pl.CostEstimate(flops=flops, bytes_accessed=moved, transcendentals=0),
    )(*operands, *along, *after)
    return list(given[:results]), list(given[results:])


def run_once(body, operands, results, scratch, flops, moved, along=(), after=(), pushed=()):
    return call(
        body,
        (1,),
        [whole(array.shape) for array in operands],
        [HBM if at in pushed else whole(shape) for at, (shape, _) in enumerate(results)],
        [jax.ShapeDtypeStruct(shape, kind) for shape, kind in results],
        scratch,
        flops,
        moved,
        operands,
        None,
        along,
        after,
    )


def push(held, out, done, head, copies):
    step = heads_a_step(held.shape[1] // HEAD_DIM)
    if head % step == step - 1:
        cols = pl.ds((head + 1 - step) * HEAD_DIM, step * HEAD_DIM)
        copy = pltpu.make_async_copy(held.at[:, cols], out.at[:, cols], done.at[head // step])
        copy.start()
        copies.append(copy)


ANY = pl.BlockSpec(memory_space=pl.ANY)
HBM = pl.BlockSpec(memory_space=pltpu.HBM)


def whole(shape):
    return pl.BlockSpec(shape, lambda *_: (0,) * len(shape))


def heads_a_part(heads):
    return -(-heads // HOLDERS)


def part_shape(heads):
    return (heads_a_part(heads) * HEAD_DIM, HEAD_DIM)


def part_at(held, head, reverse):
    each = held.shape[1] // HEAD_DIM
    at = lax.rem(head, each) * HEAD_DIM
    if not isinstance(at, int):
        at = pl.multiple_of(at, HEAD_DIM)
    return head // each + (GROUP - HOLDERS if reverse else 0), pl.ds(at, HEAD_DIM)


def store_state(held, head, state, reverse):
    slot, rows = part_at(held, head, reverse)
    held[slot, rows, :] = state


def held_state(held, head, reverse):
    slot, rows = part_at(held, head, reverse)
    return held[slot, rows, :]


def spread(held, outs):
    place = lax.rem(lax.axis_index("ctx"), GROUP)
    for other in range(GROUP):
        outs[other][...] = held[lax.bitwise_xor(place, jnp.int32(other))]


def collect(ins, held):
    place = lax.rem(lax.axis_index("ctx"), GROUP)
    for other in range(GROUP):
        held[lax.bitwise_xor(place, jnp.int32(other))] = ins[other][...]


def state_body(steps, k_ref, v_ref, *rest):
    outs, tails = rest[:GROUP], rest[GROUP:-4]
    k_held, v_held, held, done = rest[-4:]
    rows, width = k_held.shape
    wide = width // steps
    chunks = sent_chunks(width // HEAD_DIM)
    loads, sends = [], {}
    for step in range(steps):
        cols = pl.ds(step * wide, wide)
        for at, (source, target) in enumerate(((k_ref, k_held), (v_ref, v_held))):
            loads.append(pltpu.make_async_copy(source.at[:, cols], target.at[:, cols], done.at[2 * step + at]))
    for step in range(steps):
        cols = pl.ds(step * wide, wide)
        tail, place = picked(chunks, tails, step * wide // HEAD_DIM)
        sends[step] = [
            pltpu.make_async_copy(
                source.at[pl.ds(rows - WINDOW, WINDOW), cols],
                tail.at[pl.ds(at * WINDOW, WINDOW), pl.ds(place * HEAD_DIM, wide)],
                done.at[2 * (steps + step) + at],
            )
            for at, source in enumerate((k_held, v_held))
        ]
    held[...] = jnp.zeros_like(held)
    for copy in loads:
        copy.start()
    for step in range(steps):
        loads[2 * step].wait()
        loads[2 * step + 1].wait()
        for copy in sends[step]:
            copy.start()
        for head in range(step * wide // HEAD_DIM, (step + 1) * wide // HEAD_DIM):
            cols = slice(head * HEAD_DIM, (head + 1) * HEAD_DIM)
            store_state(held, head, dot_tn(k_held[:, cols], v_held[:, cols]).astype(BF16), False)
    spread(held, outs)
    for step in range(steps):
        for copy in sends[step]:
            copy.wait()


def local_states(keys, values):
    rows, width = keys.shape
    heads = width // HEAD_DIM
    tails = [(2 * WINDOW, count * HEAD_DIM) for _, count in sent_chunks(heads)]
    steps = heads // heads_a_step(heads)
    piece = part_shape(heads)
    results, _ = call(
        lambda *refs: state_body(steps, *refs),
        (1,),
        [HBM] * 2,
        [whole(piece)] * GROUP + [ANY] * len(tails),
        [jax.ShapeDtypeStruct(piece, BF16)] * GROUP + [jax.ShapeDtypeStruct(tail, BF16) for tail in tails],
        [
            pltpu.VMEM((rows, width), BF16),
            pltpu.VMEM((rows, width), BF16),
            pltpu.VMEM((GROUP,) + piece, BF16),
            pltpu.SemaphoreType.DMA((4 * steps,)),
        ],
        2 * rows * width * HEAD_DIM,
        2 * 2 * rows * width,
        [keys, values],
        vmem=VMEM_MOST,
    )
    return results[:GROUP], results[GROUP:]


def total_body(*refs):
    total = refs[0][...].astype(F32)
    for ref in refs[1:-1]:
        total = total + ref[...].astype(F32)
    refs[-1][...] = total.astype(refs[-1].dtype)


def merge_body(reverse, groups, *refs):
    block = lax.axis_index("ctx")
    group = block // GROUP
    place = lax.rem(block, GROUP)
    others = refs[: groups - 1]
    own = refs[groups - 1 : groups - 1 + GROUP]
    outs = refs[groups - 1 + GROUP :]
    total = jnp.zeros(outs[0].shape, F32)
    for step in range(1, groups):
        wanted = group + step < groups if reverse else group - step >= 0
        total = total + others[step - 1][...].astype(F32) * wanted.astype(F32)
    for target in range(GROUP):
        to = lax.bitwise_xor(place, jnp.int32(target))
        result = total
        for source in range(GROUP):
            if source == target:
                continue
            of = lax.bitwise_xor(place, jnp.int32(source))
            wanted = of > to if reverse else of < to
            result = result + own[source][...].astype(F32) * wanted.astype(F32)
        outs[target][...] = result.astype(outs[target].dtype)


def swap(value, mask):
    count = lax.axis_size("ctx")
    return lax.ppermute(value, "ctx", [(at, at ^ mask) for at in range(count)])


def turn(value, steps):
    count = lax.axis_size("ctx")
    return lax.ppermute(value, "ctx", [(at, (at + steps) % count) for at in range(count)])


def shift(value, steps, places):
    count = lax.axis_size("ctx")
    return lax.ppermute(
        value, "ctx", [(at, at + steps) for at in range(count) if at % GROUP in places and 0 <= at + steps < count]
    )


def scan(pieces, reverse, first, second):
    groups = lax.axis_size("ctx") // GROUP
    shape = pieces[0].shape
    full = whole(shape)
    size = shape[0] * shape[1]
    out = jax.ShapeDtypeStruct(shape, BF16)
    own = [pieces[0]] + [swap(pieces[other], other) for other in range(1, GROUP)]
    along, after = first()
    (total,), held = call(
        total_body, (1,), [full] * GROUP, [full], [out], [], GROUP * size, 2 * 5 * size, own, None, along, after
    )
    holders = range(GROUP - HOLDERS, GROUP) if reverse else range(HOLDERS)
    others = [shift(total, (-GROUP if reverse else GROUP) * at, holders) for at in range(1, groups)]
    operands = others + own
    along, after = second(total, held)
    merged, held = call(
        lambda *refs: merge_body(reverse, groups, *refs),
        (1,),
        [full] * len(operands),
        [full] * GROUP,
        [out] * GROUP,
        [],
        20 * size,
        2 * 11 * size,
        operands,
        None,
        along,
        after,
    )
    return [merged[0]] + [swap(merged[other], other) for other in range(1, GROUP)], merged, held


def attend(scores, masks, coef, linear):
    shown = [jnp.where(mask, score, MASKED) for score, mask in zip(scores, masks)]
    peak = jnp.max(shown[0], 0, keepdims=True)
    for tile in shown[1:]:
        peak = jnp.maximum(peak, jnp.max(tile, 0, keepdims=True))
    powers = [jnp.exp2((tile - peak) * SCALE_LOG2) for tile in shown]
    norm = jnp.sum(powers[0], 0, keepdims=True)
    for tile in powers[1:]:
        norm = norm + jnp.sum(tile, 0, keepdims=True)
    share = 1.0 / norm
    probs = [tile * share for tile in powers]
    sums = []
    for prob, score, mask, kind in zip(probs, scores, masks, linear):
        if kind == "none":
            sums.append(None)
        elif kind == "all":
            sums.append((prob + score * coef).astype(BF16))
        else:
            sums.append((prob + jnp.where(mask, score * coef, 0.0)).astype(BF16))
    lse = peak * SCALE + jnp.log(norm)
    return [prob.astype(BF16) for prob in probs], sums, lse


def late_body(first, count, q_ref, k_ref, v_ref, prob_ref, sum_ref, part_ref):
    rows = k_ref.shape[0]
    start = lax.axis_index("ctx") * rows
    keys_at, queries_at = tile_iotas()
    coef = coef_row(start + WINDOW, WINDOW)
    masks = [keys_at > queries_at, keys_at <= queries_at]
    for at in range(count):
        cols = columns_of(first + at)
        query = q_ref[WINDOW : 2 * WINDOW, cols]
        scores = [dot_nt(k_ref[tile * WINDOW : (tile + 1) * WINDOW, cols], query) for tile in range(2)]
        probs, sums, _ = attend(scores, masks, coef, ["all", "masked"])
        total = jnp.zeros((HEAD_DIM, WINDOW), F32)
        for tile in range(2):
            prob_ref[at, tile] = probs[tile]
            sum_ref[at, tile] = sums[tile]
            total = total + dot_tn(v_ref[tile * WINDOW : (tile + 1) * WINDOW, cols], sums[tile])
        part_ref[:, columns_of(at)] = total.T


def late_rows(first, count, queries, keys, values, after):
    tiles = (count, 2, WINDOW, WINDOW)
    wide = count * HEAD_DIM
    return run_once(
        lambda *refs: late_body(first, count, *refs),
        [queries, keys, values],
        [(tiles, BF16), (tiles, BF16), ((WINDOW, wide), F32)],
        [],
        4 * 2 * WINDOW * WINDOW * wide * 4,
        24 * WINDOW * wide,
        after=after,
    )[0]


def early_body(first, count, q_ref, k_ref, v_ref, tail_ref, *rest):
    prob_ref, sum_ref, inside_ref, window_ref, lse_ref = rest[-5:]
    rows = k_ref.shape[0]
    block = lax.axis_index("ctx")
    lse_ref[...] = rest[0][...] if len(rest) > 5 else jnp.zeros_like(lse_ref)
    keys_at, queries_at = tile_iotas()
    beyond = jnp.where(block > 0, 0, 2 * WINDOW)
    masks = [keys_at > queries_at + beyond, keys_at <= queries_at]
    coef = coef_row(block * rows, WINDOW)
    for at in range(count):
        cols, own = columns_of(first + at), columns_of(at)
        query = q_ref[:WINDOW, cols]
        scores = [dot_nt(tail_ref[:WINDOW, own], query), dot_nt(k_ref[:WINDOW, cols], query)]
        probs, sums, lse = attend(scores, masks, coef, ["none", "masked"])
        prob_ref[at, 0] = probs[0]
        prob_ref[at, 1] = probs[1]
        sum_ref[at] = sums[1]
        lse_ref[first + at : first + at + 1, :] = lse
        value = v_ref[:WINDOW, cols]
        before = dot_tn(tail_ref[WINDOW:, own], probs[0])
        window_ref[:, own] = (before + dot_tn(value, probs[1])).T
        inside_ref[:, own] = (before + dot_tn(value, sums[1])).T


def early_rows(first, count, queries, keys, values, before, done, after):
    wide = count * HEAD_DIM
    return run_once(
        lambda *refs: early_body(first, count, *refs),
        [queries, keys, values, before, *done],
        [
            ((count, 2, WINDOW, WINDOW), BF16),
            ((count, WINDOW, WINDOW), BF16),
            ((WINDOW, wide), F32),
            ((WINDOW, wide), F32),
            ((STATS, WINDOW), F32),
        ],
        [],
        5 * 2 * WINDOW * WINDOW * wide * 4,
        24 * WINDOW * wide,
        after=after,
    )[0]


def sum_body(sent, even, q_ref, gain_ref, cot_ref, *rest):
    ins, rest = rest[:GROUP], rest[GROUP:]
    insides, rest = rest[: len(sent)], rest[len(sent) :]
    parts, rest = rest[: len(even)], rest[len(even) :]
    hidden_ref, norm_ref, held, squares, crossed, columns = rest
    rows, width = q_ref.shape
    collect(ins, held)
    columns[...] = coef_column(lax.axis_index("ctx") * rows, rows)
    for head in range(width // HEAD_DIM):
        cols = columns_of(head)
        inside, at = picked(sent, insides, head)
        part, late = picked(even, parts, head)
        carried = columns[...] * dot_nn(q_ref[:, cols], held_state(held, head, False))
        hidden = jnp.concatenate([inside[:, columns_of(at)], part[:, columns_of(late)]], 0) + carried
        hidden_ref[:, cols] = hidden
        scaled = gain_ref[:, cols].astype(F32) * cot_ref[:, cols].astype(F32)
        if head == 0:
            squares[...] = hidden * hidden
            crossed[...] = hidden * scaled
        else:
            squares[...] += hidden * hidden
            crossed[...] += hidden * scaled
    norm_ref[...] = jnp.zeros_like(norm_ref)
    norm_ref[0:1, :] = jnp.sum(squares[...].T, 0, keepdims=True)
    norm_ref[1:2, :] = jnp.sum(crossed[...].T, 0, keepdims=True)


def add_prefix(queries, insides, parts, gain, cotangent, prefix, along):
    rows, width = queries.shape
    heads = width // HEAD_DIM
    return run_once(
        lambda *refs: sum_body(sent_chunks(heads), even_chunks(heads), *refs),
        [queries, gain, cotangent, *prefix, *insides, *parts],
        [((rows, width), F32), ((STATS, rows), F32)],
        [pltpu.VMEM((GROUP,) + prefix[0].shape, BF16)] + [pltpu.VMEM((rows, HEAD_DIM), F32)] * 3,
        2 * rows * width * HEAD_DIM,
        12 * rows * width,
        along,
    )


def stat_rows(width):
    return 2 * STATS * -(-3 * WINDOW // width)


def stat_place(width, part):
    across = width // WINDOW
    return (
        slice(WINDOW + part // across * 2 * STATS, WINDOW + (part // across + 1) * 2 * STATS),
        slice(part % across * WINDOW, (part % across + 1) * WINDOW),
    )


def norm_body(sent, features, norm_ref, hidden_ref, gain_ref, cot_ref, q_ref, lse_ref, *rest):
    windows, rest = rest[: len(sent)], rest[len(sent) :]
    out_ref, grad_ref, first_ref = rest[:3]
    outs = rest[3 : 3 + GROUP]
    held, recip, pull, columns, stats, out_held, done = rest[3 + GROUP :]
    rows, width = q_ref.shape
    root = 1.0 / jnp.sqrt(norm_ref[0:1, :] / features + EPSILON)
    slope = root * root * root * norm_ref[1:2, :] / features
    recip[...] = jnp.broadcast_to(root, (HEAD_DIM, rows)).T
    pull[...] = jnp.broadcast_to(slope, (HEAD_DIM, rows)).T
    columns[...] = coef_column(lax.axis_index("ctx") * rows, rows)
    stats[...] = jnp.zeros_like(stats)
    stats[:STATS, :] = lse_ref[...]
    held[...] = jnp.zeros_like(held)
    copies = []
    for head in range(width // HEAD_DIM):
        cols = columns_of(head)
        hidden = hidden_ref[:, cols]
        gain = gain_ref[:, cols].astype(F32)
        kept = recip[...]
        out_held[:, cols] = (hidden * kept * gain).astype(BF16)
        push(out_held, out_ref, done, head, copies)
        full = kept * (gain * cot_ref[:, cols].astype(F32)) - hidden * pull[...]
        grad = full.astype(BF16)
        grad_ref[:, cols] = grad
        first_ref[:WINDOW, cols] = grad[:WINDOW]
        window, at = picked(sent, windows, head)
        delta = (grad[:WINDOW].astype(F32) * window[:, columns_of(at)]).T
        stats[STATS + head : STATS + head + 1, :] = jnp.sum(delta, 0, keepdims=True)
        state = dot_tn(q_ref[:, cols], (full * columns[...]).astype(BF16)).astype(BF16)
        store_state(held, head, state, True)
    spread(held, outs)
    left = stats[...]
    below = WINDOW + stat_rows(width)
    first_ref[WINDOW:below, :] = jnp.zeros((below - WINDOW, width), BF16)
    first_ref[below:, :] = q_ref[AHEAD:WINDOW, :]
    for part in range(3):
        at_rows, at_cols = stat_place(width, part)
        taken = left.astype(BF16)
        first_ref[at_rows, at_cols] = taken
        left = left - taken.astype(F32)
    for copy in copies:
        copy.wait()


def normalize(norms, hidden, gain, cotangent, queries, windows, lse, features):
    rows, width = queries.shape
    heads = width // HEAD_DIM
    piece = part_shape(heads)
    return run_once(
        lambda *refs: norm_body(sent_chunks(heads), features, *refs),
        [norms, hidden, gain, cotangent, queries, lse, *windows],
        [((rows, width), BF16), ((rows, width), BF16), ((2 * WINDOW - AHEAD + stat_rows(width), width), BF16)] + [(piece, BF16)] * GROUP,
        [pltpu.VMEM((GROUP,) + piece, BF16)]
        + [pltpu.VMEM((rows, HEAD_DIM), F32)] * 3
        + [
            pltpu.VMEM((2 * STATS, WINDOW), F32),
            pltpu.VMEM((rows, width), BF16),
            pltpu.SemaphoreType.DMA((heads // heads_a_step(heads),)),
        ],
        2 * rows * width * HEAD_DIM,
        14 * rows * width,
        pushed=(0,),
    )[0]


def back_body(first, count, sent, even, q_ref, k_ref, v_ref, g_ref, *rest):
    heads = q_ref.shape[1] // HEAD_DIM
    rows = q_ref.shape[0]
    last = first + count == heads
    ins, rest = rest[:GROUP], rest[GROUP:]
    tails, rest = rest[: len(sent)], rest[len(sent) :]
    probs0, rest = rest[: len(sent)], rest[len(sent) :]
    sums0, rest = rest[: len(sent)], rest[len(sent) :]
    probs1, sums1 = rest[0], rest[1]
    made = rest[2:-3] if not last else rest[2:-5]
    if last:
        dk_ref, dv_ref, held, dq_held, done = rest[-5:]
        dq_ref, made = made[-1], made[:-1]
    else:
        dq_held, dk_ref, dv_ref, held = made[-1], *rest[-3:]
        dq_ref, made = None, made[:-1]
    collect(ins, held)
    keys_at, queries_at = tile_iotas()
    causal = keys_at <= queries_at
    start = lax.axis_index("ctx") * rows
    ratios = coef_row(start, rows) * (1.0 / SCALE)
    early, late = slice(0, WINDOW), slice(WINDOW, 2 * WINDOW)
    copies = []
    if last and made:
        dq_held[:, : first * HEAD_DIM] = made[0][...]
        for head in range(first):
            push(dq_held, dq_ref, done, head, copies)
    for at in range(count):
        head = first + at
        cols, own = columns_of(head), columns_of(at)
        before_ref, place = picked(sent, tails, head)
        prob0 = picked(sent, probs0, head)[0]
        sum0 = picked(sent, sums0, head)[0]
        grads = g_ref[early, cols], g_ref[late, cols]
        queries = q_ref[early, cols], q_ref[late, cols]
        keys = before_ref[:WINDOW, columns_of(place)], k_ref[early, cols], k_ref[late, cols]
        values = before_ref[WINDOW:, columns_of(place)], v_ref[early, cols], v_ref[late, cols]
        probs = (
            (prob0[place, 0].astype(F32), prob0[place, 1].astype(F32)),
            (probs1[at, 0].astype(F32), probs1[at, 1].astype(F32)),
        )
        edges = []
        for half in range(2):
            ratio = ratios[:, half * WINDOW : (half + 1) * WINDOW]
            pulls = [dot_nt(values[half + tile], grads[half]) for tile in range(2)]
            delta = jnp.sum(probs[half][0] * pulls[0] + probs[half][1] * pulls[1], 0, keepdims=True)
            before = probs[half][0] * (pulls[0] - delta)
            if half == 1:
                before = before + pulls[0] * ratio
            here = probs[half][1] * (pulls[1] - delta) + jnp.where(causal, pulls[1] * ratio, 0.0)
            edges.append((before.astype(BF16), here.astype(BF16)))
        state = held_state(held, head, False)
        for half, part in enumerate((early, late)):
            inner = dot_tn(keys[half], edges[half][0]) + dot_tn(keys[half + 1], edges[half][1])
            carried = (coef_row(start + half * WINDOW, WINDOW) * (1.0 / SCALE)) * dot_nt(state, grads[half])
            dq_held[part, cols if last else own] = ((inner + carried).T * SCALE).astype(BF16)
        if last:
            push(dq_held, dq_ref, done, head, copies)
        dk_ref[early, own] = SCALE * (dot_nn(edges[0][1], queries[0]) + dot_nn(edges[1][0], queries[1]))
        dk_ref[late, own] = SCALE * dot_nn(edges[1][1], queries[1])
        dv_ref[early, own] = dot_nn(sum0[place], grads[0]) + dot_nn(sums1[at, 0], grads[1])
        dv_ref[late, own] = dot_nn(sums1[at, 1], grads[1])
    for copy in copies:
        copy.wait()


def backward(first, count, queries, keys, values, grads, before, probs0, sums0, probs1, sums1, prefix, made, after):
    rows, width = keys.shape
    heads = width // HEAD_DIM
    last = first + count == heads
    wide = count * HEAD_DIM
    scratch = [pltpu.VMEM((GROUP,) + prefix[0].shape, BF16)]
    if last:
        scratch += [pltpu.VMEM((rows, width), BF16), pltpu.SemaphoreType.DMA((heads // heads_a_step(heads),))]
    return run_once(
        lambda *refs: back_body(first, count, sent_chunks(heads), even_chunks(heads), *refs),
        [queries, keys, values, grads, *prefix, *before, *probs0, *sums0, probs1, sums1, *made],
        [((rows, width if last else wide), BF16), ((rows, wide), F32), ((rows, wide), F32)],
        scratch,
        16 * 2 * WINDOW * WINDOW * wide * 2,
        40 * WINDOW * wide * 2,
        after=after,
        pushed=(0,) if last else (),
    )[0]


def edge_body(last, k_ref, v_ref, qn_ref, sent_ref, dk_ref, dv_ref):
    width = k_ref.shape[1]
    stats = jnp.zeros((2 * STATS, WINDOW), F32)
    for part in range(3):
        at_rows, at_cols = stat_place(width, 2 - part)
        stats = stats + sent_ref[at_rows, at_cols].astype(F32)
    keys_at, queries_at = tile_iotas()
    beyond = jnp.where(lax.axis_index("ctx") < last, 0, 2 * WINDOW)
    mask = keys_at > queries_at + beyond
    late = slice(WINDOW, 2 * WINDOW)
    for head in range(width // HEAD_DIM):
        cols = columns_of(head)
        query = jnp.concatenate([qn_ref[:, cols], sent_ref[WINDOW + stat_rows(width) :, cols]], 0)
        grad = sent_ref[:WINDOW, cols]
        lse = stats[head : head + 1, :] * (1.0 / LN2)
        delta = stats[STATS + head : STATS + head + 1, :]
        scores = dot_nt(k_ref[late, cols], query) * SCALE_LOG2
        probs = jnp.where(mask, jnp.exp2(scores - lse), 0.0)
        edges = probs * (dot_nt(v_ref[late, cols], grad) - delta)
        dk_ref[:, cols] = SCALE * dot_nn(edges.astype(BF16), query)
        dv_ref[:, cols] = dot_nn(probs.astype(BF16), grad)


def edge(keys, values, queries_after, grads_after, after):
    width = keys.shape[1]
    last = lax.axis_size("ctx") - 1
    return run_once(
        lambda *refs: edge_body(last, *refs),
        [keys, values, queries_after, grads_after],
        [((WINDOW, width), F32)] * 2,
        [],
        4 * 2 * WINDOW * WINDOW * width,
        12 * WINDOW * width,
        after=after,
    )[0]


def last_body(even, k_ref, v_ref, ek_ref, ev_ref, *rest):
    ins, rest = rest[:GROUP], rest[GROUP:]
    dk_in, dv_in = rest[: len(even)], rest[len(even) : 2 * len(even)]
    dk_ref, dv_ref, held, dk_held, dv_held, dk_done, dv_done = rest[2 * len(even) :]
    early, late = slice(0, WINDOW), slice(WINDOW, 2 * WINDOW)
    collect(ins, held)
    copies = []
    for head in range(k_ref.shape[1] // HEAD_DIM):
        cols = columns_of(head)
        dk_ref_in, at = picked(even, dk_in, head)
        dv_ref_in = picked(even, dv_in, head)[0]
        state = held_state(held, head, True)
        keys = dk_ref_in[:, columns_of(at)] + dot_nt(v_ref[:, cols], state)
        dk_held[early, cols] = keys[early].astype(BF16)
        dk_held[late, cols] = (keys[late] + ek_ref[:, cols]).astype(BF16)
        push(dk_held, dk_ref, dk_done, head, copies)
        values = dv_ref_in[:, columns_of(at)] + dot_nn(k_ref[:, cols], state)
        dv_held[early, cols] = values[early].astype(BF16)
        dv_held[late, cols] = (values[late] + ev_ref[:, cols]).astype(BF16)
        push(dv_held, dv_ref, dv_done, head, copies)
    for copy in copies:
        copy.wait()


def finish(keys, values, dk_parts, dv_parts, edges, suffix):
    rows, width = keys.shape
    heads = width // HEAD_DIM
    done = pltpu.SemaphoreType.DMA((heads // heads_a_step(heads),))
    return run_once(
        lambda *refs: last_body(even_chunks(heads), *refs),
        [keys, values, *edges, *suffix, *dk_parts, *dv_parts],
        [((rows, width), BF16)] * 2,
        [pltpu.VMEM((GROUP,) + suffix[0].shape, BF16)] + [pltpu.VMEM((rows, width), BF16)] * 2 + [done, done],
        4 * rows * width * HEAD_DIM,
        18 * rows * width,
        pushed=(0, 1),
    )[0]


def summed(value, axis):
    count = lax.axis_size(axis)
    mask = 1
    while mask < count:
        value = value + lax.ppermute(value, axis, [(at, at ^ mask) for at in range(count)])
        mask *= 2
    return value


def on_device(queries, keys, values, gain, cotangent):
    rows, width = queries.shape
    heads = width // HEAD_DIM
    features = width * lax.axis_size("head")
    sent, even = sent_chunks(heads), even_chunks(heads)
    gain = gain.reshape(1, width)
    late, own, grads_after = [], [], []

    pieces, tails = local_states(keys, values)
    before = [turn(tails[0], 1)]

    def first_round():
        late.append(late_rows(*even[0], queries, keys, values, pieces[:1]))
        return tails[1:], [before[0], late[0][2]]

    def second_round(total, held):
        before.extend(turn(tail, 1) for tail in held)
        late.extend(late_rows(*chunk, queries, keys, values, [total]) for chunk in even[1:])
        return [], [late[-1][2]]

    prefix, merged, _ = scan(pieces, False, first_round, second_round)
    early = []
    for chunk, tail in zip(sent, before):
        done = [early[-1][4]] if early else []
        early.append(early_rows(*chunk, queries, keys, values, tail, done, merged[:1]))
    probs0, sums0, insides, windows, lses = zip(*early)
    probs1, sums1, parts = zip(*late)
    (hidden, norms), handed = add_prefix(queries, insides, parts, gain, cotangent, prefix, [queries[:AHEAD]])
    after = turn(handed[0], -1)
    norms = summed(norms, "head")
    output, grads, first, *states = normalize(norms, hidden, gain, cotangent, queries, windows, lses[-1], features)

    def own_chunk(at, after):
        made = [own[0][0]] if own else []
        own.append(
            backward(
                *even[at], queries, keys, values, grads, before, probs0, sums0, probs1[at], sums1[at], prefix, made, after
            )
        )

    def first_back():
        own_chunk(0, [])
        return [first], [after, own[0][1]]

    def second_back(total, held):
        grads_after.append(turn(held[0], -1))
        for at in range(1, len(even)):
            own_chunk(at, [total])
        return [], [own[-1][1]]

    suffix, merged, _ = scan(states, True, first_back, second_back)
    edges = edge(keys, values, after, grads_after[0], merged[:1])
    grad_queries, dk_parts, dv_parts = zip(*own)
    grad_keys, grad_values = finish(keys, values, dk_parts, dv_parts, edges, suffix)
    return output, grad_queries[-1], grad_keys, grad_values


def solution(mesh):
    wide = P("ctx", "head")
    return jax.shard_map(
        on_device,
        mesh=mesh,
        in_specs=(wide, wide, wide, P("head"), wide),
        out_specs=(wide, wide, wide, wide),
        check_vma=False,
    )
```

```python
import math

import jax
import jax.numpy as jnp
from jax import lax
from jax.experimental import pallas as pl
from jax.experimental.pallas import tpu as pltpu
from jax.sharding import PartitionSpec as P

HEAD_DIM = 128
WINDOW = 256
GROUP = 4
HOLDERS = 3
STATS = 8
AHEAD = 192
EPSILON = 1e-06
SCALE = 1.0 / math.sqrt(HEAD_DIM)
SCALE_LOG2 = SCALE * math.log2(math.e)
LN2 = math.log(2.0)
MASKED = -1e30
BF16 = jnp.bfloat16
F32 = jnp.float32
VMEM_LIMIT = 24 * 1024 * 1024
VMEM_MOST = 60 * 1024 * 1024


def dot_nn(left, right):
    return lax.dot_general(left, right, (((1,), (0,)), ((), ())), preferred_element_type=F32)


def dot_nt(left, right):
    return lax.dot_general(left, right, (((1,), (1,)), ((), ())), preferred_element_type=F32)


def dot_tn(left, right):
    return lax.dot_general(left, right, (((0,), (0,)), ((), ())), preferred_element_type=F32)


def tile_iotas():
    keys_at = lax.broadcasted_iota(jnp.int32, (WINDOW, WINDOW), 0)
    queries_at = lax.broadcasted_iota(jnp.int32, (WINDOW, WINDOW), 1)
    return keys_at, queries_at


def coef_row(start, count):
    at = start + lax.broadcasted_iota(jnp.int32, (1, count), 1)
    return 1.0 / jnp.sqrt(HEAD_DIM * (at + 1).astype(F32))


def coef_column(start, count):
    at = start + lax.broadcasted_iota(jnp.int32, (count, HEAD_DIM), 0)
    return 1.0 / jnp.sqrt(HEAD_DIM * (at + 1).astype(F32))


def heads_a_step(heads):
    return 2 if heads % 2 == 0 else 1


def sent_chunks(heads):
    return [(0, heads - 2), (heads - 2, 2)] if heads > 4 else [(0, heads)]


def tails_apart(tails):
    return [tuple(tails[:2])] + [(tail, tail) for tail in tails[2:]]


def tail_columns(tail, place):
    keys, values = tail
    below = WINDOW if keys is values else 0
    return keys[:WINDOW, columns_of(place)], values[below : below + WINDOW, columns_of(place)]


def even_chunks(heads):
    return [(0, heads // 2), (heads // 2, heads - heads // 2)] if heads > 1 else [(0, 1)]


def picked(chunks, refs, head):
    for (first, count), ref in zip(chunks, refs):
        if first <= head < first + count:
            return ref, head - first
    raise ValueError


def columns_of(head):
    return slice(head * HEAD_DIM, (head + 1) * HEAD_DIM)


def call(body, grid, in_specs, out_specs, out_shape, scratch, flops, moved, operands, aliases=None, along=(), after=(), vmem=VMEM_LIMIT):
    inputs, results, handed, skipped = len(operands), len(out_shape), len(along), len(after)

    def run(*refs):
        outs = inputs + handed + skipped
        body(*refs[:inputs], *refs[outs : outs + results], *refs[outs + results + handed :])

    given = pl.pallas_call(
        run,
        grid=grid,
        input_output_aliases={**(aliases or {}), **{inputs + at: results + at for at in range(handed)}},
        in_specs=list(in_specs) + [ANY] * (handed + skipped),
        out_specs=list(out_specs) + [ANY] * handed,
        out_shape=list(out_shape) + [jax.ShapeDtypeStruct(array.shape, array.dtype) for array in along],
        scratch_shapes=scratch,
        compiler_params=pltpu.CompilerParams(
            vmem_limit_bytes=vmem,
            dimension_semantics=("arbitrary",) * len(grid),
        ),
        cost_estimate=pl.CostEstimate(flops=flops, bytes_accessed=moved, transcendentals=0),
    )(*operands, *along, *after)
    return list(given[:results]), list(given[results:])


def run_once(body, operands, results, scratch, flops, moved, along=(), after=(), pushed=()):
    return call(
        body,
        (1,),
        [whole(array.shape) for array in operands],
        [HBM if at in pushed else whole(shape) for at, (shape, _) in enumerate(results)],
        [jax.ShapeDtypeStruct(shape, kind) for shape, kind in results],
        scratch,
        flops,
        moved,
        operands,
        None,
        along,
        after,
    )


def push(held, out, done, head, copies):
    step = heads_a_step(held.shape[1] // HEAD_DIM)
    if head % step == step - 1:
        cols = pl.ds((head + 1 - step) * HEAD_DIM, step * HEAD_DIM)
        copy = pltpu.make_async_copy(held.at[:, cols], out.at[:, cols], done.at[head // step])
        copy.start()
        copies.append(copy)


ANY = pl.BlockSpec(memory_space=pl.ANY)
HBM = pl.BlockSpec(memory_space=pltpu.HBM)


def whole(shape):
    return pl.BlockSpec(shape, lambda *_: (0,) * len(shape))


def heads_a_part(heads):
    return -(-heads // HOLDERS)


def part_shape(heads):
    return (heads_a_part(heads) * HEAD_DIM, HEAD_DIM)


def part_at(held, head, reverse):
    each = held.shape[1] // HEAD_DIM
    at = lax.rem(head, each) * HEAD_DIM
    if not isinstance(at, int):
        at = pl.multiple_of(at, HEAD_DIM)
    return head // each + (GROUP - HOLDERS if reverse else 0), pl.ds(at, HEAD_DIM)


def store_state(held, head, state, reverse):
    slot, rows = part_at(held, head, reverse)
    held[slot, rows, :] = state


def held_state(held, head, reverse):
    slot, rows = part_at(held, head, reverse)
    return held[slot, rows, :]


def spread(held, outs):
    place = lax.rem(lax.axis_index("ctx"), GROUP)
    for other in range(GROUP):
        outs[other][...] = held[lax.bitwise_xor(place, jnp.int32(other))]


def collect(ins, held):
    place = lax.rem(lax.axis_index("ctx"), GROUP)
    for other in range(GROUP):
        held[lax.bitwise_xor(place, jnp.int32(other))] = ins[other][...]


def state_body(k_ref, v_ref, *rest):
    outs, tails = rest[:GROUP], rest[GROUP:-4]
    k_held, v_held, held, done = rest[-4:]
    rows, width = k_held.shape
    held[...] = jnp.zeros_like(held)
    loads = []
    for first in (rows - WINDOW, 0):
        part = pl.ds(first, rows - WINDOW if first == 0 else WINDOW)
        for source, target in ((k_ref, k_held), (v_ref, v_held)):
            loads.append(pltpu.make_async_copy(source.at[part, :], target.at[part, :], done.at[len(loads)]))
            loads[-1].start()
    for copy in loads[:2]:
        copy.wait()
    sends = []
    for (first, count), tail in zip(sent_chunks(width // HEAD_DIM), tails):
        for at, source in enumerate((v_held,) if first == 0 else (k_held, v_held)):
            sends.append(
                pltpu.make_async_copy(
                    source.at[pl.ds(rows - WINDOW, WINDOW), pl.ds(first * HEAD_DIM, count * HEAD_DIM)],
                    tail.at[pl.ds(at * WINDOW, WINDOW), :],
                    done.at[4 + len(sends)],
                )
            )
            sends[-1].start()
    for copy in loads[2:]:
        copy.wait()
    for head in range(width // HEAD_DIM):
        cols = columns_of(head)
        store_state(held, head, dot_tn(k_held[:, cols], v_held[:, cols]).astype(BF16), False)
    spread(held, outs)
    for copy in sends:
        copy.wait()


def local_states(keys, values):
    rows, width = keys.shape
    heads = width // HEAD_DIM
    tails = [(2 * WINDOW if first else WINDOW, count * HEAD_DIM) for first, count in sent_chunks(heads)]
    piece = part_shape(heads)
    results, _ = call(
        state_body,
        (1,),
        [HBM] * 2,
        [whole(piece)] * GROUP + [ANY] * len(tails),
        [jax.ShapeDtypeStruct(piece, BF16)] * GROUP + [jax.ShapeDtypeStruct(tail, BF16) for tail in tails],
        [
            pltpu.VMEM((rows, width), BF16),
            pltpu.VMEM((rows, width), BF16),
            pltpu.VMEM((GROUP,) + piece, BF16),
            pltpu.SemaphoreType.DMA((4 + 2 * len(tails),)),
        ],
        2 * rows * width * HEAD_DIM,
        2 * 2 * rows * width,
        [keys, values],
        vmem=VMEM_MOST,
    )
    return results[:GROUP], results[GROUP:]


def total_body(*refs):
    total = refs[0][...].astype(F32)
    for ref in refs[1:-1]:
        total = total + ref[...].astype(F32)
    refs[-1][...] = total.astype(refs[-1].dtype)


def merge_body(reverse, groups, *refs):
    block = lax.axis_index("ctx")
    group = block // GROUP
    place = lax.rem(block, GROUP)
    others = refs[: groups - 1]
    own = refs[groups - 1 : groups - 1 + GROUP]
    outs = refs[groups - 1 + GROUP :]
    total = jnp.zeros(outs[0].shape, F32)
    for step in range(1, groups):
        wanted = group + step < groups if reverse else group - step >= 0
        total = total + others[step - 1][...].astype(F32) * wanted.astype(F32)
    for target in range(GROUP):
        to = lax.bitwise_xor(place, jnp.int32(target))
        result = total
        for source in range(GROUP):
            if source == target:
                continue
            of = lax.bitwise_xor(place, jnp.int32(source))
            wanted = of > to if reverse else of < to
            result = result + own[source][...].astype(F32) * wanted.astype(F32)
        outs[target][...] = result.astype(outs[target].dtype)


def swap(value, mask):
    count = lax.axis_size("ctx")
    return lax.ppermute(value, "ctx", [(at, at ^ mask) for at in range(count)])


def turn(value, steps):
    count = lax.axis_size("ctx")
    return lax.ppermute(value, "ctx", [(at, (at + steps) % count) for at in range(count)])


def shift(value, steps, places):
    count = lax.axis_size("ctx")
    return lax.ppermute(
        value, "ctx", [(at, at + steps) for at in range(count) if at % GROUP in places and 0 <= at + steps < count]
    )


def onward(value, steps):
    return shift(value, steps, range(GROUP))


def scan(pieces, reverse, first, second):
    groups = lax.axis_size("ctx") // GROUP
    shape = pieces[0].shape
    full = whole(shape)
    size = shape[0] * shape[1]
    out = jax.ShapeDtypeStruct(shape, BF16)
    own = [pieces[0]] + [swap(pieces[other], other) for other in range(1, GROUP)]
    along, after = first()
    (total,), held = call(
        total_body, (1,), [full] * GROUP, [full], [out], [], GROUP * size, 2 * 5 * size, own, None, along, after
    )
    holders = range(GROUP - HOLDERS, GROUP) if reverse else range(HOLDERS)
    others = [shift(total, (-GROUP if reverse else GROUP) * at, holders) for at in range(1, groups)]
    operands = others + own
    along, after = second(total, held)
    merged, held = call(
        lambda *refs: merge_body(reverse, groups, *refs),
        (1,),
        [full] * len(operands),
        [full] * GROUP,
        [out] * GROUP,
        [],
        20 * size,
        2 * 11 * size,
        operands,
        None,
        along,
        after,
    )
    return [merged[0]] + [swap(merged[other], other) for other in range(1, GROUP)], merged, held


def attend(scores, masks, coef, linear):
    shown = [jnp.where(mask, score, MASKED) for score, mask in zip(scores, masks)]
    peak = jnp.max(shown[0], 0, keepdims=True)
    for tile in shown[1:]:
        peak = jnp.maximum(peak, jnp.max(tile, 0, keepdims=True))
    powers = [jnp.exp2((tile - peak) * SCALE_LOG2) for tile in shown]
    norm = jnp.sum(powers[0], 0, keepdims=True)
    for tile in powers[1:]:
        norm = norm + jnp.sum(tile, 0, keepdims=True)
    share = 1.0 / norm
    probs = [tile * share for tile in powers]
    sums = []
    for prob, score, mask, kind in zip(probs, scores, masks, linear):
        if kind == "none":
            sums.append(None)
        elif kind == "all":
            sums.append((prob + score * coef).astype(BF16))
        else:
            sums.append((prob + jnp.where(mask, score * coef, 0.0)).astype(BF16))
    lse = peak * SCALE + jnp.log(norm)
    return [prob.astype(BF16) for prob in probs], sums, lse


def late_body(first, count, q_ref, k_ref, v_ref, prob_ref, sum_ref, part_ref):
    rows = k_ref.shape[0]
    start = lax.axis_index("ctx") * rows
    keys_at, queries_at = tile_iotas()
    coef = coef_row(start + WINDOW, WINDOW)
    masks = [keys_at > queries_at, keys_at <= queries_at]
    for at in range(count):
        cols = columns_of(first + at)
        query = q_ref[WINDOW : 2 * WINDOW, cols]
        scores = [dot_nt(k_ref[tile * WINDOW : (tile + 1) * WINDOW, cols], query) for tile in range(2)]
        probs, sums, _ = attend(scores, masks, coef, ["all", "masked"])
        total = jnp.zeros((HEAD_DIM, WINDOW), F32)
        for tile in range(2):
            prob_ref[at, tile] = probs[tile]
            sum_ref[at, tile] = sums[tile]
            total = total + dot_tn(v_ref[tile * WINDOW : (tile + 1) * WINDOW, cols], sums[tile])
        part_ref[:, columns_of(at)] = total.T


def late_rows(first, count, queries, keys, values, after):
    tiles = (count, 2, WINDOW, WINDOW)
    wide = count * HEAD_DIM
    return run_once(
        lambda *refs: late_body(first, count, *refs),
        [queries, keys, values],
        [(tiles, BF16), (tiles, BF16), ((WINDOW, wide), F32)],
        [],
        4 * 2 * WINDOW * WINDOW * wide * 4,
        24 * WINDOW * wide,
        after=after,
    )[0]


def early_body(first, count, sent, q_ref, k_ref, v_ref, *rest):
    tail, rest = (rest[0], rest[sent - 1]), rest[sent:]
    prob_ref, sum_ref, inside_ref, window_ref, lse_ref = rest[-5:]
    rows = k_ref.shape[0]
    block = lax.axis_index("ctx")
    lse_ref[...] = rest[0][...] if len(rest) > 5 else jnp.zeros_like(lse_ref)
    keys_at, queries_at = tile_iotas()
    beyond = jnp.where(block > 0, 0, 2 * WINDOW)
    masks = [keys_at > queries_at + beyond, keys_at <= queries_at]
    coef = coef_row(block * rows, WINDOW)
    for at in range(count):
        cols, own = columns_of(first + at), columns_of(at)
        query = q_ref[:WINDOW, cols]
        key_before, value_before = tail_columns(tail, at)
        scores = [dot_nt(key_before, query), dot_nt(k_ref[:WINDOW, cols], query)]
        probs, sums, lse = attend(scores, masks, coef, ["none", "masked"])
        prob_ref[at, 0] = probs[0]
        prob_ref[at, 1] = probs[1]
        sum_ref[at] = sums[1]
        lse_ref[first + at : first + at + 1, :] = lse
        value = v_ref[:WINDOW, cols]
        before = dot_tn(value_before, probs[0])
        window_ref[:, own] = (before + dot_tn(value, probs[1])).T
        inside_ref[:, own] = (before + dot_tn(value, sums[1])).T


def early_rows(first, count, queries, keys, values, before, done, after):
    wide = count * HEAD_DIM
    return run_once(
        lambda *refs: early_body(first, count, len(before), *refs),
        [queries, keys, values, *before, *done],
        [
            ((count, 2, WINDOW, WINDOW), BF16),
            ((count, WINDOW, WINDOW), BF16),
            ((WINDOW, wide), F32),
            ((WINDOW, wide), F32),
            ((STATS, WINDOW), F32),
        ],
        [],
        5 * 2 * WINDOW * WINDOW * wide * 4,
        24 * WINDOW * wide,
        after=after,
    )[0]


def sum_body(sent, even, q_ref, gain_ref, cot_ref, *rest):
    ins, rest = rest[:GROUP], rest[GROUP:]
    insides, rest = rest[: len(sent)], rest[len(sent) :]
    parts, rest = rest[: len(even)], rest[len(even) :]
    hidden_ref, norm_ref, held, squares, crossed, columns = rest
    rows, width = q_ref.shape
    collect(ins, held)
    columns[...] = coef_column(lax.axis_index("ctx") * rows, rows)
    for head in range(width // HEAD_DIM):
        cols = columns_of(head)
        inside, at = picked(sent, insides, head)
        part, late = picked(even, parts, head)
        carried = columns[...] * dot_nn(q_ref[:, cols], held_state(held, head, False))
        hidden = jnp.concatenate([inside[:, columns_of(at)], part[:, columns_of(late)]], 0) + carried
        hidden_ref[:, cols] = hidden
        scaled = gain_ref[:, cols].astype(F32) * cot_ref[:, cols].astype(F32)
        if head == 0:
            squares[...] = hidden * hidden
            crossed[...] = hidden * scaled
        else:
            squares[...] += hidden * hidden
            crossed[...] += hidden * scaled
    norm_ref[...] = jnp.zeros_like(norm_ref)
    norm_ref[0:1, :] = jnp.sum(squares[...].T, 0, keepdims=True)
    norm_ref[1:2, :] = jnp.sum(crossed[...].T, 0, keepdims=True)


def add_prefix(queries, insides, parts, gain, cotangent, prefix, along):
    rows, width = queries.shape
    heads = width // HEAD_DIM
    return run_once(
        lambda *refs: sum_body(sent_chunks(heads), even_chunks(heads), *refs),
        [queries, gain, cotangent, *prefix, *insides, *parts],
        [((rows, width), F32), ((STATS, rows), F32)],
        [pltpu.VMEM((GROUP,) + prefix[0].shape, BF16)] + [pltpu.VMEM((rows, HEAD_DIM), F32)] * 3,
        2 * rows * width * HEAD_DIM,
        12 * rows * width,
        along,
    )


def stat_rows(width):
    return 2 * STATS * -(-3 * WINDOW // width)


def stat_place(width, part):
    across = width // WINDOW
    return (
        slice(WINDOW + part // across * 2 * STATS, WINDOW + (part // across + 1) * 2 * STATS),
        slice(part % across * WINDOW, (part % across + 1) * WINDOW),
    )


def norm_body(sent, features, norm_ref, hidden_ref, gain_ref, cot_ref, q_ref, lse_ref, *rest):
    windows, rest = rest[: len(sent)], rest[len(sent) :]
    out_ref, grad_ref, first_ref = rest[:3]
    outs = rest[3 : 3 + GROUP]
    held, recip, pull, columns, stats, out_held, done = rest[3 + GROUP :]
    rows, width = q_ref.shape
    root = 1.0 / jnp.sqrt(norm_ref[0:1, :] / features + EPSILON)
    slope = root * root * root * norm_ref[1:2, :] / features
    recip[...] = jnp.broadcast_to(root, (HEAD_DIM, rows)).T
    pull[...] = jnp.broadcast_to(slope, (HEAD_DIM, rows)).T
    columns[...] = coef_column(lax.axis_index("ctx") * rows, rows)
    stats[...] = jnp.zeros_like(stats)
    stats[:STATS, :] = lse_ref[...]
    held[...] = jnp.zeros_like(held)
    copies = []
    for head in range(width // HEAD_DIM):
        cols = columns_of(head)
        hidden = hidden_ref[:, cols]
        gain = gain_ref[:, cols].astype(F32)
        kept = recip[...]
        out_held[:, cols] = (hidden * kept * gain).astype(BF16)
        push(out_held, out_ref, done, head, copies)
        full = kept * (gain * cot_ref[:, cols].astype(F32)) - hidden * pull[...]
        grad = full.astype(BF16)
        grad_ref[:, cols] = grad
        first_ref[:WINDOW, cols] = grad[:WINDOW]
        window, at = picked(sent, windows, head)
        delta = (grad[:WINDOW].astype(F32) * window[:, columns_of(at)]).T
        stats[STATS + head : STATS + head + 1, :] = jnp.sum(delta, 0, keepdims=True)
        state = dot_tn(q_ref[:, cols], (full * columns[...]).astype(BF16)).astype(BF16)
        store_state(held, head, state, True)
    spread(held, outs)
    left = stats[...]
    below = WINDOW + stat_rows(width)
    first_ref[WINDOW:below, :] = jnp.zeros((below - WINDOW, width), BF16)
    first_ref[below:, :] = q_ref[AHEAD:WINDOW, :]
    for part in range(3):
        at_rows, at_cols = stat_place(width, part)
        taken = left.astype(BF16)
        first_ref[at_rows, at_cols] = taken
        left = left - taken.astype(F32)
    for copy in copies:
        copy.wait()


def normalize(norms, hidden, gain, cotangent, queries, windows, lse, features):
    rows, width = queries.shape
    heads = width // HEAD_DIM
    piece = part_shape(heads)
    return run_once(
        lambda *refs: norm_body(sent_chunks(heads), features, *refs),
        [norms, hidden, gain, cotangent, queries, lse, *windows],
        [((rows, width), BF16), ((rows, width), BF16), ((2 * WINDOW - AHEAD + stat_rows(width), width), BF16)] + [(piece, BF16)] * GROUP,
        [pltpu.VMEM((GROUP,) + piece, BF16)]
        + [pltpu.VMEM((rows, HEAD_DIM), F32)] * 3
        + [
            pltpu.VMEM((2 * STATS, WINDOW), F32),
            pltpu.VMEM((rows, width), BF16),
            pltpu.SemaphoreType.DMA((heads // heads_a_step(heads),)),
        ],
        2 * rows * width * HEAD_DIM,
        14 * rows * width,
        pushed=(0,),
    )[0]


def back_body(first, count, sent, even, q_ref, k_ref, v_ref, g_ref, *rest):
    heads = q_ref.shape[1] // HEAD_DIM
    rows = q_ref.shape[0]
    last = first + count == heads
    ins, rest = rest[:GROUP], rest[GROUP:]
    tails, rest = tails_apart(rest[: len(sent) + 1]), rest[len(sent) + 1 :]
    probs0, rest = rest[: len(sent)], rest[len(sent) :]
    sums0, rest = rest[: len(sent)], rest[len(sent) :]
    probs1, sums1 = rest[0], rest[1]
    made = rest[2:-3] if not last else rest[2:-5]
    if last:
        dk_ref, dv_ref, held, dq_held, done = rest[-5:]
        dq_ref, made = made[-1], made[:-1]
    else:
        dq_held, dk_ref, dv_ref, held = made[-1], *rest[-3:]
        dq_ref, made = None, made[:-1]
    collect(ins, held)
    keys_at, queries_at = tile_iotas()
    causal = keys_at <= queries_at
    start = lax.axis_index("ctx") * rows
    ratios = coef_row(start, rows) * (1.0 / SCALE)
    early, late = slice(0, WINDOW), slice(WINDOW, 2 * WINDOW)
    copies = []
    if last and made:
        dq_held[:, : first * HEAD_DIM] = made[0][...]
        for head in range(first):
            push(dq_held, dq_ref, done, head, copies)
    for at in range(count):
        head = first + at
        cols, own = columns_of(head), columns_of(at)
        tail, place = picked(sent, tails, head)
        key_before, value_before = tail_columns(tail, place)
        prob0 = picked(sent, probs0, head)[0]
        sum0 = picked(sent, sums0, head)[0]
        grads = g_ref[early, cols], g_ref[late, cols]
        queries = q_ref[early, cols], q_ref[late, cols]
        keys = key_before, k_ref[early, cols], k_ref[late, cols]
        values = value_before, v_ref[early, cols], v_ref[late, cols]
        probs = (
            (prob0[place, 0].astype(F32), prob0[place, 1].astype(F32)),
            (probs1[at, 0].astype(F32), probs1[at, 1].astype(F32)),
        )
        edges = []
        for half in range(2):
            ratio = ratios[:, half * WINDOW : (half + 1) * WINDOW]
            pulls = [dot_nt(values[half + tile], grads[half]) for tile in range(2)]
            delta = jnp.sum(probs[half][0] * pulls[0] + probs[half][1] * pulls[1], 0, keepdims=True)
            before = probs[half][0] * (pulls[0] - delta)
            if half == 1:
                before = before + pulls[0] * ratio
            here = probs[half][1] * (pulls[1] - delta) + jnp.where(causal, pulls[1] * ratio, 0.0)
            edges.append((before.astype(BF16), here.astype(BF16)))
        state = held_state(held, head, False)
        for half, part in enumerate((early, late)):
            inner = dot_tn(keys[half], edges[half][0]) + dot_tn(keys[half + 1], edges[half][1])
            carried = (coef_row(start + half * WINDOW, WINDOW) * (1.0 / SCALE)) * dot_nt(state, grads[half])
            dq_held[part, cols if last else own] = ((inner + carried).T * SCALE).astype(BF16)
        if last:
            push(dq_held, dq_ref, done, head, copies)
        dk_ref[early, own] = SCALE * (dot_nn(edges[0][1], queries[0]) + dot_nn(edges[1][0], queries[1]))
        dk_ref[late, own] = SCALE * dot_nn(edges[1][1], queries[1])
        dv_ref[early, own] = dot_nn(sum0[place], grads[0]) + dot_nn(sums1[at, 0], grads[1])
        dv_ref[late, own] = dot_nn(sums1[at, 1], grads[1])
    for copy in copies:
        copy.wait()


def backward(first, count, queries, keys, values, grads, before, probs0, sums0, probs1, sums1, prefix, made, after):
    rows, width = keys.shape
    heads = width // HEAD_DIM
    last = first + count == heads
    wide = count * HEAD_DIM
    scratch = [pltpu.VMEM((GROUP,) + prefix[0].shape, BF16)]
    if last:
        scratch += [pltpu.VMEM((rows, width), BF16), pltpu.SemaphoreType.DMA((heads // heads_a_step(heads),))]
    return run_once(
        lambda *refs: back_body(first, count, sent_chunks(heads), even_chunks(heads), *refs),
        [queries, keys, values, grads, *prefix, *before, *probs0, *sums0, probs1, sums1, *made],
        [((rows, width if last else wide), BF16), ((rows, wide), F32), ((rows, wide), F32)],
        scratch,
        16 * 2 * WINDOW * WINDOW * wide * 2,
        40 * WINDOW * wide * 2,
        after=after,
        pushed=(0,) if last else (),
    )[0]


def edge_body(last, k_ref, v_ref, qn_ref, sent_ref, dk_ref, dv_ref):
    width = k_ref.shape[1]
    stats = jnp.zeros((2 * STATS, WINDOW), F32)
    for part in range(3):
        at_rows, at_cols = stat_place(width, 2 - part)
        stats = stats + sent_ref[at_rows, at_cols].astype(F32)
    keys_at, queries_at = tile_iotas()
    beyond = jnp.where(lax.axis_index("ctx") < last, 0, 2 * WINDOW)
    mask = keys_at > queries_at + beyond
    late = slice(WINDOW, 2 * WINDOW)
    for head in range(width // HEAD_DIM):
        cols = columns_of(head)
        query = jnp.concatenate([qn_ref[:, cols], sent_ref[WINDOW + stat_rows(width) :, cols]], 0)
        grad = sent_ref[:WINDOW, cols]
        lse = stats[head : head + 1, :] * (1.0 / LN2)
        delta = stats[STATS + head : STATS + head + 1, :]
        scores = dot_nt(k_ref[late, cols], query) * SCALE_LOG2
        probs = jnp.where(mask, jnp.exp2(scores - lse), 0.0)
        edges = probs * (dot_nt(v_ref[late, cols], grad) - delta)
        dk_ref[:, cols] = SCALE * dot_nn(edges.astype(BF16), query)
        dv_ref[:, cols] = dot_nn(probs.astype(BF16), grad)


def edge(keys, values, queries_after, grads_after, after):
    width = keys.shape[1]
    last = lax.axis_size("ctx") - 1
    return run_once(
        lambda *refs: edge_body(last, *refs),
        [keys, values, queries_after, grads_after],
        [((WINDOW, width), F32)] * 2,
        [],
        4 * 2 * WINDOW * WINDOW * width,
        12 * WINDOW * width,
        after=after,
    )[0]


def last_body(even, k_ref, v_ref, ek_ref, ev_ref, *rest):
    ins, rest = rest[:GROUP], rest[GROUP:]
    dk_in, dv_in = rest[: len(even)], rest[len(even) : 2 * len(even)]
    dk_ref, dv_ref, held, dk_held, dv_held, dk_done, dv_done = rest[2 * len(even) :]
    early, late = slice(0, WINDOW), slice(WINDOW, 2 * WINDOW)
    collect(ins, held)
    copies = []
    for head in range(k_ref.shape[1] // HEAD_DIM):
        cols = columns_of(head)
        dk_ref_in, at = picked(even, dk_in, head)
        dv_ref_in = picked(even, dv_in, head)[0]
        state = held_state(held, head, True)
        keys = dk_ref_in[:, columns_of(at)] + dot_nt(v_ref[:, cols], state)
        dk_held[early, cols] = keys[early].astype(BF16)
        dk_held[late, cols] = (keys[late] + ek_ref[:, cols]).astype(BF16)
        push(dk_held, dk_ref, dk_done, head, copies)
        values = dv_ref_in[:, columns_of(at)] + dot_nn(k_ref[:, cols], state)
        dv_held[early, cols] = values[early].astype(BF16)
        dv_held[late, cols] = (values[late] + ev_ref[:, cols]).astype(BF16)
        push(dv_held, dv_ref, dv_done, head, copies)
    for copy in copies:
        copy.wait()


def finish(keys, values, dk_parts, dv_parts, edges, suffix):
    rows, width = keys.shape
    heads = width // HEAD_DIM
    done = pltpu.SemaphoreType.DMA((heads // heads_a_step(heads),))
    return run_once(
        lambda *refs: last_body(even_chunks(heads), *refs),
        [keys, values, *edges, *suffix, *dk_parts, *dv_parts],
        [((rows, width), BF16)] * 2,
        [pltpu.VMEM((GROUP,) + suffix[0].shape, BF16)] + [pltpu.VMEM((rows, width), BF16)] * 2 + [done, done],
        4 * rows * width * HEAD_DIM,
        18 * rows * width,
        pushed=(0, 1),
    )[0]


def summed(value, axis):
    count = lax.axis_size(axis)
    mask = 1
    while mask < count:
        value = value + lax.ppermute(value, axis, [(at, at ^ mask) for at in range(count)])
        mask *= 2
    return value


def on_device(queries, keys, values, gain, cotangent):
    rows, width = queries.shape
    heads = width // HEAD_DIM
    features = width * lax.axis_size("head")
    sent, even = sent_chunks(heads), even_chunks(heads)
    gain = gain.reshape(1, width)
    late, own, grads_after = [], [], []

    before = [turn(keys[rows - WINDOW :, : sent[0][1] * HEAD_DIM], 1)]
    pieces, tails = local_states(keys, values)

    def first_round():
        late.append(late_rows(*even[0], queries, keys, values, pieces[:1]))
        return tails, [before[0], late[0][2]]

    def second_round(total, held):
        before.extend(onward(tail, 1) if at else turn(tail, 1) for at, tail in enumerate(held))
        late.extend(late_rows(*chunk, queries, keys, values, [total]) for chunk in even[1:])
        return [], [late[-1][2]]

    prefix, merged, _ = scan(pieces, False, first_round, second_round)
    early = []
    for chunk, tail in zip(sent, [before[:2]] + [[tail] for tail in before[2:]]):
        done = [early[-1][4]] if early else []
        early.append(early_rows(*chunk, queries, keys, values, tail, done, merged[:1]))
    probs0, sums0, insides, windows, lses = zip(*early)
    probs1, sums1, parts = zip(*late)
    (hidden, norms), handed = add_prefix(queries, insides, parts, gain, cotangent, prefix, [queries[:AHEAD]])
    after = turn(handed[0], -1)
    norms = summed(norms, "head")
    output, grads, first, *states = normalize(norms, hidden, gain, cotangent, queries, windows, lses[-1], features)

    def own_chunk(at, after):
        made = [own[0][0]] if own else []
        own.append(
            backward(
                *even[at], queries, keys, values, grads, before, probs0, sums0, probs1[at], sums1[at], prefix, made, after
            )
        )

    def first_back():
        own_chunk(0, [])
        return [first], [after, own[0][1]]

    def second_back(total, held):
        grads_after.append(turn(held[0], -1))
        for at in range(1, len(even)):
            own_chunk(at, [total])
        return [], [own[-1][1]]

    suffix, merged, _ = scan(states, True, first_back, second_back)
    edges = edge(keys, values, after, grads_after[0], merged[:1])
    grad_queries, dk_parts, dv_parts = zip(*own)
    grad_keys, grad_values = finish(keys, values, dk_parts, dv_parts, edges, suffix)
    return output, grad_queries[-1], grad_keys, grad_values


def solution(mesh):
    wide = P("ctx", "head")
    return jax.shard_map(
        on_device,
        mesh=mesh,
        in_specs=(wide, wide, wide, P("head"), wide),
        out_specs=(wide, wide, wide, wide),
        check_vma=False,
    )
```

```python
import math

import jax
import jax.numpy as jnp
from jax import lax
from jax.experimental import pallas as pl
from jax.experimental.pallas import tpu as pltpu
from jax.sharding import PartitionSpec as P

HEAD_DIM = 128
WINDOW = 256
GROUP = 4
HOLDERS = 3
STATS = 8
AHEAD = 192
EPSILON = 1e-06
SCALE = 1.0 / math.sqrt(HEAD_DIM)
SCALE_LOG2 = SCALE * math.log2(math.e)
LN2 = math.log(2.0)
MASKED = -1e30
BF16 = jnp.bfloat16
F32 = jnp.float32
VMEM_LIMIT = 24 * 1024 * 1024
VMEM_MOST = 60 * 1024 * 1024


def dot_nn(left, right):
    return lax.dot_general(left, right, (((1,), (0,)), ((), ())), preferred_element_type=F32)


def dot_nt(left, right):
    return lax.dot_general(left, right, (((1,), (1,)), ((), ())), preferred_element_type=F32)


def dot_tn(left, right):
    return lax.dot_general(left, right, (((0,), (0,)), ((), ())), preferred_element_type=F32)


def tile_iotas():
    keys_at = lax.broadcasted_iota(jnp.int32, (WINDOW, WINDOW), 0)
    queries_at = lax.broadcasted_iota(jnp.int32, (WINDOW, WINDOW), 1)
    return keys_at, queries_at


def coef_row(start, count):
    at = start + lax.broadcasted_iota(jnp.int32, (1, count), 1)
    return 1.0 / jnp.sqrt(HEAD_DIM * (at + 1).astype(F32))


def coef_column(start, count):
    at = start + lax.broadcasted_iota(jnp.int32, (count, HEAD_DIM), 0)
    return 1.0 / jnp.sqrt(HEAD_DIM * (at + 1).astype(F32))


def heads_a_step(heads):
    return 2 if heads % 2 == 0 else 1


def sent_chunks(heads):
    return [(0, heads - 2), (heads - 2, 2)] if heads > 4 else [(0, heads)]


def tails_apart(tails):
    return [tuple(tails[:2])] + [(tail, tail) for tail in tails[2:]]


def tail_columns(tail, place):
    keys, values = tail
    below = WINDOW if keys is values else 0
    return keys[:WINDOW, columns_of(place)], values[below : below + WINDOW, columns_of(place)]


def even_chunks(heads):
    return [(0, heads // 2), (heads // 2, heads - heads // 2)] if heads > 1 else [(0, 1)]


def picked(chunks, refs, head):
    for (first, count), ref in zip(chunks, refs):
        if first <= head < first + count:
            return ref, head - first
    raise ValueError


def columns_of(head):
    return slice(head * HEAD_DIM, (head + 1) * HEAD_DIM)


def call(body, grid, in_specs, out_specs, out_shape, scratch, flops, moved, operands, aliases=None, along=(), after=(), vmem=VMEM_LIMIT):
    inputs, results, handed, skipped = len(operands), len(out_shape), len(along), len(after)

    def run(*refs):
        outs = inputs + handed + skipped
        body(*refs[:inputs], *refs[outs : outs + results], *refs[outs + results + handed :])

    given = pl.pallas_call(
        run,
        grid=grid,
        input_output_aliases={**(aliases or {}), **{inputs + at: results + at for at in range(handed)}},
        in_specs=list(in_specs) + [ANY] * (handed + skipped),
        out_specs=list(out_specs) + [ANY] * handed,
        out_shape=list(out_shape) + [jax.ShapeDtypeStruct(array.shape, array.dtype) for array in along],
        scratch_shapes=scratch,
        compiler_params=pltpu.CompilerParams(
            vmem_limit_bytes=vmem,
            dimension_semantics=("arbitrary",) * len(grid),
        ),
        cost_estimate=pl.CostEstimate(flops=flops, bytes_accessed=moved, transcendentals=0),
    )(*operands, *along, *after)
    return list(given[:results]), list(given[results:])


def run_once(body, operands, results, scratch, flops, moved, along=(), after=(), pushed=()):
    return call(
        body,
        (1,),
        [whole(array.shape) for array in operands],
        [HBM if at in pushed else whole(shape) for at, (shape, _) in enumerate(results)],
        [jax.ShapeDtypeStruct(shape, kind) for shape, kind in results],
        scratch,
        flops,
        moved,
        operands,
        None,
        along,
        after,
    )


def push(held, out, done, head, copies):
    step = heads_a_step(held.shape[1] // HEAD_DIM)
    if head % step == step - 1:
        cols = pl.ds((head + 1 - step) * HEAD_DIM, step * HEAD_DIM)
        copy = pltpu.make_async_copy(held.at[:, cols], out.at[:, cols], done.at[head // step])
        copy.start()
        copies.append(copy)


ANY = pl.BlockSpec(memory_space=pl.ANY)
HBM = pl.BlockSpec(memory_space=pltpu.HBM)


def whole(shape):
    return pl.BlockSpec(shape, lambda *_: (0,) * len(shape))


def part_shape(heads):
    return (-(-heads * HEAD_DIM // (HOLDERS * 16)) * 16, HEAD_DIM)


def spans(held, head, reverse):
    rows = held.shape[1]
    first, last = head * HEAD_DIM, (head + 1) * HEAD_DIM
    at = first
    while at < last:
        count = min(last, (at // rows + 1) * rows) - at
        yield at // rows + (GROUP - HOLDERS if reverse else 0), at % rows, at - first, count
        at += count


def store_state(held, head, state, reverse):
    for slot, at, start, count in spans(held, head, reverse):
        held[slot, at : at + count, :] = state[start : start + count]


def held_state(held, head, reverse):
    pieces = [held[slot, at : at + count, :] for slot, at, _, count in spans(held, head, reverse)]
    return pieces[0] if len(pieces) == 1 else jnp.concatenate(pieces, 0)


def spread(held, outs):
    place = lax.rem(lax.axis_index("ctx"), GROUP)
    for other in range(GROUP):
        outs[other][...] = held[lax.bitwise_xor(place, jnp.int32(other))]


def collect(ins, held):
    place = lax.rem(lax.axis_index("ctx"), GROUP)
    for other in range(GROUP):
        held[lax.bitwise_xor(place, jnp.int32(other))] = ins[other][...]


def state_body(k_ref, v_ref, *rest):
    outs, tails = rest[:GROUP], rest[GROUP:-4]
    k_held, v_held, held, done = rest[-4:]
    rows, width = k_held.shape
    held[...] = jnp.zeros_like(held)
    loads = []
    for first in (rows - WINDOW, 0):
        part = pl.ds(first, rows - WINDOW if first == 0 else WINDOW)
        for source, target in ((k_ref, k_held), (v_ref, v_held)):
            loads.append(pltpu.make_async_copy(source.at[part, :], target.at[part, :], done.at[len(loads)]))
            loads[-1].start()
    for copy in loads[:2]:
        copy.wait()
    sends = []
    for (first, count), tail in zip(sent_chunks(width // HEAD_DIM), tails):
        for at, source in enumerate((v_held,) if first == 0 else (k_held, v_held)):
            sends.append(
                pltpu.make_async_copy(
                    source.at[pl.ds(rows - WINDOW, WINDOW), pl.ds(first * HEAD_DIM, count * HEAD_DIM)],
                    tail.at[pl.ds(at * WINDOW, WINDOW), :],
                    done.at[4 + len(sends)],
                )
            )
            sends[-1].start()
    for copy in loads[2:]:
        copy.wait()
    for head in range(width // HEAD_DIM):
        cols = columns_of(head)
        store_state(held, head, dot_tn(k_held[:, cols], v_held[:, cols]).astype(BF16), False)
    spread(held, outs)
    for copy in sends:
        copy.wait()


def local_states(keys, values):
    rows, width = keys.shape
    heads = width // HEAD_DIM
    tails = [(2 * WINDOW if first else WINDOW, count * HEAD_DIM) for first, count in sent_chunks(heads)]
    piece = part_shape(heads)
    results, _ = call(
        state_body,
        (1,),
        [HBM] * 2,
        [whole(piece)] * GROUP + [ANY] * len(tails),
        [jax.ShapeDtypeStruct(piece, BF16)] * GROUP + [jax.ShapeDtypeStruct(tail, BF16) for tail in tails],
        [
            pltpu.VMEM((rows, width), BF16),
            pltpu.VMEM((rows, width), BF16),
            pltpu.VMEM((GROUP,) + piece, BF16),
            pltpu.SemaphoreType.DMA((4 + 2 * len(tails),)),
        ],
        2 * rows * width * HEAD_DIM,
        2 * 2 * rows * width,
        [keys, values],
        vmem=VMEM_MOST,
    )
    return results[:GROUP], results[GROUP:]


def total_body(*refs):
    total = refs[0][...].astype(F32)
    for ref in refs[1:-1]:
        total = total + ref[...].astype(F32)
    refs[-1][...] = total.astype(refs[-1].dtype)


def merge_body(reverse, groups, *refs):
    block = lax.axis_index("ctx")
    group = block // GROUP
    place = lax.rem(block, GROUP)
    others = refs[: groups - 1]
    own = refs[groups - 1 : groups - 1 + GROUP]
    outs = refs[groups - 1 + GROUP :]
    total = jnp.zeros(outs[0].shape, F32)
    for step in range(1, groups):
        wanted = group + step < groups if reverse else group - step >= 0
        total = total + others[step - 1][...].astype(F32) * wanted.astype(F32)
    for target in range(GROUP):
        to = lax.bitwise_xor(place, jnp.int32(target))
        result = total
        for source in range(GROUP):
            if source == target:
                continue
            of = lax.bitwise_xor(place, jnp.int32(source))
            wanted = of > to if reverse else of < to
            result = result + own[source][...].astype(F32) * wanted.astype(F32)
        outs[target][...] = result.astype(outs[target].dtype)


def swap(value, mask):
    count = lax.axis_size("ctx")
    return lax.ppermute(value, "ctx", [(at, at ^ mask) for at in range(count)])


def turn(value, steps):
    count = lax.axis_size("ctx")
    return lax.ppermute(value, "ctx", [(at, (at + steps) % count) for at in range(count)])


def shift(value, steps, places):
    count = lax.axis_size("ctx")
    return lax.ppermute(
        value, "ctx", [(at, at + steps) for at in range(count) if at % GROUP in places and 0 <= at + steps < count]
    )


def onward(value, steps):
    return shift(value, steps, range(GROUP))


def scan(pieces, reverse, first, second):
    groups = lax.axis_size("ctx") // GROUP
    shape = pieces[0].shape
    full = whole(shape)
    size = shape[0] * shape[1]
    out = jax.ShapeDtypeStruct(shape, BF16)
    own = [pieces[0]] + [swap(pieces[other], other) for other in range(1, GROUP)]
    along, after = first()
    (total,), held = call(
        total_body, (1,), [full] * GROUP, [full], [out], [], GROUP * size, 2 * 5 * size, own, None, along, after
    )
    holders = range(GROUP - HOLDERS, GROUP) if reverse else range(HOLDERS)
    others = [shift(total, (-GROUP if reverse else GROUP) * at, holders) for at in range(1, groups)]
    operands = others + own
    along, after = second(total, held)
    merged, held = call(
        lambda *refs: merge_body(reverse, groups, *refs),
        (1,),
        [full] * len(operands),
        [full] * GROUP,
        [out] * GROUP,
        [],
        20 * size,
        2 * 11 * size,
        operands,
        None,
        along,
        after,
    )
    return [merged[0]] + [swap(merged[other], other) for other in range(1, GROUP)], merged, held


def attend(scores, masks, coef, linear):
    shown = [jnp.where(mask, score, MASKED) for score, mask in zip(scores, masks)]
    peak = jnp.max(shown[0], 0, keepdims=True)
    for tile in shown[1:]:
        peak = jnp.maximum(peak, jnp.max(tile, 0, keepdims=True))
    powers = [jnp.exp2((tile - peak) * SCALE_LOG2) for tile in shown]
    norm = jnp.sum(powers[0], 0, keepdims=True)
    for tile in powers[1:]:
        norm = norm + jnp.sum(tile, 0, keepdims=True)
    share = 1.0 / norm
    probs = [tile * share for tile in powers]
    sums = []
    for prob, score, mask, kind in zip(probs, scores, masks, linear):
        if kind == "none":
            sums.append(None)
        elif kind == "all":
            sums.append((prob + score * coef).astype(BF16))
        else:
            sums.append((prob + jnp.where(mask, score * coef, 0.0)).astype(BF16))
    lse = peak * SCALE + jnp.log(norm)
    return [prob.astype(BF16) for prob in probs], sums, lse


def late_body(first, count, q_ref, k_ref, v_ref, prob_ref, sum_ref, part_ref):
    rows = k_ref.shape[0]
    start = lax.axis_index("ctx") * rows
    keys_at, queries_at = tile_iotas()
    coef = coef_row(start + WINDOW, WINDOW)
    masks = [keys_at > queries_at, keys_at <= queries_at]
    for at in range(count):
        cols = columns_of(first + at)
        query = q_ref[WINDOW : 2 * WINDOW, cols]
        scores = [dot_nt(k_ref[tile * WINDOW : (tile + 1) * WINDOW, cols], query) for tile in range(2)]
        probs, sums, _ = attend(scores, masks, coef, ["all", "masked"])
        total = jnp.zeros((HEAD_DIM, WINDOW), F32)
        for tile in range(2):
            prob_ref[at, tile] = probs[tile]
            sum_ref[at, tile] = sums[tile]
            total = total + dot_tn(v_ref[tile * WINDOW : (tile + 1) * WINDOW, cols], sums[tile])
        part_ref[:, columns_of(at)] = total.T


def late_rows(first, count, queries, keys, values, after):
    tiles = (count, 2, WINDOW, WINDOW)
    wide = count * HEAD_DIM
    return run_once(
        lambda *refs: late_body(first, count, *refs),
        [queries, keys, values],
        [(tiles, BF16), (tiles, BF16), ((WINDOW, wide), F32)],
        [],
        4 * 2 * WINDOW * WINDOW * wide * 4,
        24 * WINDOW * wide,
        after=after,
    )[0]


def early_body(first, count, sent, q_ref, k_ref, v_ref, *rest):
    tail, rest = (rest[0], rest[sent - 1]), rest[sent:]
    prob_ref, sum_ref, inside_ref, window_ref, lse_ref = rest[-5:]
    rows = k_ref.shape[0]
    block = lax.axis_index("ctx")
    lse_ref[...] = rest[0][...] if len(rest) > 5 else jnp.zeros_like(lse_ref)
    keys_at, queries_at = tile_iotas()
    beyond = jnp.where(block > 0, 0, 2 * WINDOW)
    masks = [keys_at > queries_at + beyond, keys_at <= queries_at]
    coef = coef_row(block * rows, WINDOW)
    for at in range(count):
        cols, own = columns_of(first + at), columns_of(at)
        query = q_ref[:WINDOW, cols]
        key_before, value_before = tail_columns(tail, at)
        scores = [dot_nt(key_before, query), dot_nt(k_ref[:WINDOW, cols], query)]
        probs, sums, lse = attend(scores, masks, coef, ["none", "masked"])
        prob_ref[at, 0] = probs[0]
        prob_ref[at, 1] = probs[1]
        sum_ref[at] = sums[1]
        lse_ref[first + at : first + at + 1, :] = lse
        value = v_ref[:WINDOW, cols]
        before = dot_tn(value_before, probs[0])
        window_ref[:, own] = (before + dot_tn(value, probs[1])).T
        inside_ref[:, own] = (before + dot_tn(value, sums[1])).T


def early_rows(first, count, queries, keys, values, before, done, after):
    wide = count * HEAD_DIM
    return run_once(
        lambda *refs: early_body(first, count, len(before), *refs),
        [queries, keys, values, *before, *done],
        [
            ((count, 2, WINDOW, WINDOW), BF16),
            ((count, WINDOW, WINDOW), BF16),
            ((WINDOW, wide), F32),
            ((WINDOW, wide), F32),
            ((STATS, WINDOW), F32),
        ],
        [],
        5 * 2 * WINDOW * WINDOW * wide * 4,
        24 * WINDOW * wide,
        after=after,
    )[0]


def sum_body(sent, even, q_ref, gain_ref, cot_ref, *rest):
    ins, rest = rest[:GROUP], rest[GROUP:]
    insides, rest = rest[: len(sent)], rest[len(sent) :]
    parts, rest = rest[: len(even)], rest[len(even) :]
    hidden_ref, norm_ref, held, squares, crossed, columns = rest
    rows, width = q_ref.shape
    collect(ins, held)
    columns[...] = coef_column(lax.axis_index("ctx") * rows, rows)
    for head in range(width // HEAD_DIM):
        cols = columns_of(head)
        inside, at = picked(sent, insides, head)
        part, late = picked(even, parts, head)
        carried = columns[...] * dot_nn(q_ref[:, cols], held_state(held, head, False))
        hidden = jnp.concatenate([inside[:, columns_of(at)], part[:, columns_of(late)]], 0) + carried
        hidden_ref[:, cols] = hidden
        scaled = gain_ref[:, cols].astype(F32) * cot_ref[:, cols].astype(F32)
        if head == 0:
            squares[...] = hidden * hidden
            crossed[...] = hidden * scaled
        else:
            squares[...] += hidden * hidden
            crossed[...] += hidden * scaled
    norm_ref[...] = jnp.zeros_like(norm_ref)
    norm_ref[0:1, :] = jnp.sum(squares[...].T, 0, keepdims=True)
    norm_ref[1:2, :] = jnp.sum(crossed[...].T, 0, keepdims=True)


def add_prefix(queries, insides, parts, gain, cotangent, prefix, along):
    rows, width = queries.shape
    heads = width // HEAD_DIM
    return run_once(
        lambda *refs: sum_body(sent_chunks(heads), even_chunks(heads), *refs),
        [queries, gain, cotangent, *prefix, *insides, *parts],
        [((rows, width), F32), ((STATS, rows), F32)],
        [pltpu.VMEM((GROUP,) + prefix[0].shape, BF16)] + [pltpu.VMEM((rows, HEAD_DIM), F32)] * 3,
        2 * rows * width * HEAD_DIM,
        12 * rows * width,
        along,
    )


def stat_rows(width):
    return 2 * STATS * -(-3 * WINDOW // width)


def stat_place(width, part):
    across = width // WINDOW
    return (
        slice(WINDOW + part // across * 2 * STATS, WINDOW + (part // across + 1) * 2 * STATS),
        slice(part % across * WINDOW, (part % across + 1) * WINDOW),
    )


def norm_body(sent, features, norm_ref, hidden_ref, gain_ref, cot_ref, q_ref, lse_ref, *rest):
    windows, rest = rest[: len(sent)], rest[len(sent) :]
    out_ref, grad_ref, first_ref = rest[:3]
    outs = rest[3 : 3 + GROUP]
    held, recip, pull, columns, stats, out_held, done = rest[3 + GROUP :]
    rows, width = q_ref.shape
    root = 1.0 / jnp.sqrt(norm_ref[0:1, :] / features + EPSILON)
    slope = root * root * root * norm_ref[1:2, :] / features
    recip[...] = jnp.broadcast_to(root, (HEAD_DIM, rows)).T
    pull[...] = jnp.broadcast_to(slope, (HEAD_DIM, rows)).T
    columns[...] = coef_column(lax.axis_index("ctx") * rows, rows)
    stats[...] = jnp.zeros_like(stats)
    stats[:STATS, :] = lse_ref[...]
    held[...] = jnp.zeros_like(held)
    copies = []
    for head in range(width // HEAD_DIM):
        cols = columns_of(head)
        hidden = hidden_ref[:, cols]
        gain = gain_ref[:, cols].astype(F32)
        kept = recip[...]
        out_held[:, cols] = (hidden * kept * gain).astype(BF16)
        push(out_held, out_ref, done, head, copies)
        full = kept * (gain * cot_ref[:, cols].astype(F32)) - hidden * pull[...]
        grad = full.astype(BF16)
        grad_ref[:, cols] = grad
        first_ref[:WINDOW, cols] = grad[:WINDOW]
        window, at = picked(sent, windows, head)
        delta = (grad[:WINDOW].astype(F32) * window[:, columns_of(at)]).T
        stats[STATS + head : STATS + head + 1, :] = jnp.sum(delta, 0, keepdims=True)
        state = dot_tn(q_ref[:, cols], (full * columns[...]).astype(BF16)).astype(BF16)
        store_state(held, head, state, True)
    spread(held, outs)
    left = stats[...]
    below = WINDOW + stat_rows(width)
    first_ref[WINDOW:below, :] = jnp.zeros((below - WINDOW, width), BF16)
    first_ref[below:, :] = q_ref[AHEAD:WINDOW, :]
    for part in range(3):
        at_rows, at_cols = stat_place(width, part)
        taken = left.astype(BF16)
        first_ref[at_rows, at_cols] = taken
        left = left - taken.astype(F32)
    for copy in copies:
        copy.wait()


def normalize(norms, hidden, gain, cotangent, queries, windows, lse, features):
    rows, width = queries.shape
    heads = width // HEAD_DIM
    piece = part_shape(heads)
    return run_once(
        lambda *refs: norm_body(sent_chunks(heads), features, *refs),
        [norms, hidden, gain, cotangent, queries, lse, *windows],
        [((rows, width), BF16), ((rows, width), BF16), ((2 * WINDOW - AHEAD + stat_rows(width), width), BF16)] + [(piece, BF16)] * GROUP,
        [pltpu.VMEM((GROUP,) + piece, BF16)]
        + [pltpu.VMEM((rows, HEAD_DIM), F32)] * 3
        + [
            pltpu.VMEM((2 * STATS, WINDOW), F32),
            pltpu.VMEM((rows, width), BF16),
            pltpu.SemaphoreType.DMA((heads // heads_a_step(heads),)),
        ],
        2 * rows * width * HEAD_DIM,
        14 * rows * width,
        pushed=(0,),
    )[0]


def back_body(first, count, sent, even, q_ref, k_ref, v_ref, g_ref, *rest):
    heads = q_ref.shape[1] // HEAD_DIM
    rows = q_ref.shape[0]
    last = first + count == heads
    ins, rest = rest[:GROUP], rest[GROUP:]
    tails, rest = tails_apart(rest[: len(sent) + 1]), rest[len(sent) + 1 :]
    probs0, rest = rest[: len(sent)], rest[len(sent) :]
    sums0, rest = rest[: len(sent)], rest[len(sent) :]
    probs1, sums1 = rest[0], rest[1]
    made = rest[2:-3] if not last else rest[2:-5]
    if last:
        dk_ref, dv_ref, held, dq_held, done = rest[-5:]
        dq_ref, made = made[-1], made[:-1]
    else:
        dq_held, dk_ref, dv_ref, held = made[-1], *rest[-3:]
        dq_ref, made = None, made[:-1]
    collect(ins, held)
    keys_at, queries_at = tile_iotas()
    causal = keys_at <= queries_at
    start = lax.axis_index("ctx") * rows
    ratios = coef_row(start, rows) * (1.0 / SCALE)
    early, late = slice(0, WINDOW), slice(WINDOW, 2 * WINDOW)
    copies = []
    if last and made:
        dq_held[:, : first * HEAD_DIM] = made[0][...]
        for head in range(first):
            push(dq_held, dq_ref, done, head, copies)
    for at in range(count):
        head = first + at
        cols, own = columns_of(head), columns_of(at)
        tail, place = picked(sent, tails, head)
        key_before, value_before = tail_columns(tail, place)
        prob0 = picked(sent, probs0, head)[0]
        sum0 = picked(sent, sums0, head)[0]
        grads = g_ref[early, cols], g_ref[late, cols]
        queries = q_ref[early, cols], q_ref[late, cols]
        keys = key_before, k_ref[early, cols], k_ref[late, cols]
        values = value_before, v_ref[early, cols], v_ref[late, cols]
        probs = (
            (prob0[place, 0].astype(F32), prob0[place, 1].astype(F32)),
            (probs1[at, 0].astype(F32), probs1[at, 1].astype(F32)),
        )
        edges = []
        for half in range(2):
            ratio = ratios[:, half * WINDOW : (half + 1) * WINDOW]
            pulls = [dot_nt(values[half + tile], grads[half]) for tile in range(2)]
            delta = jnp.sum(probs[half][0] * pulls[0] + probs[half][1] * pulls[1], 0, keepdims=True)
            before = probs[half][0] * (pulls[0] - delta)
            if half == 1:
                before = before + pulls[0] * ratio
            here = probs[half][1] * (pulls[1] - delta) + jnp.where(causal, pulls[1] * ratio, 0.0)
            edges.append((before.astype(BF16), here.astype(BF16)))
        state = held_state(held, head, False)
        for half, part in enumerate((early, late)):
            inner = dot_tn(keys[half], edges[half][0]) + dot_tn(keys[half + 1], edges[half][1])
            carried = (coef_row(start + half * WINDOW, WINDOW) * (1.0 / SCALE)) * dot_nt(state, grads[half])
            dq_held[part, cols if last else own] = ((inner + carried).T * SCALE).astype(BF16)
        if last:
            push(dq_held, dq_ref, done, head, copies)
        dk_ref[early, own] = SCALE * (dot_nn(edges[0][1], queries[0]) + dot_nn(edges[1][0], queries[1]))
        dk_ref[late, own] = SCALE * dot_nn(edges[1][1], queries[1])
        dv_ref[early, own] = dot_nn(sum0[place], grads[0]) + dot_nn(sums1[at, 0], grads[1])
        dv_ref[late, own] = dot_nn(sums1[at, 1], grads[1])
    for copy in copies:
        copy.wait()


def backward(first, count, queries, keys, values, grads, before, probs0, sums0, probs1, sums1, prefix, made, after):
    rows, width = keys.shape
    heads = width // HEAD_DIM
    last = first + count == heads
    wide = count * HEAD_DIM
    scratch = [pltpu.VMEM((GROUP,) + prefix[0].shape, BF16)]
    if last:
        scratch += [pltpu.VMEM((rows, width), BF16), pltpu.SemaphoreType.DMA((heads // heads_a_step(heads),))]
    return run_once(
        lambda *refs: back_body(first, count, sent_chunks(heads), even_chunks(heads), *refs),
        [queries, keys, values, grads, *prefix, *before, *probs0, *sums0, probs1, sums1, *made],
        [((rows, width if last else wide), BF16), ((rows, wide), F32), ((rows, wide), F32)],
        scratch,
        16 * 2 * WINDOW * WINDOW * wide * 2,
        40 * WINDOW * wide * 2,
        after=after,
        pushed=(0,) if last else (),
    )[0]


def edge_body(last, k_ref, v_ref, qn_ref, sent_ref, dk_ref, dv_ref):
    width = k_ref.shape[1]
    stats = jnp.zeros((2 * STATS, WINDOW), F32)
    for part in range(3):
        at_rows, at_cols = stat_place(width, 2 - part)
        stats = stats + sent_ref[at_rows, at_cols].astype(F32)
    keys_at, queries_at = tile_iotas()
    beyond = jnp.where(lax.axis_index("ctx") < last, 0, 2 * WINDOW)
    mask = keys_at > queries_at + beyond
    late = slice(WINDOW, 2 * WINDOW)
    for head in range(width // HEAD_DIM):
        cols = columns_of(head)
        query = jnp.concatenate([qn_ref[:, cols], sent_ref[WINDOW + stat_rows(width) :, cols]], 0)
        grad = sent_ref[:WINDOW, cols]
        lse = stats[head : head + 1, :] * (1.0 / LN2)
        delta = stats[STATS + head : STATS + head + 1, :]
        scores = dot_nt(k_ref[late, cols], query) * SCALE_LOG2
        probs = jnp.where(mask, jnp.exp2(scores - lse), 0.0)
        edges = probs * (dot_nt(v_ref[late, cols], grad) - delta)
        dk_ref[:, cols] = SCALE * dot_nn(edges.astype(BF16), query)
        dv_ref[:, cols] = dot_nn(probs.astype(BF16), grad)


def edge(keys, values, queries_after, grads_after, after):
    width = keys.shape[1]
    last = lax.axis_size("ctx") - 1
    return run_once(
        lambda *refs: edge_body(last, *refs),
        [keys, values, queries_after, grads_after],
        [((WINDOW, width), F32)] * 2,
        [],
        4 * 2 * WINDOW * WINDOW * width,
        12 * WINDOW * width,
        after=after,
    )[0]


def last_body(even, k_ref, v_ref, ek_ref, ev_ref, *rest):
    ins, rest = rest[:GROUP], rest[GROUP:]
    dk_in, dv_in = rest[: len(even)], rest[len(even) : 2 * len(even)]
    dk_ref, dv_ref, held, dk_held, dv_held, dk_done, dv_done = rest[2 * len(even) :]
    early, late = slice(0, WINDOW), slice(WINDOW, 2 * WINDOW)
    collect(ins, held)
    copies = []
    for head in range(k_ref.shape[1] // HEAD_DIM):
        cols = columns_of(head)
        dk_ref_in, at = picked(even, dk_in, head)
        dv_ref_in = picked(even, dv_in, head)[0]
        state = held_state(held, head, True)
        keys = dk_ref_in[:, columns_of(at)] + dot_nt(v_ref[:, cols], state)
        dk_held[early, cols] = keys[early].astype(BF16)
        dk_held[late, cols] = (keys[late] + ek_ref[:, cols]).astype(BF16)
        push(dk_held, dk_ref, dk_done, head, copies)
        values = dv_ref_in[:, columns_of(at)] + dot_nn(k_ref[:, cols], state)
        dv_held[early, cols] = values[early].astype(BF16)
        dv_held[late, cols] = (values[late] + ev_ref[:, cols]).astype(BF16)
        push(dv_held, dv_ref, dv_done, head, copies)
    for copy in copies:
        copy.wait()


def finish(keys, values, dk_parts, dv_parts, edges, suffix):
    rows, width = keys.shape
    heads = width // HEAD_DIM
    done = pltpu.SemaphoreType.DMA((heads // heads_a_step(heads),))
    return run_once(
        lambda *refs: last_body(even_chunks(heads), *refs),
        [keys, values, *edges, *suffix, *dk_parts, *dv_parts],
        [((rows, width), BF16)] * 2,
        [pltpu.VMEM((GROUP,) + suffix[0].shape, BF16)] + [pltpu.VMEM((rows, width), BF16)] * 2 + [done, done],
        4 * rows * width * HEAD_DIM,
        18 * rows * width,
        pushed=(0, 1),
    )[0]


def summed(value, axis):
    count = lax.axis_size(axis)
    mask = 1
    while mask < count:
        value = value + lax.ppermute(value, axis, [(at, at ^ mask) for at in range(count)])
        mask *= 2
    return value


def on_device(queries, keys, values, gain, cotangent):
    rows, width = queries.shape
    heads = width // HEAD_DIM
    features = width * lax.axis_size("head")
    sent, even = sent_chunks(heads), even_chunks(heads)
    gain = gain.reshape(1, width)
    late, own, grads_after = [], [], []

    before = [turn(keys[rows - WINDOW :, : sent[0][1] * HEAD_DIM], 1)]
    pieces, tails = local_states(keys, values)

    def first_round():
        late.append(late_rows(*even[0], queries, keys, values, pieces[:1]))
        return tails, [before[0], late[0][2]]

    def second_round(total, held):
        before.extend(onward(tail, 1) if at else turn(tail, 1) for at, tail in enumerate(held))
        late.extend(late_rows(*chunk, queries, keys, values, [total]) for chunk in even[1:])
        return [], [late[-1][2]]

    prefix, merged, _ = scan(pieces, False, first_round, second_round)
    early = []
    for chunk, tail in zip(sent, [before[:2]] + [[tail] for tail in before[2:]]):
        done = [early[-1][4]] if early else []
        early.append(early_rows(*chunk, queries, keys, values, tail, done, merged[:1]))
    probs0, sums0, insides, windows, lses = zip(*early)
    probs1, sums1, parts = zip(*late)
    (hidden, norms), handed = add_prefix(queries, insides, parts, gain, cotangent, prefix, [queries[:AHEAD]])
    after = turn(handed[0], -1)
    norms = summed(norms, "head")
    output, grads, first, *states = normalize(norms, hidden, gain, cotangent, queries, windows, lses[-1], features)

    def own_chunk(at, after):
        made = [own[0][0]] if own else []
        own.append(
            backward(
                *even[at], queries, keys, values, grads, before, probs0, sums0, probs1[at], sums1[at], prefix, made, after
            )
        )

    def first_back():
        own_chunk(0, [])
        return [first], [after, own[0][1]]

    def second_back(total, held):
        grads_after.append(turn(held[0], -1))
        for at in range(1, len(even)):
            own_chunk(at, [total])
        return [], [own[-1][1]]

    suffix, merged, _ = scan(states, True, first_back, second_back)
    edges = edge(keys, values, after, grads_after[0], merged[:1])
    grad_queries, dk_parts, dv_parts = zip(*own)
    grad_keys, grad_values = finish(keys, values, dk_parts, dv_parts, edges, suffix)
    return output, grad_queries[-1], grad_keys, grad_values


def solution(mesh):
    wide = P("ctx", "head")
    return jax.shard_map(
        on_device,
        mesh=mesh,
        in_specs=(wide, wide, wide, P("head"), wide),
        out_specs=(wide, wide, wide, wide),
        check_vma=False,
    )
```

```python
import math

import jax
import jax.numpy as jnp
from jax import lax
from jax.experimental import pallas as pl
from jax.experimental.pallas import tpu as pltpu
from jax.sharding import PartitionSpec as P

HEAD_DIM = 128
WINDOW = 256
GROUP = 4
HOLDERS = 3
STATS = 8
AHEAD = 192
EPSILON = 1e-06
SCALE = 1.0 / math.sqrt(HEAD_DIM)
SCALE_LOG2 = SCALE * math.log2(math.e)
LN2 = math.log(2.0)
MASKED = -1e30
BF16 = jnp.bfloat16
F32 = jnp.float32
VMEM_LIMIT = 24 * 1024 * 1024
VMEM_MOST = 60 * 1024 * 1024


def dot_nn(left, right):
    return lax.dot_general(left, right, (((1,), (0,)), ((), ())), preferred_element_type=F32)


def dot_nt(left, right):
    return lax.dot_general(left, right, (((1,), (1,)), ((), ())), preferred_element_type=F32)


def dot_tn(left, right):
    return lax.dot_general(left, right, (((0,), (0,)), ((), ())), preferred_element_type=F32)


def tile_iotas():
    keys_at = lax.broadcasted_iota(jnp.int32, (WINDOW, WINDOW), 0)
    queries_at = lax.broadcasted_iota(jnp.int32, (WINDOW, WINDOW), 1)
    return keys_at, queries_at


def coef_row(start, count):
    at = start + lax.broadcasted_iota(jnp.int32, (1, count), 1)
    return 1.0 / jnp.sqrt(HEAD_DIM * (at + 1).astype(F32))


def coef_column(start, count):
    at = start + lax.broadcasted_iota(jnp.int32, (count, HEAD_DIM), 0)
    return 1.0 / jnp.sqrt(HEAD_DIM * (at + 1).astype(F32))


def heads_a_step(heads):
    return 2 if heads % 2 == 0 else 1


def sent_chunks(heads):
    return [(0, heads - 2), (heads - 2, 2)] if heads > 4 else [(0, heads)]


def tails_apart(tails):
    return [tuple(tails[:2])] + [(tail, tail) for tail in tails[2:]]


def tail_columns(tail, place):
    keys, values = tail
    below = WINDOW if keys is values else 0
    return keys[:WINDOW, columns_of(place)], values[below : below + WINDOW, columns_of(place)]


def even_chunks(heads):
    first = max(1, heads * 5 // 8)
    return [(0, first), (first, heads - first)] if heads > 1 else [(0, 1)]


def picked(chunks, refs, head):
    for (first, count), ref in zip(chunks, refs):
        if first <= head < first + count:
            return ref, head - first
    raise ValueError


def columns_of(head):
    return slice(head * HEAD_DIM, (head + 1) * HEAD_DIM)


def call(body, grid, in_specs, out_specs, out_shape, scratch, flops, moved, operands, aliases=None, along=(), after=(), vmem=VMEM_LIMIT):
    inputs, results, handed, skipped = len(operands), len(out_shape), len(along), len(after)

    def run(*refs):
        outs = inputs + handed + skipped
        body(*refs[:inputs], *refs[outs : outs + results], *refs[outs + results + handed :])

    given = pl.pallas_call(
        run,
        grid=grid,
        input_output_aliases={**(aliases or {}), **{inputs + at: results + at for at in range(handed)}},
        in_specs=list(in_specs) + [ANY] * (handed + skipped),
        out_specs=list(out_specs) + [ANY] * handed,
        out_shape=list(out_shape) + [jax.ShapeDtypeStruct(array.shape, array.dtype) for array in along],
        scratch_shapes=scratch,
        compiler_params=pltpu.CompilerParams(
            vmem_limit_bytes=vmem,
            dimension_semantics=("arbitrary",) * len(grid),
        ),
        cost_estimate=pl.CostEstimate(flops=flops, bytes_accessed=moved, transcendentals=0),
    )(*operands, *along, *after)
    return list(given[:results]), list(given[results:])


def run_once(body, operands, results, scratch, flops, moved, along=(), after=(), pushed=()):
    return call(
        body,
        (1,),
        [whole(array.shape) for array in operands],
        [HBM if at in pushed else whole(shape) for at, (shape, _) in enumerate(results)],
        [jax.ShapeDtypeStruct(shape, kind) for shape, kind in results],
        scratch,
        flops,
        moved,
        operands,
        None,
        along,
        after,
    )


def push(held, out, done, head, copies):
    step = heads_a_step(held.shape[1] // HEAD_DIM)
    if head % step == step - 1:
        cols = pl.ds((head + 1 - step) * HEAD_DIM, step * HEAD_DIM)
        copy = pltpu.make_async_copy(held.at[:, cols], out.at[:, cols], done.at[head // step])
        copy.start()
        copies.append(copy)


ANY = pl.BlockSpec(memory_space=pl.ANY)
HBM = pl.BlockSpec(memory_space=pltpu.HBM)


def whole(shape):
    return pl.BlockSpec(shape, lambda *_: (0,) * len(shape))


def part_shape(heads):
    return (-(-heads * HEAD_DIM // (HOLDERS * 16)) * 16, HEAD_DIM)


def spans(held, head, reverse):
    rows = held.shape[1]
    first, last = head * HEAD_DIM, (head + 1) * HEAD_DIM
    at = first
    while at < last:
        count = min(last, (at // rows + 1) * rows) - at
        yield at // rows + (GROUP - HOLDERS if reverse else 0), at % rows, at - first, count
        at += count


def store_state(held, head, state, reverse):
    for slot, at, start, count in spans(held, head, reverse):
        held[slot, at : at + count, :] = state[start : start + count]


def held_state(held, head, reverse):
    pieces = [held[slot, at : at + count, :] for slot, at, _, count in spans(held, head, reverse)]
    return pieces[0] if len(pieces) == 1 else jnp.concatenate(pieces, 0)


def spread(held, outs):
    place = lax.rem(lax.axis_index("ctx"), GROUP)
    for other in range(GROUP):
        outs[other][...] = held[lax.bitwise_xor(place, jnp.int32(other))]


def collect(ins, held):
    place = lax.rem(lax.axis_index("ctx"), GROUP)
    for other in range(GROUP):
        held[lax.bitwise_xor(place, jnp.int32(other))] = ins[other][...]


def state_body(k_ref, v_ref, *rest):
    outs, tails = rest[:GROUP], rest[GROUP:-4]
    k_held, v_held, held, done = rest[-4:]
    rows, width = k_held.shape
    held[...] = jnp.zeros_like(held)
    loads = []
    for first in (rows - WINDOW, 0):
        part = pl.ds(first, rows - WINDOW if first == 0 else WINDOW)
        for source, target in ((k_ref, k_held), (v_ref, v_held)):
            loads.append(pltpu.make_async_copy(source.at[part, :], target.at[part, :], done.at[len(loads)]))
            loads[-1].start()
    for copy in loads[:2]:
        copy.wait()
    sends = []
    for (first, count), tail in zip(sent_chunks(width // HEAD_DIM), tails):
        for at, source in enumerate((v_held,) if first == 0 else (k_held, v_held)):
            sends.append(
                pltpu.make_async_copy(
                    source.at[pl.ds(rows - WINDOW, WINDOW), pl.ds(first * HEAD_DIM, count * HEAD_DIM)],
                    tail.at[pl.ds(at * WINDOW, WINDOW), :],
                    done.at[4 + len(sends)],
                )
            )
            sends[-1].start()
    for copy in loads[2:]:
        copy.wait()
    for head in range(width // HEAD_DIM):
        cols = columns_of(head)
        store_state(held, head, dot_tn(k_held[:, cols], v_held[:, cols]).astype(BF16), False)
    spread(held, outs)
    for copy in sends:
        copy.wait()


def local_states(keys, values):
    rows, width = keys.shape
    heads = width // HEAD_DIM
    tails = [(2 * WINDOW if first else WINDOW, count * HEAD_DIM) for first, count in sent_chunks(heads)]
    piece = part_shape(heads)
    results, _ = call(
        state_body,
        (1,),
        [HBM] * 2,
        [whole(piece)] * GROUP + [ANY] * len(tails),
        [jax.ShapeDtypeStruct(piece, BF16)] * GROUP + [jax.ShapeDtypeStruct(tail, BF16) for tail in tails],
        [
            pltpu.VMEM((rows, width), BF16),
            pltpu.VMEM((rows, width), BF16),
            pltpu.VMEM((GROUP,) + piece, BF16),
            pltpu.SemaphoreType.DMA((4 + 2 * len(tails),)),
        ],
        2 * rows * width * HEAD_DIM,
        2 * 2 * rows * width,
        [keys, values],
        vmem=VMEM_MOST,
    )
    return results[:GROUP], results[GROUP:]


def total_body(*refs):
    total = refs[0][...].astype(F32)
    for ref in refs[1:-1]:
        total = total + ref[...].astype(F32)
    refs[-1][...] = total.astype(refs[-1].dtype)


def merge_body(reverse, groups, *refs):
    block = lax.axis_index("ctx")
    group = block // GROUP
    place = lax.rem(block, GROUP)
    others = refs[: groups - 1]
    own = refs[groups - 1 : groups - 1 + GROUP]
    outs = refs[groups - 1 + GROUP :]
    total = jnp.zeros(outs[0].shape, F32)
    for step in range(1, groups):
        wanted = group + step < groups if reverse else group - step >= 0
        total = total + others[step - 1][...].astype(F32) * wanted.astype(F32)
    for target in range(GROUP):
        to = lax.bitwise_xor(place, jnp.int32(target))
        result = total
        for source in range(GROUP):
            if source == target:
                continue
            of = lax.bitwise_xor(place, jnp.int32(source))
            wanted = of > to if reverse else of < to
            result = result + own[source][...].astype(F32) * wanted.astype(F32)
        outs[target][...] = result.astype(outs[target].dtype)


def swap(value, mask):
    count = lax.axis_size("ctx")
    return lax.ppermute(value, "ctx", [(at, at ^ mask) for at in range(count)])


def turn(value, steps):
    count = lax.axis_size("ctx")
    return lax.ppermute(value, "ctx", [(at, (at + steps) % count) for at in range(count)])


def shift(value, steps, places):
    count = lax.axis_size("ctx")
    return lax.ppermute(
        value, "ctx", [(at, at + steps) for at in range(count) if at % GROUP in places and 0 <= at + steps < count]
    )


def onward(value, steps):
    return shift(value, steps, range(GROUP))


def scan(pieces, reverse, first, second):
    groups = lax.axis_size("ctx") // GROUP
    shape = pieces[0].shape
    full = whole(shape)
    size = shape[0] * shape[1]
    out = jax.ShapeDtypeStruct(shape, BF16)
    own = [pieces[0]] + [swap(pieces[other], other) for other in range(GROUP - 1, 0, -1)][::-1]
    along, after = first()
    (total,), held = call(
        total_body, (1,), [full] * GROUP, [full], [out], [], GROUP * size, 2 * 5 * size, own, None, along, after
    )
    holders = range(GROUP - HOLDERS, GROUP) if reverse else range(HOLDERS)
    others = [shift(total, (-GROUP if reverse else GROUP) * at, holders) for at in range(1, groups)]
    operands = others + own
    along, after = second(total, held)
    merged, held = call(
        lambda *refs: merge_body(reverse, groups, *refs),
        (1,),
        [full] * len(operands),
        [full] * GROUP,
        [out] * GROUP,
        [],
        20 * size,
        2 * 11 * size,
        operands,
        None,
        along,
        after,
    )
    return [merged[0]] + [swap(merged[other], other) for other in range(GROUP - 1, 0, -1)][::-1], merged, held


def attend(scores, masks, coef, linear):
    shown = [jnp.where(mask, score, MASKED) for score, mask in zip(scores, masks)]
    peak = jnp.max(shown[0], 0, keepdims=True)
    for tile in shown[1:]:
        peak = jnp.maximum(peak, jnp.max(tile, 0, keepdims=True))
    powers = [jnp.exp2((tile - peak) * SCALE_LOG2) for tile in shown]
    norm = jnp.sum(powers[0], 0, keepdims=True)
    for tile in powers[1:]:
        norm = norm + jnp.sum(tile, 0, keepdims=True)
    share = 1.0 / norm
    probs = [tile * share for tile in powers]
    sums = []
    for prob, score, mask, kind in zip(probs, scores, masks, linear):
        if kind == "none":
            sums.append(None)
        elif kind == "all":
            sums.append((prob + score * coef).astype(BF16))
        else:
            sums.append((prob + jnp.where(mask, score * coef, 0.0)).astype(BF16))
    lse = peak * SCALE + jnp.log(norm)
    return [prob.astype(BF16) for prob in probs], sums, lse


def late_body(first, count, q_ref, k_ref, v_ref, prob_ref, sum_ref, part_ref):
    rows = k_ref.shape[0]
    start = lax.axis_index("ctx") * rows
    keys_at, queries_at = tile_iotas()
    coef = coef_row(start + WINDOW, WINDOW)
    masks = [keys_at > queries_at, keys_at <= queries_at]
    for at in range(count):
        cols = columns_of(first + at)
        query = q_ref[WINDOW : 2 * WINDOW, cols]
        scores = [dot_nt(k_ref[tile * WINDOW : (tile + 1) * WINDOW, cols], query) for tile in range(2)]
        probs, sums, _ = attend(scores, masks, coef, ["all", "masked"])
        total = jnp.zeros((HEAD_DIM, WINDOW), F32)
        for tile in range(2):
            prob_ref[at, tile] = probs[tile]
            sum_ref[at, tile] = sums[tile]
            total = total + dot_tn(v_ref[tile * WINDOW : (tile + 1) * WINDOW, cols], sums[tile])
        part_ref[:, columns_of(at)] = total.T


def late_rows(first, count, queries, keys, values, after):
    tiles = (count, 2, WINDOW, WINDOW)
    wide = count * HEAD_DIM
    return run_once(
        lambda *refs: late_body(first, count, *refs),
        [queries, keys, values],
        [(tiles, BF16), (tiles, BF16), ((WINDOW, wide), F32)],
        [],
        4 * 2 * WINDOW * WINDOW * wide * 4,
        24 * WINDOW * wide,
        after=after,
    )[0]


def early_body(first, count, sent, q_ref, k_ref, v_ref, *rest):
    tail, rest = (rest[0], rest[sent - 1]), rest[sent:]
    prob_ref, sum_ref, inside_ref, window_ref, lse_ref = rest[-5:]
    rows = k_ref.shape[0]
    block = lax.axis_index("ctx")
    lse_ref[...] = rest[0][...] if len(rest) > 5 else jnp.zeros_like(lse_ref)
    keys_at, queries_at = tile_iotas()
    beyond = jnp.where(block > 0, 0, 2 * WINDOW)
    masks = [keys_at > queries_at + beyond, keys_at <= queries_at]
    coef = coef_row(block * rows, WINDOW)
    for at in range(count):
        cols, own = columns_of(first + at), columns_of(at)
        query = q_ref[:WINDOW, cols]
        key_before, value_before = tail_columns(tail, at)
        scores = [dot_nt(key_before, query), dot_nt(k_ref[:WINDOW, cols], query)]
        probs, sums, lse = attend(scores, masks, coef, ["none", "masked"])
        prob_ref[at, 0] = probs[0]
        prob_ref[at, 1] = probs[1]
        sum_ref[at] = sums[1]
        lse_ref[first + at : first + at + 1, :] = lse
        value = v_ref[:WINDOW, cols]
        before = dot_tn(value_before, probs[0])
        window_ref[:, own] = (before + dot_tn(value, probs[1])).T
        inside_ref[:, own] = (before + dot_tn(value, sums[1])).T


def early_rows(first, count, queries, keys, values, before, done, after):
    wide = count * HEAD_DIM
    return run_once(
        lambda *refs: early_body(first, count, len(before), *refs),
        [queries, keys, values, *before, *done],
        [
            ((count, 2, WINDOW, WINDOW), BF16),
            ((count, WINDOW, WINDOW), BF16),
            ((WINDOW, wide), F32),
            ((WINDOW, wide), F32),
            ((STATS, WINDOW), F32),
        ],
        [],
        5 * 2 * WINDOW * WINDOW * wide * 4,
        24 * WINDOW * wide,
        after=after,
    )[0]


def sum_body(sent, even, q_ref, gain_ref, cot_ref, *rest):
    ins, rest = rest[:GROUP], rest[GROUP:]
    insides, rest = rest[: len(sent)], rest[len(sent) :]
    parts, rest = rest[: len(even)], rest[len(even) :]
    hidden_ref, norm_ref, held, squares, crossed, columns = rest
    rows, width = q_ref.shape
    collect(ins, held)
    columns[...] = coef_column(lax.axis_index("ctx") * rows, rows)
    for head in range(width // HEAD_DIM):
        cols = columns_of(head)
        inside, at = picked(sent, insides, head)
        part, late = picked(even, parts, head)
        carried = columns[...] * dot_nn(q_ref[:, cols], held_state(held, head, False))
        hidden = jnp.concatenate([inside[:, columns_of(at)], part[:, columns_of(late)]], 0) + carried
        hidden_ref[:, cols] = hidden
        scaled = gain_ref[:, cols].astype(F32) * cot_ref[:, cols].astype(F32)
        if head == 0:
            squares[...] = hidden * hidden
            crossed[...] = hidden * scaled
        else:
            squares[...] += hidden * hidden
            crossed[...] += hidden * scaled
    norm_ref[...] = jnp.zeros_like(norm_ref)
    norm_ref[0:1, :] = jnp.sum(squares[...].T, 0, keepdims=True)
    norm_ref[1:2, :] = jnp.sum(crossed[...].T, 0, keepdims=True)


def add_prefix(queries, insides, parts, gain, cotangent, prefix, along):
    rows, width = queries.shape
    heads = width // HEAD_DIM
    return run_once(
        lambda *refs: sum_body(sent_chunks(heads), even_chunks(heads), *refs),
        [queries, gain, cotangent, *prefix, *insides, *parts],
        [((rows, width), F32), ((STATS, rows), F32)],
        [pltpu.VMEM((GROUP,) + prefix[0].shape, BF16)] + [pltpu.VMEM((rows, HEAD_DIM), F32)] * 3,
        2 * rows * width * HEAD_DIM,
        12 * rows * width,
        along,
    )


def stat_rows(width):
    return 2 * STATS * -(-3 * WINDOW // width)


def stat_place(width, part):
    across = width // WINDOW
    return (
        slice(WINDOW + part // across * 2 * STATS, WINDOW + (part // across + 1) * 2 * STATS),
        slice(part % across * WINDOW, (part % across + 1) * WINDOW),
    )


def norm_body(sent, features, norm_ref, hidden_ref, gain_ref, cot_ref, q_ref, lse_ref, *rest):
    windows, rest = rest[: len(sent)], rest[len(sent) :]
    out_ref, grad_ref, first_ref = rest[:3]
    outs = rest[3 : 3 + GROUP]
    held, recip, pull, columns, stats, out_held, done = rest[3 + GROUP :]
    rows, width = q_ref.shape
    root = 1.0 / jnp.sqrt(norm_ref[0:1, :] / features + EPSILON)
    slope = root * root * root * norm_ref[1:2, :] / features
    recip[...] = jnp.broadcast_to(root, (HEAD_DIM, rows)).T
    pull[...] = jnp.broadcast_to(slope, (HEAD_DIM, rows)).T
    columns[...] = coef_column(lax.axis_index("ctx") * rows, rows)
    stats[...] = jnp.zeros_like(stats)
    stats[:STATS, :] = lse_ref[...]
    held[...] = jnp.zeros_like(held)
    copies = []
    for head in range(width // HEAD_DIM):
        cols = columns_of(head)
        hidden = hidden_ref[:, cols]
        gain = gain_ref[:, cols].astype(F32)
        kept = recip[...]
        out_held[:, cols] = (hidden * kept * gain).astype(BF16)
        push(out_held, out_ref, done, head, copies)
        full = kept * (gain * cot_ref[:, cols].astype(F32)) - hidden * pull[...]
        grad = full.astype(BF16)
        grad_ref[:, cols] = grad
        first_ref[:WINDOW, cols] = grad[:WINDOW]
        window, at = picked(sent, windows, head)
        delta = (grad[:WINDOW].astype(F32) * window[:, columns_of(at)]).T
        stats[STATS + head : STATS + head + 1, :] = jnp.sum(delta, 0, keepdims=True)
        state = dot_tn(q_ref[:, cols], (full * columns[...]).astype(BF16)).astype(BF16)
        store_state(held, head, state, True)
    spread(held, outs)
    left = stats[...]
    below = WINDOW + stat_rows(width)
    first_ref[WINDOW:below, :] = jnp.zeros((below - WINDOW, width), BF16)
    first_ref[below:, :] = q_ref[AHEAD:WINDOW, :]
    for part in range(3):
        at_rows, at_cols = stat_place(width, part)
        taken = left.astype(BF16)
        first_ref[at_rows, at_cols] = taken
        left = left - taken.astype(F32)
    for copy in copies:
        copy.wait()


def normalize(norms, hidden, gain, cotangent, queries, windows, lse, features):
    rows, width = queries.shape
    heads = width // HEAD_DIM
    piece = part_shape(heads)
    return run_once(
        lambda *refs: norm_body(sent_chunks(heads), features, *refs),
        [norms, hidden, gain, cotangent, queries, lse, *windows],
        [((rows, width), BF16), ((rows, width), BF16), ((2 * WINDOW - AHEAD + stat_rows(width), width), BF16)] + [(piece, BF16)] * GROUP,
        [pltpu.VMEM((GROUP,) + piece, BF16)]
        + [pltpu.VMEM((rows, HEAD_DIM), F32)] * 3
        + [
            pltpu.VMEM((2 * STATS, WINDOW), F32),
            pltpu.VMEM((rows, width), BF16),
            pltpu.SemaphoreType.DMA((heads // heads_a_step(heads),)),
        ],
        2 * rows * width * HEAD_DIM,
        14 * rows * width,
        pushed=(0,),
    )[0]


def back_body(first, count, sent, even, q_ref, k_ref, v_ref, g_ref, *rest):
    heads = q_ref.shape[1] // HEAD_DIM
    rows = q_ref.shape[0]
    last = first + count == heads
    ins, rest = rest[:GROUP], rest[GROUP:]
    tails, rest = tails_apart(rest[: len(sent) + 1]), rest[len(sent) + 1 :]
    probs0, rest = rest[: len(sent)], rest[len(sent) :]
    sums0, rest = rest[: len(sent)], rest[len(sent) :]
    probs1, sums1 = rest[0], rest[1]
    made = rest[2:-3] if not last else rest[2:-5]
    if last:
        dk_ref, dv_ref, held, dq_held, done = rest[-5:]
        dq_ref, made = made[-1], made[:-1]
    else:
        dq_held, dk_ref, dv_ref, held = made[-1], *rest[-3:]
        dq_ref, made = None, made[:-1]
    collect(ins, held)
    keys_at, queries_at = tile_iotas()
    causal = keys_at <= queries_at
    start = lax.axis_index("ctx") * rows
    ratios = coef_row(start, rows) * (1.0 / SCALE)
    early, late = slice(0, WINDOW), slice(WINDOW, 2 * WINDOW)
    copies = []
    if last and made:
        dq_held[:, : first * HEAD_DIM] = made[0][...]
        for head in range(first):
            push(dq_held, dq_ref, done, head, copies)
    for at in range(count):
        head = first + at
        cols, own = columns_of(head), columns_of(at)
        tail, place = picked(sent, tails, head)
        key_before, value_before = tail_columns(tail, place)
        prob0 = picked(sent, probs0, head)[0]
        sum0 = picked(sent, sums0, head)[0]
        grads = g_ref[early, cols], g_ref[late, cols]
        queries = q_ref[early, cols], q_ref[late, cols]
        keys = key_before, k_ref[early, cols], k_ref[late, cols]
        values = value_before, v_ref[early, cols], v_ref[late, cols]
        probs = (
            (prob0[place, 0].astype(F32), prob0[place, 1].astype(F32)),
            (probs1[at, 0].astype(F32), probs1[at, 1].astype(F32)),
        )
        edges = []
        for half in range(2):
            ratio = ratios[:, half * WINDOW : (half + 1) * WINDOW]
            pulls = [dot_nt(values[half + tile], grads[half]) for tile in range(2)]
            delta = jnp.sum(probs[half][0] * pulls[0] + probs[half][1] * pulls[1], 0, keepdims=True)
            before = probs[half][0] * (pulls[0] - delta)
            if half == 1:
                before = before + pulls[0] * ratio
            here = probs[half][1] * (pulls[1] - delta) + jnp.where(causal, pulls[1] * ratio, 0.0)
            edges.append((before.astype(BF16), here.astype(BF16)))
        state = held_state(held, head, False)
        for half, part in enumerate((early, late)):
            inner = dot_tn(keys[half], edges[half][0]) + dot_tn(keys[half + 1], edges[half][1])
            carried = (coef_row(start + half * WINDOW, WINDOW) * (1.0 / SCALE)) * dot_nt(state, grads[half])
            dq_held[part, cols if last else own] = ((inner + carried).T * SCALE).astype(BF16)
        if last:
            push(dq_held, dq_ref, done, head, copies)
        dk_ref[early, own] = SCALE * (dot_nn(edges[0][1], queries[0]) + dot_nn(edges[1][0], queries[1]))
        dk_ref[late, own] = SCALE * dot_nn(edges[1][1], queries[1])
        dv_ref[early, own] = dot_nn(sum0[place], grads[0]) + dot_nn(sums1[at, 0], grads[1])
        dv_ref[late, own] = dot_nn(sums1[at, 1], grads[1])
    for copy in copies:
        copy.wait()


def backward(first, count, queries, keys, values, grads, before, probs0, sums0, probs1, sums1, prefix, made, after):
    rows, width = keys.shape
    heads = width // HEAD_DIM
    last = first + count == heads
    wide = count * HEAD_DIM
    scratch = [pltpu.VMEM((GROUP,) + prefix[0].shape, BF16)]
    if last:
        scratch += [pltpu.VMEM((rows, width), BF16), pltpu.SemaphoreType.DMA((heads // heads_a_step(heads),))]
    return run_once(
        lambda *refs: back_body(first, count, sent_chunks(heads), even_chunks(heads), *refs),
        [queries, keys, values, grads, *prefix, *before, *probs0, *sums0, probs1, sums1, *made],
        [((rows, width if last else wide), BF16), ((rows, wide), F32), ((rows, wide), F32)],
        scratch,
        16 * 2 * WINDOW * WINDOW * wide * 2,
        40 * WINDOW * wide * 2,
        after=after,
        pushed=(0,) if last else (),
    )[0]


def edge_body(last, k_ref, v_ref, qn_ref, sent_ref, dk_ref, dv_ref):
    width = k_ref.shape[1]
    stats = jnp.zeros((2 * STATS, WINDOW), F32)
    for part in range(3):
        at_rows, at_cols = stat_place(width, 2 - part)
        stats = stats + sent_ref[at_rows, at_cols].astype(F32)
    keys_at, queries_at = tile_iotas()
    beyond = jnp.where(lax.axis_index("ctx") < last, 0, 2 * WINDOW)
    mask = keys_at > queries_at + beyond
    late = slice(WINDOW, 2 * WINDOW)
    for head in range(width // HEAD_DIM):
        cols = columns_of(head)
        query = jnp.concatenate([qn_ref[:, cols], sent_ref[WINDOW + stat_rows(width) :, cols]], 0)
        grad = sent_ref[:WINDOW, cols]
        lse = stats[head : head + 1, :] * (1.0 / LN2)
        delta = stats[STATS + head : STATS + head + 1, :]
        scores = dot_nt(k_ref[late, cols], query) * SCALE_LOG2
        probs = jnp.where(mask, jnp.exp2(scores - lse), 0.0)
        edges = probs * (dot_nt(v_ref[late, cols], grad) - delta)
        dk_ref[:, cols] = SCALE * dot_nn(edges.astype(BF16), query)
        dv_ref[:, cols] = dot_nn(probs.astype(BF16), grad)


def edge(keys, values, queries_after, grads_after, after):
    width = keys.shape[1]
    last = lax.axis_size("ctx") - 1
    return run_once(
        lambda *refs: edge_body(last, *refs),
        [keys, values, queries_after, grads_after],
        [((WINDOW, width), F32)] * 2,
        [],
        4 * 2 * WINDOW * WINDOW * width,
        12 * WINDOW * width,
        after=after,
    )[0]


def last_body(even, k_ref, v_ref, ek_ref, ev_ref, *rest):
    ins, rest = rest[:GROUP], rest[GROUP:]
    dk_in, dv_in = rest[: len(even)], rest[len(even) : 2 * len(even)]
    dk_ref, dv_ref, held, dk_held, dv_held, dk_done, dv_done = rest[2 * len(even) :]
    early, late = slice(0, WINDOW), slice(WINDOW, 2 * WINDOW)
    collect(ins, held)
    copies = []
    for head in range(k_ref.shape[1] // HEAD_DIM):
        cols = columns_of(head)
        dk_ref_in, at = picked(even, dk_in, head)
        dv_ref_in = picked(even, dv_in, head)[0]
        state = held_state(held, head, True)
        keys = dk_ref_in[:, columns_of(at)] + dot_nt(v_ref[:, cols], state)
        dk_held[early, cols] = keys[early].astype(BF16)
        dk_held[late, cols] = (keys[late] + ek_ref[:, cols]).astype(BF16)
        push(dk_held, dk_ref, dk_done, head, copies)
        values = dv_ref_in[:, columns_of(at)] + dot_nn(k_ref[:, cols], state)
        dv_held[early, cols] = values[early].astype(BF16)
        dv_held[late, cols] = (values[late] + ev_ref[:, cols]).astype(BF16)
        push(dv_held, dv_ref, dv_done, head, copies)
    for copy in copies:
        copy.wait()


def finish(keys, values, dk_parts, dv_parts, edges, suffix):
    rows, width = keys.shape
    heads = width // HEAD_DIM
    done = pltpu.SemaphoreType.DMA((heads // heads_a_step(heads),))
    return run_once(
        lambda *refs: last_body(even_chunks(heads), *refs),
        [keys, values, *edges, *suffix, *dk_parts, *dv_parts],
        [((rows, width), BF16)] * 2,
        [pltpu.VMEM((GROUP,) + suffix[0].shape, BF16)] + [pltpu.VMEM((rows, width), BF16)] * 2 + [done, done],
        4 * rows * width * HEAD_DIM,
        18 * rows * width,
        pushed=(0, 1),
    )[0]


def summed(value, axis):
    count = lax.axis_size(axis)
    mask = 1
    while mask < count:
        value = value + lax.ppermute(value, axis, [(at, at ^ mask) for at in range(count)])
        mask *= 2
    return value


def on_device(queries, keys, values, gain, cotangent):
    rows, width = queries.shape
    heads = width // HEAD_DIM
    features = width * lax.axis_size("head")
    sent, even = sent_chunks(heads), even_chunks(heads)
    gain = gain.reshape(1, width)
    late, own, grads_after = [], [], []

    before = [turn(keys[rows - WINDOW :, : sent[0][1] * HEAD_DIM], 1)]
    pieces, tails = local_states(keys, values)

    def first_round():
        late.append(late_rows(*even[0], queries, keys, values, pieces[:1]))
        return tails, [before[0], late[0][2]]

    def second_round(total, held):
        before.extend(onward(tail, 1) if at else turn(tail, 1) for at, tail in enumerate(held))
        late.extend(late_rows(*chunk, queries, keys, values, [total]) for chunk in even[1:])
        return [], [late[-1][2]]

    prefix, merged, _ = scan(pieces, False, first_round, second_round)
    early = []
    for chunk, tail in zip(sent, [before[:2]] + [[tail] for tail in before[2:]]):
        done = [early[-1][4]] if early else []
        early.append(early_rows(*chunk, queries, keys, values, tail, done, merged[:1]))
    probs0, sums0, insides, windows, lses = zip(*early)
    probs1, sums1, parts = zip(*late)
    (hidden, norms), handed = add_prefix(queries, insides, parts, gain, cotangent, prefix, [queries[:AHEAD]])
    after = turn(handed[0], -1)
    norms = summed(norms, "head")
    output, grads, first, *states = normalize(norms, hidden, gain, cotangent, queries, windows, lses[-1], features)

    def own_chunk(at, after):
        made = [own[0][0]] if own else []
        own.append(
            backward(
                *even[at], queries, keys, values, grads, before, probs0, sums0, probs1[at], sums1[at], prefix, made, after
            )
        )

    def first_back():
        own_chunk(0, [])
        return [first], [after, own[0][1]]

    def second_back(total, held):
        grads_after.append(turn(held[0], -1))
        for at in range(1, len(even)):
            own_chunk(at, [total])
        return [], [own[-1][1]]

    suffix, merged, _ = scan(states, True, first_back, second_back)
    edges = edge(keys, values, after, grads_after[0], merged[:1])
    grad_queries, dk_parts, dv_parts = zip(*own)
    grad_keys, grad_values = finish(keys, values, dk_parts, dv_parts, edges, suffix)
    return output, grad_queries[-1], grad_keys, grad_values


def solution(mesh):
    wide = P("ctx", "head")
    return jax.shard_map(
        on_device,
        mesh=mesh,
        in_specs=(wide, wide, wide, P("head"), wide),
        out_specs=(wide, wide, wide, wide),
        check_vma=False,
    )
```
